128 devices in a mesh: dp: 8 (over x, core), seq: 16 (over z, y).
Axes of the slice: x: 4, y: 4, z: 4, core: 2. Of those that a mesh axis runs over, the one named last changes fastest.
Arguments:
- tokens: bfloat16 [8, 2048, 768], P('dp', 'seq'), may hold values from -6 to 6
- params: bfloat16 [7094272], P(('dp', 'seq')), may hold values from -6 to 6, as said below
- out_grad: bfloat16 [8, 2048, 768], P('dp', 'seq'), may hold values from -6 to 6
Outputs:
- layer_out: bfloat16 [8, 2048, 768], P('dp', 'seq')
- input_grad: float32 [8, 2048, 768], P('dp', 'seq')
- param_grad: float32 [7094272], P(('dp', 'seq'))
The draws below stay inside these ranges and needn't reach their ends.
Inputs may be any that keep to these rules, and one draw needn't show every extreme that they name: `params`: gains lie near 1.
All inputs are finite; a program needn't handle non-finite values.
Results may differ from the reference program's by a relative error of at most 0.0055.
Values may be sent and summed in bfloat16 or wider, within the bound.
A program may use at most 320 MiB of HBM per device.

```python
import math
import jax
import jax.numpy as jnp
from jax import lax

D = 768
HEADS = 12
HEAD_DIM = 64
ROT = 16
FF = 3072
SEQS = 8
LENGTH = 2048
P_PAD = 7094272


def draw_params(key, part):
    key = jax.random.fold_in(key, 7)
    noise = jnp.clip(jax.random.normal(key, (P_PAD,), jnp.float32), -6.0, 6.0)
    position = jnp.arange(P_PAD)
    scales = [(D, 0.1), (D, 0.2), (D, 0.1), (D, 0.2), (3 * D * D, D ** (-0.5)), (3 * D, 0.2), (D * D, 3.0 * D ** (-0.5)), (D, 0.2), (D * FF, D ** (-0.5)), (FF, 0.2), (FF * D, FF ** (-0.5)), (D, 0.2)]
    scale = jnp.ones((P_PAD,), jnp.float32)
    offset = jnp.zeros((P_PAD,), jnp.float32)
    start = 0
    for number, pair in enumerate(scales):
        inside = (position >= start) & (position < start + pair[0])
        scale = jnp.where(inside, pair[1], scale)
        if number == 0 or number == 2:
            offset = jnp.where(inside, 1.0, offset)
        start += pair[0]
    return (offset + scale * noise).astype(jnp.bfloat16)


def levels(rng, shape, cuts, low, largest):
    def one(dim, blocks):
        steps = jax.random.uniform(jax.random.fold_in(jax.random.fold_in(rng, 6), dim), (blocks,), jnp.float32, low / len(cuts), largest / len(cuts))
        return jnp.repeat(jnp.exp(steps), shape[dim] // blocks).reshape((-1,) + (1,) * (len(shape) - dim - 1))

    loudness = one(*cuts[0])
    for cut in cuts[1:]:
        loudness = loudness * one(*cut)
    return loudness


def normal_values(own_key, extent, scale, reach, shards=(), held_as=jnp.bfloat16):
    factor_of = levels(own_key, extent, shards, -0.22, 0.18) if shards else 1.0
    array = jax.random.normal(own_key, extent, jnp.float32) * scale * factor_of
    return jnp.minimum(jnp.maximum(array, -reach), reach).astype(held_as)


def setup_inputs(seed: int = 0) -> dict:
    arg_keys = jax.random.split(jax.random.key(seed), 4)
    tokens = normal_values(arg_keys[0], (SEQS, LENGTH, D), 1.0, 6.0, ((0, 8), (1, 16)))
    params = draw_params(jax.random.fold_in(arg_keys[3], 71), 0)
    out_grad = normal_values(arg_keys[2], (SEQS, LENGTH, D), 1.0, 6.0, ((0, 8), (1, 16)))
    return {"tokens": tokens, "params": params, "out_grad": out_grad}


EPS = 1e-05
HIGH = lax.Precision.HIGHEST

@jax.custom_vjp
def low(v):
    return lax.optimization_barrier(v.astype(jnp.bfloat16)).astype(jnp.float32)

@jax.custom_vjp
def low_back(v):
    return v

def low_keep(v):
    return (low(v), None)

def low_pass(kept, grad):
    return (grad,)

def back_keep(v):
    return (v, None)

def back_low(kept, grad):
    return (low(grad),)
low.defvjp(low_keep, low_pass)
low_back.defvjp(back_keep, back_low)

def sections(width, hidden):
    return [('ln1_gain', (width,)), ('ln1_shift', (width,)), ('ln2_gain', (width,)), ('ln2_shift', (width,)), ('w_qkv', (width, 3 * width)), ('b_qkv', (3 * width,)), ('w_out', (width, width)), ('b_out', (width,)), ('w_up', (width, hidden)), ('b_up', (hidden,)), ('w_down', (hidden, width)), ('b_down', (width,))]

def unpack(flat, width, hidden):
    pieces = {}
    offset = 0
    for label, dims in sections(width, hidden):
        amount = math.prod(dims)
        pieces[label] = flat[offset:offset + amount].reshape(dims)
        offset += amount
    return pieces

def norm(values, gain, shift):
    center = lax.optimization_barrier(jnp.mean(values, -1, keepdims=True))
    centered = values - center
    spread = lax.optimization_barrier(jnp.mean(centered * centered, -1, keepdims=True))
    return centered * lax.rsqrt(spread + EPS) * gain + shift

def rotate(tensor, positions, sign):
    half = ROT // 2
    freq = 10000.0 ** (-jnp.arange(half).astype(tensor.dtype) * 2.0 / ROT)
    angles = positions.astype(tensor.dtype)[:, None] * freq[None, :]
    cosine = jnp.cos(angles)[:, None, :]
    sine = jnp.sin(angles)[:, None, :] * sign
    first = tensor[..., :half]
    second = tensor[..., half:ROT]
    return jnp.concatenate([first * cosine - second * sine, second * cosine + first * sine, tensor[..., ROT:]], -1)

def attend_one(triple):
    query, keys, values = triple
    length = query.shape[0]
    raw = jnp.einsum('qhd,khd->hqk', query, keys, precision=HIGH) * HEAD_DIM ** (-0.5)
    scores = low_back(raw)
    causal = jnp.arange(length)[:, None] >= jnp.arange(length)[None, :]
    scores = jnp.where(causal[None], scores, -1e+30)
    probs = low(jax.nn.softmax(scores, -1))
    return jnp.einsum('hqk,khd->qhd', probs, values, precision=HIGH)

def forward(inputs, flat):
    weights = unpack(flat, D, FF)
    seqs, length, width = inputs.shape
    positions = jnp.arange(length)
    h1 = low(norm(inputs, weights['ln1_gain'], weights['ln1_shift']))
    h2 = low(norm(inputs, weights['ln2_gain'], weights['ln2_shift']))
    qkv = low_back(jnp.dot(h1, weights['w_qkv'], precision=HIGH) + weights['b_qkv'])
    shaped = qkv.reshape(seqs, length, 3, HEADS, HEAD_DIM)
    query = low_back(low(rotate(shaped[:, :, 0], positions, 1.0)))
    keys = low_back(low(rotate(shaped[:, :, 1], positions, 1.0)))
    values = low_back(low(shaped[:, :, 2]))
    mixed = lax.map(jax.checkpoint(attend_one), (query, keys, values))
    attended = low_back(low(mixed.reshape(seqs, length, width)))
    attn_branch = jnp.dot(attended, weights['w_out'], precision=HIGH) + weights['b_out']
    up = low_back(jnp.dot(h2, weights['w_up'], precision=HIGH) + weights['b_up'])
    act = low(jax.nn.gelu(up, approximate=False))
    mlp_branch = jnp.dot(act, weights['w_down'], precision=HIGH) + weights['b_down']
    return inputs + attn_branch + mlp_branch

def reference(tokens, params, out_grad):
    inputs = tokens.astype(jnp.float32)
    flat = params.astype(jnp.float32)
    result, pull = jax.vjp(forward, inputs, flat)
    input_grad, param_grad = pull(out_grad.astype(jnp.float32))
    return (result.astype(jnp.bfloat16), input_grad, param_grad)
```

```python
import functools
import math

import jax
import jax.numpy as jnp
from jax import lax
from jax.experimental import pallas as pl
from jax.experimental.pallas import tpu as pltpu
from jax.sharding import Mesh
from jax.sharding import PartitionSpec as P

D = 768
HEADS = 12
HEAD_DIM = 64
ROT = 16
FF = 3072
DP_SEQ = ("dp_0", "dp_1", "seq_0", "seq_1")
SEQ = ("seq_0", "seq_1")
DP = ("dp_0", "dp_1")


EPS = 1e-05


MESH = pl.DeviceIdType.MESH
ROWS = 448
PARTS = ((0, 144, (0, 2, 1)), (144, 144, (2, 1, 0)), (288, 160, (1, 0, 2)))


def place():
    return [lax.axis_index("dp_0"), lax.axis_index("seq_0"), lax.axis_index("seq_1")], lax.axis_index("dp_1")


def device(pos, core):
    return (pos[0], core, pos[1], pos[2])


def moved(pos, axis, by):
    out = list(pos)
    out[axis] = lax.rem(pos[axis] + by, 4)
    return out


def greet(pos, core, sibling=True):
    barrier = pltpu.get_barrier_semaphore()
    others = [device(moved(pos, a, by), core) for a in range(3) for by in (1, 3)]
    if sibling:
        others.append(device(pos, 1 - core))
    for other in others:
        pl.semaphore_signal(barrier, inc=1, device_id=other, device_id_type=MESH)
    pl.semaphore_wait(barrier, len(others))


def gather_kernel(own_ref, out_ref, send, recv, sib_send, sib_recv, local):
    pos, core = place()
    greet(pos, core)

    def region(part, where, c, start, size):
        idx = [slice(None) if w is None else w for w in where]
        return out_ref.at[idx[0], c, idx[1], idx[2], pl.ds(start, size), :]

    own = pltpu.make_async_copy(own_ref, out_ref.at[pos[0], core, pos[1], pos[2]], local)
    own.start()
    own.wait()
    sibs = []

    def to_sibling(number, part, where):
        start, size, _ = PARTS[part]
        ref = region(part, where, core, start, size)
        copy = pltpu.make_async_remote_copy(ref, ref, sib_send.at[part, number], sib_recv.at[part, number],
                                            device_id=device(pos, 1 - core), device_id_type=MESH)
        copy.start()
        sibs.append(copy)

    def push(part, phase, number, where, start, size, axis, by):
        ref = region(part, where, core, start, size)
        copy = pltpu.make_async_remote_copy(ref, ref, send.at[part, phase, number], recv.at[part, phase, number],
                                            device_id=device(moved(pos, axis, by), core), device_id_type=MESH)
        copy.start()
        return copy

    def before(order, phase):
        where = [pos[0], pos[1], pos[2]]
        for a in order[:phase]:
            where[a] = None
        return where

    for part in range(3):
        to_sibling(0, part, before(PARTS[part][2], 0))
    for phase in range(3):
        firsts, seconds = [], []
        for part in range(3):
            start, size, order = PARTS[part]
            axis = order[phase]
            where = before(order, phase)
            firsts.append((push(part, phase, 0, where, start, size, axis, 1), push(part, phase, 1, where, start, size, axis, 3)))
        for part in range(3):
            start, size, order = PARTS[part]
            axis = order[phase]
            up, down = firsts[part]
            half = size // 32 * 16
            left = before(order, phase)
            left[axis] = lax.rem(pos[axis] + 3, 4)
            right = before(order, phase)
            right[axis] = lax.rem(pos[axis] + 1, 4)
            up.wait_recv()
            one = push(part, phase, 2, left, start, half, axis, 1)
            to_sibling(1 + 3 * phase, part, left)
            down.wait_recv()
            two = push(part, phase, 3, right, start + half, size - half, axis, 3)
            to_sibling(2 + 3 * phase, part, right)
            seconds.append((one, two))
        for part in range(3):
            start, size, order = PARTS[part]
            axis = order[phase]
            one, two = seconds[part]
            one.wait_recv()
            two.wait_recv()
            far = before(order, phase)
            far[axis] = lax.rem(pos[axis] + 2, 4)
            to_sibling(3 + 3 * phase, part, far)
        for copy in [c for pair in firsts + seconds for c in pair]:
            copy.wait_send()
    for copy in sibs:
        copy.wait_send()
        copy.wait_recv()


def gather(own):
    return pl.pallas_call(
        gather_kernel,
        out_shape=jax.ShapeDtypeStruct((4, 2, 4, 4, ROWS, 128), jnp.bfloat16),
        in_specs=[pl.BlockSpec(memory_space=pl.ANY)],
        out_specs=pl.BlockSpec(memory_space=pl.ANY),
        scratch_shapes=[pltpu.SemaphoreType.DMA((3, 3, 4)), pltpu.SemaphoreType.DMA((3, 3, 4)),
                        pltpu.SemaphoreType.DMA((3, 10)), pltpu.SemaphoreType.DMA((3, 10)), pltpu.SemaphoreType.DMA],
        compiler_params=pltpu.CompilerParams(collective_id=0, has_side_effects=True),
    )(own)


EIGHTH = 16 * 433
W_QKV = (24, 768, 18)
W_OUT = (13866, 768, 6)
W_UP = (18480, 768, 24)
W_DOWN = (36936, 3072, 6)
VECTORS = {"ln1_gain": (0, 6), "ln1_shift": (6, 6), "ln2_gain": (12, 6), "ln2_shift": (18, 6),
           "b_qkv": (13848, 18), "b_out": (18474, 6), "b_up": (36912, 24), "b_down": (55368, 6)}


def unpack_kernel(first, count, plan, g_ref, *rest):
    outs, flat = rest[:-1], rest[-1]
    step = pl.program_id(0)

    @pl.loop(0, 16)
    def _(k):
        base = (step * 16 + k) * 433
        flat[pl.ds(base, 440), :] = g_ref[k, 0:440, :].astype(jnp.float32)

    for (offset, rows, blocks), ready, out in zip(plan, READY[first], outs):
        @pl.when(step == ready - first)
        def _(offset=offset, rows=rows, blocks=blocks, out=out):
            start = offset - first * EIGHTH
            size = 64

            @pl.loop(0, rows // size)
            def _(i):
                for j in range(blocks):
                    piece = flat[pl.ds(start + j + i * (size * blocks), size, stride=blocks), :]
                    out[pl.ds(pl.multiple_of(i * size, size), size), 128 * j:128 * (j + 1)] = piece.astype(jnp.bfloat16)


READY = {0: (1, 2), 2: (5, 7)}


def unpack_call(gathered, first, count, plan):
    whole = lambda rows, cols: pl.BlockSpec((rows, cols), lambda e: (0, 0))
    return pl.pallas_call(
        functools.partial(unpack_kernel, first, count, plan),
        grid=(count,),
        out_shape=[jax.ShapeDtypeStruct((r, 128 * b), jnp.bfloat16) for _, r, b in plan],
        in_specs=[pl.BlockSpec((16, 448, 128), lambda e: (e + first, 0, 0))],
        out_specs=[whole(r, 128 * b) for _, r, b in plan],
        scratch_shapes=[pltpu.VMEM((count * EIGHTH + 16, 128), jnp.float32)],
        compiler_params=pltpu.CompilerParams(vmem_limit_bytes=56 * 2**20),
    )(gathered)


def unpack(gathered):
    w_qkv, w_out = unpack_call(gathered, 0, 3, (W_QKV, W_OUT))
    w_up, w_down = unpack_call(gathered, 2, 6, (W_UP, W_DOWN))
    def vector(name):
        start, rows = VECTORS[name]
        pieces = []
        row = start
        while row < start + rows:
            shard, at = divmod(row, 433)
            take = min(start + rows - row, 433 - at)
            pieces.append(gathered[shard, at:at + take])
            row += take
        return jnp.concatenate(pieces, 0).reshape(-1)
    out = {n: vector(n) for n in VECTORS}
    out.update(w_qkv=w_qkv, w_out=w_out, w_up=w_up, w_down=w_down)
    return out


MARGIN = 384
CHUNK = 128
ORDER = ("ln1_gain", "ln1_shift", "ln2_gain", "ln2_shift", "b_qkv", "b_out", "b_up", "b_down")


def weight_kernel(core_ref, vec_ref, h1_ref, att_ref, h2_ref, act_ref, dqkv_ref, g_ref, dup_ref, out_ref, flat):
    step = pl.program_id(0)
    core = core_ref[0]
    pairs = ((W_QKV, h1_ref, dqkv_ref), (W_OUT, att_ref, g_ref), (W_UP, h2_ref, dup_ref), (W_DOWN, act_ref, g_ref))

    def eighth(number):
        low, high = number * EIGHTH, (number + 1) * EIGHTH
        at = MARGIN - low
        for (offset, rows, blocks), left, right in pairs:
            first = max(0, (low - offset) // blocks) // 16 * 16
            last = min(rows, -(-(high - offset) // blocks))
            last = -(-last // 16) * 16
            if last <= first:
                continue
            size = min(CHUNK, last - first)
            count = -(-(last - first) // size)
            base = offset + at

            @pl.loop(0, count)
            def _(i, first=first, last=last, size=size, blocks=blocks, base=base, left=left, right=right):
                row = pl.multiple_of(jnp.minimum(first + i * size, last - size), 16)
                lhs = left[pl.ds(row, size), :]

                @pl.loop(0, blocks // 2, unroll=3)
                def _(j):
                    rhs = right[:, pl.ds(pl.multiple_of(j * 256, 256), 256)]
                    product = jnp.dot(lhs, rhs, preferred_element_type=jnp.float32)
                    start = base + row * blocks + 2 * j
                    flat[pl.ds(start, size, stride=blocks), :] = product[:, :128]
                    flat[pl.ds(start + 1, size, stride=blocks), :] = product[:, 128:]

        row = 0
        for name in ORDER:
            start, count = VECTORS[name]
            lo, hi = max(start, low), min(start + count, high)
            if lo < hi:
                flat[lo + at:hi + at, :] = vec_ref[row + lo - start:row + hi - start, :]
            row += count
        end = 55374
        if high > end:
            flat[end + at:high + at, :] = jnp.zeros((high - end, 128), jnp.float32)

    for t in range(4):
        for c in range(2):
            pl.when((step == t) & (core == c))(lambda number=2 * t + c: eighth(number))

    @pl.loop(0, 16)
    def _(k):
        out_ref[0, k] = flat[pl.ds(MARGIN + 433 * k, 448), :].astype(jnp.bfloat16)


def weight_grads(core, vec, h1t, att_t, h2t, act_t, dqkv, g, dup):
    whole = pl.BlockSpec(memory_space=pltpu.VMEM)
    return pl.pallas_call(
        weight_kernel,
        grid=(4,),
        out_shape=jax.ShapeDtypeStruct((4, 16, 448, 128), jnp.bfloat16),
        in_specs=[pl.BlockSpec(memory_space=pltpu.SMEM)] + [whole] * 8,
        out_specs=pl.BlockSpec((1, 16, 448, 128), lambda e: (e, 0, 0, 0)),
        scratch_shapes=[pltpu.VMEM((EIGHTH + 2 * MARGIN, 128), jnp.float32)],
        compiler_params=pltpu.CompilerParams(vmem_limit_bytes=48 * 2**20),
    )(core, vec, h1t, att_t, h2t, act_t, dqkv, g, dup)


def halves(size):
    half = size // 32 * 16
    return half, size - half


def pick(ref, axes, axis, index, start, size):
    idx = tuple(index if a == axis else slice(None) for a in axes)
    return ref.at[idx + (pl.ds(start, size), slice(None))]


def each(count, body):
    if count == 0:
        body(())
        return
    @pl.loop(0, 4 ** count)
    def _(n):
        body(tuple(lax.rem(lax.div(n, 4 ** (count - 1 - d)), 4) for d in range(count)))


def scatter_kernel(in_ref, out_ref, *scratch):
    send, recv = scratch[-2:]
    bufs = list(scratch[:-2])
    pos, core = place()
    greet(pos, core, sibling=False)
    take = iter(bufs)
    got = {}
    for part in range(3):
        for phase in range(3):
            got[part, phase] = [next(take) for _ in range(9 if phase < 2 else 8)]

    def push(part, phase, number, src, dst, axis, by):
        copy = pltpu.make_async_remote_copy(src, dst, send.at[part, phase, number], recv.at[part, phase, number],
                                            device_id=device(moved(pos, axis, by), core), device_id_type=MESH)
        copy.start()
        return copy

    def current(part, phase):
        start, size, order = PARTS[part]
        axes = [0, 1, 2]
        for a in order[::-1][:phase]:
            axes.remove(a)
        if phase == 0:
            return in_ref, axes, start
        return got[part, phase - 1][8], axes, 0

    copies = {}

    def begin(part, phase):
        ref, axes, base = current(part, phase)
        start, size, order = PARTS[part]
        axis = order[2 - phase]
        h0, h1 = halves(size)
        q = pos[axis]
        far, right, left = (lax.rem(q + k, 4) for k in (2, 1, 3))
        b = got[part, phase]
        copies[part, phase] = [
            push(part, phase, 0, pick(ref, axes, axis, far, base, h0), b[0], axis, 1),
            push(part, phase, 1, pick(ref, axes, axis, far, base + h0, h1), b[1], axis, 3),
            push(part, phase, 2, pick(ref, axes, axis, right, base + h0, h1), b[2], axis, 1),
            push(part, phase, 3, pick(ref, axes, axis, left, base, h0), b[3], axis, 3),
        ]

    def add(ref, axes, axis, index, base, size, others, put):
        rest = [a for a in axes if a != axis]

        def body(at):
            full = dict(zip(rest, at))
            idx = tuple(index if a == axis else full[a] for a in axes)
            total = ref[idx + (pl.ds(base, size), slice(None))].astype(jnp.float32)
            for other in others:
                total = total + other[at + (slice(None), slice(None))].astype(jnp.float32)
            put(at, total)

        each(len(rest), body)

    def middle(part, phase):
        ref, axes, base = current(part, phase)
        start, size, order = PARTS[part]
        axis = order[2 - phase]
        h0, h1 = halves(size)
        q = pos[axis]
        right, left = (lax.rem(q + k, 4) for k in (1, 3))
        b = got[part, phase]
        c = copies[part, phase]

        def to(ref):
            def put(at, total):
                ref[at + (slice(None), slice(None))] = total.astype(jnp.bfloat16)
            return put

        c[0].wait_recv()
        add(ref, axes, axis, right, base, h0, [b[0]], to(b[6]))
        c.append(push(part, phase, 4, b[6], b[4], axis, 1))
        c[1].wait_recv()
        add(ref, axes, axis, left, base + h0, h1, [b[1]], to(b[7]))
        c.append(push(part, phase, 5, b[7], b[5], axis, 3))

    def finish(part, phase):
        ref, axes, base = current(part, phase)
        start, size, order = PARTS[part]
        axis = order[2 - phase]
        h0, h1 = halves(size)
        q = pos[axis]
        b = got[part, phase]
        c = copies[part, phase]
        for copy in c[2:]:
            copy.wait_recv()
        for lo, n, others in ((0, h0, [b[3], b[4]]), (h0, h1, [b[2], b[5]])):
            def put(at, total, lo=lo, n=n):
                if phase == 2:
                    out_ref[start + lo:start + lo + n, :] = total
                else:
                    b[8][at + (pl.ds(lo, n), slice(None))] = total.astype(jnp.bfloat16)
            add(ref, axes, axis, q, base + lo, n, others, put)

    for phase in range(3):
        for part in range(3):
            if phase == 0:
                begin(part, 0)
        for part in range(3):
            middle(part, phase)
        for part in range(3):
            finish(part, phase)
            if phase < 2:
                begin(part, phase + 1)
    for c in copies.values():
        for copy in c:
            copy.wait_send()


def scatter(parts):
    scratch = []
    for part in range(3):
        _, size, _ = PARTS[part]
        h0, h1 = halves(size)
        for phase in range(3):
            lead = (4,) * (2 - phase)
            sizes = [h0, h1, h1, h0, h0, h1, h0, h1] + ([size] if phase < 2 else [])
            scratch += [pltpu.VMEM(lead + (n, 128), jnp.bfloat16) for n in sizes]
    scratch += [pltpu.SemaphoreType.DMA((3, 3, 6)), pltpu.SemaphoreType.DMA((3, 3, 6))]
    return pl.pallas_call(
        scatter_kernel,
        out_shape=jax.ShapeDtypeStruct((ROWS, 128), jnp.float32),
        in_specs=[pl.BlockSpec(memory_space=pltpu.VMEM)],
        out_specs=pl.BlockSpec(memory_space=pltpu.VMEM),
        scratch_shapes=scratch,
        compiler_params=pltpu.CompilerParams(collective_id=1, has_side_effects=True, vmem_limit_bytes=40 * 2**20),
    )(parts)


def in_one_piece(arrays, axis, dim, along):
    widths = [a.shape[along] for a in arrays]
    both = jnp.concatenate(arrays, axis=along)
    out = lax.all_gather(both, axis, axis=dim, tiled=True)
    return tuple(jnp.split(out, [sum(widths[:k]) for k in range(1, len(widths))], axis=along))


def norm_forward(values, gain, shift):
    center = jnp.mean(values, -1, keepdims=True)
    centered = values - center
    spread = jnp.mean(centered * centered, -1, keepdims=True)
    factor = lax.rsqrt(spread + EPS)
    normal = centered * factor
    return (normal * gain.astype(jnp.float32) + shift.astype(jnp.float32), normal, factor)


def norm_backward(grad_out, normal, factor, gain):
    grad_gain = jnp.sum(grad_out * normal, 0)
    grad_shift = jnp.sum(grad_out, 0)
    scaled = grad_out * gain.astype(jnp.float32)
    inner = (
        scaled
        - jnp.mean(scaled, -1, keepdims=True)
        - normal * jnp.mean(scaled * normal, -1, keepdims=True)
    )
    return (factor * inner, grad_gain, grad_shift)


def rotate(tensor, positions, sign):
    half = ROT // 2
    freq = 10000.0 ** (-jnp.arange(half).astype(jnp.float32) * 2.0 / ROT)
    angles = positions.astype(jnp.float32)[:, None] * freq[None, :]
    cosine = jnp.cos(angles)[:, None, :]
    sine = jnp.sin(angles)[:, None, :] * sign
    first = tensor[..., :half]
    second = tensor[..., half:ROT]
    return jnp.concatenate(
        [first * cosine - second * sine, second * cosine + first * sine, tensor[..., ROT:]], -1
    )


def masked_scores(query, keys, query_pos, key_pos):
    raw = jnp.einsum(
        "qhd,khd->hqk", query, keys, preferred_element_type=jnp.float32
    ) * HEAD_DIM ** (-0.5)
    causal = query_pos[:, None] >= key_pos[None, :]
    return (jnp.where(causal[None], raw, -1e30), causal)


def attend_forward(query, keys, values, query_pos, key_pos):
    scores, causal = masked_scores(query, keys, query_pos, key_pos)
    top = jnp.max(scores, -1, keepdims=True)
    expo = jnp.exp(scores - top)
    total = jnp.sum(expo, -1, keepdims=True)
    probs = (expo / total).astype(jnp.bfloat16)
    result = jnp.einsum("hqk,khd->qhd", probs, values, preferred_element_type=jnp.float32)
    return (result, top + jnp.log(total))


def query_side(query, keys, values, grad_att, logsum, query_pos, key_pos):
    scores, causal = masked_scores(query, keys, query_pos, key_pos)
    probs = jnp.exp(scores - logsum)
    grad_probs = jnp.einsum("qhd,khd->hqk", grad_att, values, preferred_element_type=jnp.float32)
    inner = jnp.sum(grad_probs * probs, -1, keepdims=True)
    grad_scores = jnp.where(causal[None], probs * (grad_probs - inner), 0.0).astype(jnp.bfloat16)
    grad_query = jnp.einsum(
        "hqk,khd->qhd", grad_scores, keys, preferred_element_type=jnp.float32
    ) * HEAD_DIM ** (-0.5)
    return (grad_query, inner[..., 0])


def key_side(queries, own_keys, own_values, grad_rows, logsum_rows, inner_rows, query_pos, key_pos):
    scores, causal = masked_scores(queries, own_keys, query_pos, key_pos)
    probs = jnp.exp(scores - logsum_rows[:, :, None])
    grad_probs = jnp.einsum(
        "qhd,khd->hqk", grad_rows, own_values, preferred_element_type=jnp.float32
    )
    grad_scores = jnp.where(
        causal[None], probs * (grad_probs - inner_rows[:, :, None]), 0.0
    ).astype(jnp.bfloat16)
    grad_keys = jnp.einsum(
        "hqk,qhd->khd", grad_scores, queries, preferred_element_type=jnp.float32
    ) * HEAD_DIM ** (-0.5)
    grad_values = jnp.einsum(
        "hqk,qhd->khd", probs.astype(jnp.bfloat16), grad_rows, preferred_element_type=jnp.float32
    )
    return (grad_keys, grad_values)


def exact_gelu(values):
    return jax.nn.gelu(values, approximate=False)


def twin(array):
    return lax.ppermute(array, "dp_1", [(0, 1), (1, 0)])


def body(tokens, params, out_grad):
    own = jnp.pad(params.reshape(433, 128), ((0, ROWS - 433), (0, 0)))
    weights = unpack(gather(own).reshape(128, ROWS, 128))
    seq_dev, piece, width = tokens.shape
    total_rows = seq_dev * piece
    length = piece * lax.axis_size(SEQ)
    query_pos = lax.axis_index(SEQ) * piece + jnp.arange(piece)
    key_pos = jnp.arange(length)
    inputs = tokens.astype(jnp.float32).reshape(total_rows, width)
    normed1, normal1, factor1 = norm_forward(inputs, weights["ln1_gain"], weights["ln1_shift"])
    normed2, normal2, factor2 = norm_forward(inputs, weights["ln2_gain"], weights["ln2_shift"])
    h_first = normed1.astype(jnp.bfloat16)
    h_second = normed2.astype(jnp.bfloat16)
    qkv = jnp.dot(h_first, weights["w_qkv"], preferred_element_type=jnp.float32) + weights[
        "b_qkv"
    ].astype(jnp.float32)
    shaped = qkv.reshape(seq_dev, piece, 3, HEADS, HEAD_DIM)
    query = rotate(shaped[:, :, 0], query_pos, 1.0).astype(jnp.bfloat16)
    key_part = (
        rotate(shaped[:, :, 1], query_pos, 1.0).astype(jnp.bfloat16).reshape(seq_dev, piece, width)
    )
    value_part = shaped[:, :, 2].astype(jnp.bfloat16).reshape(seq_dev, piece, width)
    keys_all, values_all = in_one_piece((key_part, value_part), SEQ, 1, 0)
    keys_all = keys_all.reshape(seq_dev, length, HEADS, HEAD_DIM)
    values_all = values_all.reshape(seq_dev, length, HEADS, HEAD_DIM)
    sequence = 0
    result, logsum = attend_forward(
        query[sequence], keys_all[sequence], values_all[sequence], query_pos, key_pos
    )
    results = [result]
    logsums = [logsum]
    attended = jnp.stack(results).reshape(total_rows, width).astype(jnp.bfloat16)
    attn_branch = jnp.dot(attended, weights["w_out"], preferred_element_type=jnp.float32) + weights[
        "b_out"
    ].astype(jnp.float32)
    up_value = jnp.dot(h_second, weights["w_up"], preferred_element_type=jnp.float32) + weights[
        "b_up"
    ].astype(jnp.float32)
    act_value, gelu_pull = jax.vjp(exact_gelu, up_value)
    act_low = act_value.astype(jnp.bfloat16)
    mlp_branch = jnp.dot(act_low, weights["w_down"], preferred_element_type=jnp.float32) + weights[
        "b_down"
    ].astype(jnp.float32)
    layer_out = (
        (inputs + attn_branch + mlp_branch).astype(jnp.bfloat16).reshape(seq_dev, piece, width)
    )
    grad_out = out_grad.reshape(total_rows, width)
    grad_float = grad_out.astype(jnp.float32)
    grad_b_down = jnp.sum(grad_float, 0)
    grad_act = jnp.dot(grad_out, weights["w_down"].T, preferred_element_type=jnp.float32)
    grad_up = gelu_pull(grad_act)[0].astype(jnp.bfloat16)
    grad_b_up = jnp.sum(grad_up.astype(jnp.float32), 0)
    grad_h_second = jnp.dot(grad_up, weights["w_up"].T, preferred_element_type=jnp.float32)
    grad_att = jnp.dot(grad_out, weights["w_out"].T, preferred_element_type=jnp.float32).astype(
        jnp.bfloat16
    )
    grad_att = grad_att.reshape(seq_dev, piece, HEADS, HEAD_DIM)
    sequence = 0
    grad_query, inner = query_side(
        query[sequence],
        keys_all[sequence],
        values_all[sequence],
        grad_att[sequence],
        logsums[sequence],
        query_pos,
        key_pos,
    )
    query_grads = [grad_query]
    inners = [inner]
    query_rows, grad_rows = in_one_piece(
        (query.reshape(seq_dev, piece, width), grad_att.reshape(seq_dev, piece, width)), SEQ, 1, 0
    )
    logsum_stack = jnp.stack([entry[..., 0] for entry in logsums])
    logsum_rows, inner_rows = in_one_piece((logsum_stack, jnp.stack(inners)), SEQ, 2, 0)
    query_rows = query_rows.reshape(seq_dev, length, HEADS, HEAD_DIM)
    grad_rows = grad_rows.reshape(seq_dev, length, HEADS, HEAD_DIM)
    own_k = key_part.reshape(seq_dev, piece, HEADS, HEAD_DIM)
    own_v = value_part.reshape(seq_dev, piece, HEADS, HEAD_DIM)
    sequence = 0
    grad_keys, grad_values = key_side(
        query_rows[sequence],
        own_k[sequence],
        own_v[sequence],
        grad_rows[sequence],
        logsum_rows[sequence],
        inner_rows[sequence],
        key_pos,
        query_pos,
    )
    key_list = [grad_keys]
    value_list = [grad_values]
    own_keys = jnp.stack(key_list)
    own_values = jnp.stack(value_list)
    grad_query_low = jnp.stack(query_grads).astype(jnp.bfloat16).astype(jnp.float32)
    grad_keys_low = own_keys.astype(jnp.bfloat16).astype(jnp.float32)
    grad_values_low = own_values.astype(jnp.bfloat16).astype(jnp.float32)
    grad_qkv = jnp.stack(
        [
            rotate(grad_query_low, query_pos, -1.0),
            rotate(grad_keys_low, query_pos, -1.0),
            grad_values_low,
        ],
        2,
    )
    grad_qkv = grad_qkv.reshape(total_rows, 3 * width).astype(jnp.bfloat16)
    grad_b_qkv = jnp.sum(grad_qkv.astype(jnp.float32), 0)
    grad_h_first = jnp.dot(grad_qkv, weights["w_qkv"].T, preferred_element_type=jnp.float32)
    grad_in_first, grad_gain_first, grad_shift_first = norm_backward(
        grad_h_first, normal1, factor1, weights["ln1_gain"]
    )
    grad_in_second, grad_gain_second, grad_shift_second = norm_backward(
        grad_h_second, normal2, factor2, weights["ln2_gain"]
    )
    input_grad = (grad_float + grad_in_first + grad_in_second).reshape(seq_dev, piece, width)
    vectors = [
        grad_gain_first,
        grad_shift_first,
        grad_gain_second,
        grad_shift_second,
        grad_b_qkv,
        grad_b_down,
        grad_b_up,
        grad_b_down,
    ]
    vec = jnp.concatenate(vectors).reshape(-1, 128)
    vec = vec + twin(vec)
    core = lax.axis_index("dp_1").astype(jnp.int32).reshape(1)
    both = lambda a: jnp.concatenate([a, twin(a)], 0)
    halves_sum = weight_grads(
        core,
        vec,
        both(h_first).T,
        both(attended).T,
        both(h_second).T,
        both(act_low).T,
        both(grad_qkv),
        both(grad_out),
        both(grad_up),
    )
    param_grad = scatter(halves_sum.reshape(4, 4, 4, ROWS, 128))[:433].reshape(-1)
    return (layer_out, input_grad, param_grad)


def solution(mesh):
    finer = Mesh(mesh.devices.reshape(4, 2, 4, 4), ("dp_0", "dp_1", "seq_0", "seq_1"))
    in_specs = (P(DP, SEQ, None), P(DP_SEQ), P(DP, SEQ, None))
    out_specs = (P(DP, SEQ, None), P(DP, SEQ, None), P(DP_SEQ))
    return jax.shard_map(body, mesh=finer, in_specs=in_specs, out_specs=out_specs, check_vma=False)
```

```python
import functools
import math

import jax
import jax.numpy as jnp
from jax import lax
from jax.experimental import pallas as pl
from jax.experimental.pallas import tpu as pltpu
from jax.sharding import Mesh
from jax.sharding import PartitionSpec as P

D = 768
HEADS = 12
HEAD_DIM = 64
ROT = 16
FF = 3072
DP_SEQ = ("dp_0", "dp_1", "seq_0", "seq_1")
SEQ = ("seq_0", "seq_1")
DP = ("dp_0", "dp_1")


EPS = 1e-05


MESH = pl.DeviceIdType.MESH
ROWS = 448
PARTS = ((0, 144, (0, 2, 1)), (144, 144, (2, 1, 0)), (288, 160, (1, 0, 2)))


def place():
    return [lax.axis_index("dp_0"), lax.axis_index("seq_0"), lax.axis_index("seq_1")], lax.axis_index("dp_1")


def device(pos, core):
    return (pos[0], core, pos[1], pos[2])


def moved(pos, axis, by):
    out = list(pos)
    out[axis] = lax.rem(pos[axis] + by, 4)
    return out


def greet(pos, core, sibling=True):
    barrier = pltpu.get_barrier_semaphore()
    others = [device(moved(pos, a, by), core) for a in range(3) for by in (1, 3)]
    if sibling:
        others.append(device(pos, 1 - core))
    for other in others:
        pl.semaphore_signal(barrier, inc=1, device_id=other, device_id_type=MESH)
    pl.semaphore_wait(barrier, len(others))


def gather_kernel(own_ref, out_ref, send, recv, sib_send, sib_recv, local):
    pos, core = place()
    greet(pos, core)

    def region(part, where, c, start, size):
        idx = [slice(None) if w is None else w for w in where]
        return out_ref.at[idx[0], c, idx[1], idx[2], pl.ds(start, size), :]

    own = pltpu.make_async_copy(own_ref, out_ref.at[pos[0], core, pos[1], pos[2]], local)
    own.start()
    own.wait()
    sibs = []

    def to_sibling(number, part, where):
        start, size, _ = PARTS[part]
        ref = region(part, where, core, start, size)
        copy = pltpu.make_async_remote_copy(ref, ref, sib_send.at[part, number], sib_recv.at[part, number],
                                            device_id=device(pos, 1 - core), device_id_type=MESH)
        copy.start()
        sibs.append(copy)

    def push(part, phase, number, where, start, size, axis, by):
        ref = region(part, where, core, start, size)
        copy = pltpu.make_async_remote_copy(ref, ref, send.at[part, phase, number], recv.at[part, phase, number],
                                            device_id=device(moved(pos, axis, by), core), device_id_type=MESH)
        copy.start()
        return copy

    def before(order, phase):
        where = [pos[0], pos[1], pos[2]]
        for a in order[:phase]:
            where[a] = None
        return where

    for part in range(3):
        to_sibling(0, part, before(PARTS[part][2], 0))
    for phase in range(3):
        firsts, seconds = [], []
        for part in range(3):
            start, size, order = PARTS[part]
            axis = order[phase]
            where = before(order, phase)
            firsts.append((push(part, phase, 0, where, start, size, axis, 1), push(part, phase, 1, where, start, size, axis, 3)))
        for part in range(3):
            start, size, order = PARTS[part]
            axis = order[phase]
            up, down = firsts[part]
            half = size // 32 * 16
            left = before(order, phase)
            left[axis] = lax.rem(pos[axis] + 3, 4)
            right = before(order, phase)
            right[axis] = lax.rem(pos[axis] + 1, 4)
            up.wait_recv()
            one = push(part, phase, 2, left, start, half, axis, 1)
            to_sibling(1 + 3 * phase, part, left)
            down.wait_recv()
            two = push(part, phase, 3, right, start + half, size - half, axis, 3)
            to_sibling(2 + 3 * phase, part, right)
            seconds.append((one, two))
        for part in range(3):
            start, size, order = PARTS[part]
            axis = order[phase]
            one, two = seconds[part]
            one.wait_recv()
            two.wait_recv()
            far = before(order, phase)
            far[axis] = lax.rem(pos[axis] + 2, 4)
            to_sibling(3 + 3 * phase, part, far)
        for copy in [c for pair in firsts + seconds for c in pair]:
            copy.wait_send()
    for copy in sibs:
        copy.wait_send()
        copy.wait_recv()


def gather(own):
    return pl.pallas_call(
        gather_kernel,
        out_shape=jax.ShapeDtypeStruct((4, 2, 4, 4, ROWS, 128), jnp.bfloat16),
        in_specs=[pl.BlockSpec(memory_space=pl.ANY)],
        out_specs=pl.BlockSpec(memory_space=pl.ANY),
        scratch_shapes=[pltpu.SemaphoreType.DMA((3, 3, 4)), pltpu.SemaphoreType.DMA((3, 3, 4)),
                        pltpu.SemaphoreType.DMA((3, 10)), pltpu.SemaphoreType.DMA((3, 10)), pltpu.SemaphoreType.DMA],
        compiler_params=pltpu.CompilerParams(collective_id=0, has_side_effects=True),
    )(own)


EIGHTH = 16 * 433
W_QKV = (24, 768, 18)
W_OUT = (13866, 768, 6)
W_UP = (18480, 768, 24)
W_DOWN = (36936, 3072, 6)
VECTORS = {"ln1_gain": (0, 6), "ln1_shift": (6, 6), "ln2_gain": (12, 6), "ln2_shift": (18, 6),
           "b_qkv": (13848, 18), "b_out": (18474, 6), "b_up": (36912, 24), "b_down": (55368, 6)}


def unpack_kernel(first, count, plan, g_ref, *rest):
    outs, flat = rest[:-1], rest[-1]
    step = pl.program_id(0)

    @pl.loop(0, 16)
    def _(k):
        base = (step * 16 + k) * 433
        flat[pl.ds(base, 440), :] = g_ref[k, 0:440, :].astype(jnp.float32)

    for (offset, rows, blocks), ready, out in zip(plan, READY[first], outs):
        @pl.when(step == ready - first)
        def _(offset=offset, rows=rows, blocks=blocks, out=out):
            start = offset - first * EIGHTH
            size = 64

            @pl.loop(0, rows // size)
            def _(i):
                for j in range(blocks):
                    piece = flat[pl.ds(start + j + i * (size * blocks), size, stride=blocks), :]
                    out[pl.ds(pl.multiple_of(i * size, size), size), 128 * j:128 * (j + 1)] = piece.astype(jnp.bfloat16)


READY = {0: (1, 2), 2: (5, 7)}


def unpack_call(gathered, first, count, plan):
    whole = lambda rows, cols: pl.BlockSpec((rows, cols), lambda e: (0, 0))
    return pl.pallas_call(
        functools.partial(unpack_kernel, first, count, plan),
        grid=(count,),
        out_shape=[jax.ShapeDtypeStruct((r, 128 * b), jnp.bfloat16) for _, r, b in plan],
        in_specs=[pl.BlockSpec((16, 448, 128), lambda e: (e + first, 0, 0))],
        out_specs=[whole(r, 128 * b) for _, r, b in plan],
        scratch_shapes=[pltpu.VMEM((count * EIGHTH + 16, 128), jnp.float32)],
        compiler_params=pltpu.CompilerParams(vmem_limit_bytes=56 * 2**20),
    )(gathered)


def unpack(gathered):
    w_qkv, w_out = unpack_call(gathered, 0, 3, (W_QKV, W_OUT))
    w_up, w_down = unpack_call(gathered, 2, 6, (W_UP, W_DOWN))
    def vector(name):
        start, rows = VECTORS[name]
        pieces = []
        row = start
        while row < start + rows:
            shard, at = divmod(row, 433)
            take = min(start + rows - row, 433 - at)
            pieces.append(gathered[shard, at:at + take])
            row += take
        return jnp.concatenate(pieces, 0).reshape(-1)
    out = {n: vector(n) for n in VECTORS}
    out.update(w_qkv=w_qkv, w_out=w_out, w_up=w_up, w_down=w_down)
    return out


MARGIN = 384
CHUNK = 128
ORDER = ("ln1_gain", "ln1_shift", "ln2_gain", "ln2_shift", "b_qkv", "b_out", "b_up", "b_down")


def weight_kernel(core_ref, vec_ref, h1_ref, att_ref, h2_ref, act_ref, dqkv_ref, g_ref, dup_ref, out_ref, flat):
    step = pl.program_id(0)
    core = core_ref[0]
    pairs = ((W_QKV, h1_ref, dqkv_ref), (W_OUT, att_ref, g_ref), (W_UP, h2_ref, dup_ref), (W_DOWN, act_ref, g_ref))

    def eighth(number):
        low, high = number * EIGHTH, (number + 1) * EIGHTH
        at = MARGIN - low
        for (offset, rows, blocks), left, right in pairs:
            first = max(0, (low - offset) // blocks) // 16 * 16
            last = min(rows, -(-(high - offset) // blocks))
            last = -(-last // 16) * 16
            if last <= first:
                continue
            size = min(CHUNK, last - first)
            count = -(-(last - first) // size)
            base = offset + at

            @pl.loop(0, count)
            def _(i, first=first, last=last, size=size, blocks=blocks, base=base, left=left, right=right):
                row = pl.multiple_of(jnp.minimum(first + i * size, last - size), 16)
                lhs = left[pl.ds(row, size), :]

                @pl.loop(0, blocks // 2, unroll=3)
                def _(j):
                    rhs = right[:, pl.ds(pl.multiple_of(j * 256, 256), 256)]
                    product = jnp.dot(lhs, rhs, preferred_element_type=jnp.float32)
                    start = base + row * blocks + 2 * j
                    flat[pl.ds(start, size, stride=blocks), :] = product[:, :128]
                    flat[pl.ds(start + 1, size, stride=blocks), :] = product[:, 128:]

        row = 0
        for name in ORDER:
            start, count = VECTORS[name]
            lo, hi = max(start, low), min(start + count, high)
            if lo < hi:
                flat[lo + at:hi + at, :] = vec_ref[row + lo - start:row + hi - start, :]
            row += count
        end = 55374
        if high > end:
            flat[end + at:high + at, :] = jnp.zeros((high - end, 128), jnp.float32)

    for t in range(4):
        for c in range(2):
            pl.when((step == t) & (core == c))(lambda number=2 * t + c: eighth(number))

    @pl.loop(0, 16)
    def _(k):
        out_ref[0, k] = flat[pl.ds(MARGIN + 433 * k, 448), :].astype(jnp.bfloat16)


def weight_grads(core, vec, h1t, att_t, h2t, act_t, dqkv, g, dup):
    whole = pl.BlockSpec(memory_space=pltpu.VMEM)
    return pl.pallas_call(
        weight_kernel,
        grid=(4,),
        out_shape=jax.ShapeDtypeStruct((4, 16, 448, 128), jnp.bfloat16),
        in_specs=[pl.BlockSpec(memory_space=pltpu.SMEM)] + [whole] * 8,
        out_specs=pl.BlockSpec((1, 16, 448, 128), lambda e: (e, 0, 0, 0)),
        scratch_shapes=[pltpu.VMEM((EIGHTH + 2 * MARGIN, 128), jnp.float32)],
        compiler_params=pltpu.CompilerParams(vmem_limit_bytes=48 * 2**20),
    )(core, vec, h1t, att_t, h2t, act_t, dqkv, g, dup)


def halves(size):
    half = size // 32 * 16
    return half, size - half


def pick(ref, axes, axis, index, start, size):
    idx = tuple(index if a == axis else slice(None) for a in axes)
    return ref.at[idx + (pl.ds(start, size), slice(None))]


def each(count, body):
    if count == 0:
        body(())
        return
    @pl.loop(0, 4 ** count)
    def _(n):
        body(tuple(lax.rem(lax.div(n, 4 ** (count - 1 - d)), 4) for d in range(count)))


def scatter_kernel(in_ref, out_ref, *scratch):
    send, recv = scratch[-2:]
    bufs = list(scratch[:-2])
    pos, core = place()
    greet(pos, core, sibling=False)
    take = iter(bufs)
    got = {}
    for part in range(3):
        for phase in range(3):
            got[part, phase] = [next(take) for _ in range(9 if phase < 2 else 8)]

    def push(part, phase, number, src, dst, axis, by):
        copy = pltpu.make_async_remote_copy(src, dst, send.at[part, phase, number], recv.at[part, phase, number],
                                            device_id=device(moved(pos, axis, by), core), device_id_type=MESH)
        copy.start()
        return copy

    def current(part, phase):
        start, size, order = PARTS[part]
        axes = [0, 1, 2]
        for a in order[::-1][:phase]:
            axes.remove(a)
        if phase == 0:
            return in_ref, axes, start
        return got[part, phase - 1][8], axes, 0

    copies = {}

    def begin(part, phase):
        ref, axes, base = current(part, phase)
        start, size, order = PARTS[part]
        axis = order[2 - phase]
        h0, h1 = halves(size)
        q = pos[axis]
        far, right, left = (lax.rem(q + k, 4) for k in (2, 1, 3))
        b = got[part, phase]
        copies[part, phase] = [
            push(part, phase, 0, pick(ref, axes, axis, far, base, h0), b[0], axis, 1),
            push(part, phase, 1, pick(ref, axes, axis, far, base + h0, h1), b[1], axis, 3),
            push(part, phase, 2, pick(ref, axes, axis, right, base + h0, h1), b[2], axis, 1),
            push(part, phase, 3, pick(ref, axes, axis, left, base, h0), b[3], axis, 3),
        ]

    def add(ref, axes, axis, index, base, size, others, put):
        rest = [a for a in axes if a != axis]

        def body(at):
            full = dict(zip(rest, at))
            idx = tuple(index if a == axis else full[a] for a in axes)
            total = ref[idx + (pl.ds(base, size), slice(None))].astype(jnp.float32)
            for other in others:
                total = total + other[at + (slice(None), slice(None))].astype(jnp.float32)
            put(at, total)

        each(len(rest), body)

    def middle(part, phase):
        ref, axes, base = current(part, phase)
        start, size, order = PARTS[part]
        axis = order[2 - phase]
        h0, h1 = halves(size)
        q = pos[axis]
        right, left = (lax.rem(q + k, 4) for k in (1, 3))
        b = got[part, phase]
        c = copies[part, phase]

        def to(ref):
            def put(at, total):
                ref[at + (slice(None), slice(None))] = total.astype(jnp.bfloat16)
            return put

        c[0].wait_recv()
        add(ref, axes, axis, right, base, h0, [b[0]], to(b[6]))
        c.append(push(part, phase, 4, b[6], b[4], axis, 1))
        c[1].wait_recv()
        add(ref, axes, axis, left, base + h0, h1, [b[1]], to(b[7]))
        c.append(push(part, phase, 5, b[7], b[5], axis, 3))

    def finish(part, phase):
        ref, axes, base = current(part, phase)
        start, size, order = PARTS[part]
        axis = order[2 - phase]
        h0, h1 = halves(size)
        q = pos[axis]
        b = got[part, phase]
        c = copies[part, phase]
        for copy in c[2:]:
            copy.wait_recv()
        for lo, n, others in ((0, h0, [b[3], b[4]]), (h0, h1, [b[2], b[5]])):
            def put(at, total, lo=lo, n=n):
                if phase == 2:
                    out_ref[start + lo:start + lo + n, :] = total
                else:
                    b[8][at + (pl.ds(lo, n), slice(None))] = total.astype(jnp.bfloat16)
            add(ref, axes, axis, q, base + lo, n, others, put)

    for phase in range(3):
        for part in range(3):
            if phase == 0:
                begin(part, 0)
        for part in range(3):
            middle(part, phase)
        for part in range(3):
            finish(part, phase)
            if phase < 2:
                begin(part, phase + 1)
    for c in copies.values():
        for copy in c:
            copy.wait_send()


def scatter(parts):
    scratch = []
    for part in range(3):
        _, size, _ = PARTS[part]
        h0, h1 = halves(size)
        for phase in range(3):
            lead = (4,) * (2 - phase)
            sizes = [h0, h1, h1, h0, h0, h1, h0, h1] + ([size] if phase < 2 else [])
            scratch += [pltpu.VMEM(lead + (n, 128), jnp.bfloat16) for n in sizes]
    scratch += [pltpu.SemaphoreType.DMA((3, 3, 6)), pltpu.SemaphoreType.DMA((3, 3, 6))]
    return pl.pallas_call(
        scatter_kernel,
        out_shape=jax.ShapeDtypeStruct((ROWS, 128), jnp.float32),
        in_specs=[pl.BlockSpec(memory_space=pltpu.VMEM)],
        out_specs=pl.BlockSpec(memory_space=pltpu.VMEM),
        scratch_shapes=scratch,
        compiler_params=pltpu.CompilerParams(collective_id=1, has_side_effects=True, vmem_limit_bytes=40 * 2**20),
    )(parts)


TILE = 1024
KEYS = 1024


def exchange_kernel(to_heads, in_ref, out_ref, send, recv, local):
    x, core = lax.axis_index("dp_0"), lax.axis_index("dp_1")
    me = lax.axis_index("seq_0") * 4 + lax.axis_index("seq_1")
    barrier = pltpu.get_barrier_semaphore()
    others = [lax.rem(me + k, 16) for k in range(1, 16)]
    where = lambda t: (x, core, lax.div(t, 4), lax.rem(t, 4))
    for t in others:
        pl.semaphore_signal(barrier, inc=1, device_id=where(t), device_id_type=MESH)
    pl.semaphore_wait(barrier, 15)

    def copy(t):
        return pltpu.make_async_remote_copy(in_ref.at[t], out_ref.at[me], send.at[t], recv.at[me],
                                            device_id=where(t), device_id_type=MESH)

    def arrival(t):
        return pltpu.make_async_remote_copy(out_ref.at[t], out_ref.at[t], send.at[t], recv.at[t],
                                            device_id=where(t), device_id_type=MESH)

    own = pltpu.make_async_copy(in_ref.at[me], out_ref.at[me], local)
    if to_heads:
        for t in others:
            pl.when(t < HEADS)(lambda t=t: copy(t).start())

        @pl.when(me < HEADS)
        def _():
            own.start()
            for t in others:
                arrival(t).wait_recv()
            own.wait()
        for t in others:
            pl.when(t < HEADS)(lambda t=t: copy(t).wait_send())
    else:
        @pl.when(me < HEADS)
        def _():
            for t in others:
                copy(t).start()
            own.start()
        for t in others:
            pl.when(t < HEADS)(lambda t=t: arrival(t).wait_recv())

        @pl.when(me < HEADS)
        def _():
            for t in others:
                copy(t).wait_send()
            own.wait()


def exchange(blocks, to_heads):
    count = 16 if to_heads else HEADS
    return pl.pallas_call(
        functools.partial(exchange_kernel, to_heads),
        out_shape=jax.ShapeDtypeStruct((count,) + blocks.shape[1:], blocks.dtype),
        in_specs=[pl.BlockSpec(memory_space=pl.ANY)],
        out_specs=pl.BlockSpec(memory_space=pl.ANY),
        scratch_shapes=[pltpu.SemaphoreType.DMA((16,)), pltpu.SemaphoreType.DMA((16,)), pltpu.SemaphoreType.DMA],
        compiler_params=pltpu.CompilerParams(collective_id=2 if to_heads else 3, has_side_effects=True),
    )(blocks)


NT = (((1,), (1,)), ((), ()))


def product(a, b, dims=(((1,), (0,)), ((), ()))):
    return lax.dot_general(a, b, dims, preferred_element_type=jnp.float32)


def head_kernel(in_ref, out_ref, k, v, kt, vt, scores, dk, dv):
    blocks = 2048 // TILE
    per = TILE // 128

    def rows(which, i):
        return jnp.concatenate([in_ref[i * per + p, which] for p in range(per)], 0)

    @pl.loop(0, blocks)
    def _(i):
        at = pl.ds(pl.multiple_of(i * TILE, TILE), TILE)
        key = rows(0, i)[:, 64:]
        value = rows(1, i)[:, :64]
        k[at, :] = key
        v[at, :] = value
        kt[:, at] = key.T
        vt[:, at] = value.T
        dk[at, :] = jnp.zeros((TILE, 64), jnp.float32)
        dv[at, :] = jnp.zeros((TILE, 64), jnp.float32)

    @pl.loop(0, blocks)
    def _(i):
        query = rows(0, i)[:, :64] * jnp.bfloat16(0.125)
        grad = rows(1, i)[:, 64:]

        def tile(j):
            return pl.ds(pl.multiple_of(j * KEYS, KEYS), KEYS)

        last = lax.div(i * TILE, KEYS)

        def first(j, top):
            s = product(k[tile(j), :], query, NT)
            scores[tile(j), :] = s
            return jnp.maximum(top, jnp.max(s, 0, keepdims=True))

        top = lax.fori_loop(0, last, first, jnp.full((1, TILE), -1e30, jnp.float32))
        s = product(k[tile(last), :], query, NT)
        keep = lax.broadcasted_iota(jnp.int32, (KEYS, TILE), 0) - lax.broadcasted_iota(jnp.int32, (KEYS, TILE), 1) <= i * TILE - last * KEYS
        s = jnp.where(keep, s, -1e30)
        scores[tile(last), :] = s
        top = jnp.maximum(top, jnp.max(s, 0, keepdims=True))

        def second(j, carry):
            total, out = carry
            e = jnp.exp(scores[tile(j), :] - top)
            scores[tile(j), :] = e
            return total + jnp.sum(e, 0, keepdims=True), out + product(vt[:, tile(j)], e.astype(jnp.bfloat16))

        total, out = lax.fori_loop(0, last + 1, second, (jnp.zeros((1, TILE), jnp.float32), jnp.zeros((64, TILE), jnp.float32)))
        scale = 1.0 / total
        out = out * scale
        inner = jnp.sum(out * grad.astype(jnp.float32).T, 0, keepdims=True)

        def third(j, dq):
            p = scores[tile(j), :] * scale
            dp = product(v[tile(j), :], grad, NT)
            ds = (p * (dp - inner)).astype(jnp.bfloat16)
            dv[tile(j), :] += product(p.astype(jnp.bfloat16), grad)
            dk[tile(j), :] += product(ds, query)
            return dq + product(kt[:, tile(j)], ds)

        dq = lax.fori_loop(0, last + 1, third, jnp.zeros((64, TILE), jnp.float32)) * 0.125
        both = jnp.concatenate([out, dq], 0).T.astype(jnp.bfloat16)
        for p in range(per):
            out_ref[i * per + p, 0] = both[128 * p:128 * (p + 1)]

    @pl.loop(0, blocks)
    def _(i):
        at = pl.ds(pl.multiple_of(i * TILE, TILE), TILE)
        both = jnp.concatenate([dk[at, :], dv[at, :]], 1).astype(jnp.bfloat16)
        for p in range(per):
            out_ref[i * per + p, 1] = both[128 * p:128 * (p + 1)]


def heads(blocks):
    return pl.pallas_call(
        head_kernel,
        out_shape=jax.ShapeDtypeStruct((16, 2, 128, 128), jnp.bfloat16),
        in_specs=[pl.BlockSpec(memory_space=pltpu.VMEM)],
        out_specs=pl.BlockSpec(memory_space=pltpu.VMEM),
        scratch_shapes=[pltpu.VMEM((2048, 64), jnp.bfloat16), pltpu.VMEM((2048, 64), jnp.bfloat16),
                        pltpu.VMEM((64, 2048), jnp.bfloat16), pltpu.VMEM((64, 2048), jnp.bfloat16),
                        pltpu.VMEM((2048, TILE), jnp.float32),
                        pltpu.VMEM((2048, 64), jnp.float32), pltpu.VMEM((2048, 64), jnp.float32)],
        compiler_params=pltpu.CompilerParams(vmem_limit_bytes=32 * 2**20),
    )(blocks)


def norm_forward(values, gain, shift):
    center = jnp.mean(values, -1, keepdims=True)
    centered = values - center
    spread = jnp.mean(centered * centered, -1, keepdims=True)
    factor = lax.rsqrt(spread + EPS)
    normal = centered * factor
    return (normal * gain.astype(jnp.float32) + shift.astype(jnp.float32), normal, factor)


def norm_backward(grad_out, normal, factor, gain):
    grad_gain = jnp.sum(grad_out * normal, 0)
    grad_shift = jnp.sum(grad_out, 0)
    scaled = grad_out * gain.astype(jnp.float32)
    inner = (
        scaled
        - jnp.mean(scaled, -1, keepdims=True)
        - normal * jnp.mean(scaled * normal, -1, keepdims=True)
    )
    return (factor * inner, grad_gain, grad_shift)


def rotate(tensor, positions, sign):
    half = ROT // 2
    freq = 10000.0 ** (-jnp.arange(half).astype(jnp.float32) * 2.0 / ROT)
    angles = positions.astype(jnp.float32)[:, None] * freq[None, :]
    cosine = jnp.cos(angles)[:, None, :]
    sine = jnp.sin(angles)[:, None, :] * sign
    first = tensor[..., :half]
    second = tensor[..., half:ROT]
    return jnp.concatenate(
        [first * cosine - second * sine, second * cosine + first * sine, tensor[..., ROT:]], -1
    )


def exact_gelu(values):
    return jax.nn.gelu(values, approximate=False)


def twin(array):
    return lax.ppermute(array, "dp_1", [(0, 1), (1, 0)])


def body(tokens, params, out_grad):
    own = jnp.pad(params.reshape(433, 128), ((0, ROWS - 433), (0, 0)))
    weights = unpack(gather(own).reshape(128, ROWS, 128))
    seq_dev, piece, width = tokens.shape
    total_rows = seq_dev * piece
    query_pos = lax.axis_index(SEQ) * piece + jnp.arange(piece)
    inputs = tokens.astype(jnp.float32).reshape(total_rows, width)
    normed1, normal1, factor1 = norm_forward(inputs, weights["ln1_gain"], weights["ln1_shift"])
    normed2, normal2, factor2 = norm_forward(inputs, weights["ln2_gain"], weights["ln2_shift"])
    h_first = normed1.astype(jnp.bfloat16)
    h_second = normed2.astype(jnp.bfloat16)
    qkv = jnp.dot(h_first, weights["w_qkv"], preferred_element_type=jnp.float32) + weights[
        "b_qkv"
    ].astype(jnp.float32)
    shaped = qkv.reshape(seq_dev, piece, 3, HEADS, HEAD_DIM)
    grad_out = out_grad.reshape(total_rows, width)
    grad_att = jnp.dot(grad_out, weights["w_out"].T, preferred_element_type=jnp.float32).astype(
        jnp.bfloat16
    )
    query = rotate(shaped[0, :, 0], query_pos, 1.0).astype(jnp.bfloat16)
    key = rotate(shaped[0, :, 1], query_pos, 1.0).astype(jnp.bfloat16)
    value = shaped[0, :, 2].astype(jnp.bfloat16)
    blocks = jnp.stack(
        [
            jnp.concatenate([query, key], -1),
            jnp.concatenate([value, grad_att.reshape(piece, HEADS, HEAD_DIM)], -1),
        ]
    )
    back = exchange(heads(exchange(blocks.transpose(2, 0, 1, 3), True)), False)
    back = back.transpose(1, 2, 0, 3)
    attended = back[0, :, :, :HEAD_DIM].reshape(total_rows, width)
    attn_branch = jnp.dot(attended, weights["w_out"], preferred_element_type=jnp.float32) + weights[
        "b_out"
    ].astype(jnp.float32)
    up_value = jnp.dot(h_second, weights["w_up"], preferred_element_type=jnp.float32) + weights[
        "b_up"
    ].astype(jnp.float32)
    act_value, gelu_pull = jax.vjp(exact_gelu, up_value)
    act_low = act_value.astype(jnp.bfloat16)
    mlp_branch = jnp.dot(act_low, weights["w_down"], preferred_element_type=jnp.float32) + weights[
        "b_down"
    ].astype(jnp.float32)
    layer_out = (
        (inputs + attn_branch + mlp_branch).astype(jnp.bfloat16).reshape(seq_dev, piece, width)
    )
    grad_float = grad_out.astype(jnp.float32)
    grad_b_down = jnp.sum(grad_float, 0)
    grad_act = jnp.dot(grad_out, weights["w_down"].T, preferred_element_type=jnp.float32)
    grad_up = gelu_pull(grad_act)[0].astype(jnp.bfloat16)
    grad_b_up = jnp.sum(grad_up.astype(jnp.float32), 0)
    grad_h_second = jnp.dot(grad_up, weights["w_up"].T, preferred_element_type=jnp.float32)
    grad_qkv = jnp.stack(
        [
            rotate(back[0, :, :, HEAD_DIM:].astype(jnp.float32), query_pos, -1.0),
            rotate(back[1, :, :, :HEAD_DIM].astype(jnp.float32), query_pos, -1.0),
            back[1, :, :, HEAD_DIM:].astype(jnp.float32),
        ],
        1,
    )
    grad_qkv = grad_qkv.reshape(total_rows, 3 * width).astype(jnp.bfloat16)
    grad_b_qkv = jnp.sum(grad_qkv.astype(jnp.float32), 0)
    grad_h_first = jnp.dot(grad_qkv, weights["w_qkv"].T, preferred_element_type=jnp.float32)
    grad_in_first, grad_gain_first, grad_shift_first = norm_backward(
        grad_h_first, normal1, factor1, weights["ln1_gain"]
    )
    grad_in_second, grad_gain_second, grad_shift_second = norm_backward(
        grad_h_second, normal2, factor2, weights["ln2_gain"]
    )
    input_grad = (grad_float + grad_in_first + grad_in_second).reshape(seq_dev, piece, width)
    vectors = [
        grad_gain_first,
        grad_shift_first,
        grad_gain_second,
        grad_shift_second,
        grad_b_qkv,
        grad_b_down,
        grad_b_up,
        grad_b_down,
    ]
    vec = jnp.concatenate(vectors).reshape(-1, 128)
    vec = vec + twin(vec)
    core = lax.axis_index("dp_1").astype(jnp.int32).reshape(1)
    both = lambda a: jnp.concatenate([a, twin(a)], 0)
    halves_sum = weight_grads(
        core,
        vec,
        both(h_first).T,
        both(attended).T,
        both(h_second).T,
        both(act_low).T,
        both(grad_qkv),
        both(grad_out),
        both(grad_up),
    )
    param_grad = scatter(halves_sum.reshape(4, 4, 4, ROWS, 128))[:433].reshape(-1)
    return (layer_out, input_grad, param_grad)


def solution(mesh):
    finer = Mesh(mesh.devices.reshape(4, 2, 4, 4), ("dp_0", "dp_1", "seq_0", "seq_1"))
    in_specs = (P(DP, SEQ, None), P(DP_SEQ), P(DP, SEQ, None))
    out_specs = (P(DP, SEQ, None), P(DP, SEQ, None), P(DP_SEQ))
    return jax.shard_map(body, mesh=finer, in_specs=in_specs, out_specs=out_specs, check_vma=False)
```

```python
import functools

import jax
import jax.numpy as jnp
from jax import lax
from jax.experimental import pallas as pl
from jax.experimental.pallas import tpu as pltpu
from jax.sharding import Mesh
from jax.sharding import PartitionSpec as P

DP_SEQ = ("dp_0", "dp_1", "seq_0", "seq_1")
SEQ = ("seq_0", "seq_1")
DP = ("dp_0", "dp_1")
MESH = pl.DeviceIdType.MESH
ROWS = 448
PARTS = ((0, 144, (0, 2, 1)), (144, 144, (2, 1, 0)), (288, 160, (1, 0, 2)))


def place():
    return [lax.axis_index("dp_0"), lax.axis_index("seq_0"), lax.axis_index("seq_1")], lax.axis_index("dp_1")


def device(pos, core):
    return (pos[0], core, pos[1], pos[2])


def moved(pos, axis, by):
    out = list(pos)
    out[axis] = lax.rem(pos[axis] + by, 4)
    return out


def greet(pos, core, sibling=True):
    barrier = pltpu.get_barrier_semaphore()
    others = [device(moved(pos, a, by), core) for a in range(3) for by in (1, 3)]
    if sibling:
        others.append(device(pos, 1 - core))
    for other in others:
        pl.semaphore_signal(barrier, inc=1, device_id=other, device_id_type=MESH)
    pl.semaphore_wait(barrier, len(others))


def gather_kernel(own_ref, out_ref, send, recv, sib_send, sib_recv, local):
    pos, core = place()
    greet(pos, core)

    def region(part, where, c, start, size):
        idx = [slice(None) if w is None else w for w in where]
        return out_ref.at[idx[0], c, idx[1], idx[2], pl.ds(start, size), :]

    own = pltpu.make_async_copy(own_ref, out_ref.at[pos[0], core, pos[1], pos[2]], local)
    own.start()
    own.wait()
    sibs = []

    def to_sibling(number, part, where):
        start, size, _ = PARTS[part]
        ref = region(part, where, core, start, size)
        copy = pltpu.make_async_remote_copy(ref, ref, sib_send.at[part, number], sib_recv.at[part, number],
                                            device_id=device(pos, 1 - core), device_id_type=MESH)
        copy.start()
        sibs.append(copy)

    def push(part, phase, number, where, start, size, axis, by):
        ref = region(part, where, core, start, size)
        copy = pltpu.make_async_remote_copy(ref, ref, send.at[part, phase, number], recv.at[part, phase, number],
                                            device_id=device(moved(pos, axis, by), core), device_id_type=MESH)
        copy.start()
        return copy

    def before(order, phase):
        where = [pos[0], pos[1], pos[2]]
        for a in order[:phase]:
            where[a] = None
        return where

    for part in range(3):
        to_sibling(0, part, before(PARTS[part][2], 0))
    for phase in range(3):
        firsts, seconds = [], []
        for part in range(3):
            start, size, order = PARTS[part]
            axis = order[phase]
            where = before(order, phase)
            firsts.append((push(part, phase, 0, where, start, size, axis, 1), push(part, phase, 1, where, start, size, axis, 3)))
        for part in range(3):
            start, size, order = PARTS[part]
            axis = order[phase]
            up, down = firsts[part]
            half = size // 32 * 16
            left = before(order, phase)
            left[axis] = lax.rem(pos[axis] + 3, 4)
            right = before(order, phase)
            right[axis] = lax.rem(pos[axis] + 1, 4)
            up.wait_recv()
            one = push(part, phase, 2, left, start, half, axis, 1)
            to_sibling(1 + 3 * phase, part, left)
            down.wait_recv()
            two = push(part, phase, 3, right, start + half, size - half, axis, 3)
            to_sibling(2 + 3 * phase, part, right)
            seconds.append((one, two))
        for part in range(3):
            start, size, order = PARTS[part]
            axis = order[phase]
            one, two = seconds[part]
            one.wait_recv()
            two.wait_recv()
            far = before(order, phase)
            far[axis] = lax.rem(pos[axis] + 2, 4)
            to_sibling(3 + 3 * phase, part, far)
        for copy in [c for pair in firsts + seconds for c in pair]:
            copy.wait_send()
    for copy in sibs:
        copy.wait_send()
        copy.wait_recv()


def gather(own):
    return pl.pallas_call(
        gather_kernel,
        out_shape=jax.ShapeDtypeStruct((4, 2, 4, 4, ROWS, 128), jnp.bfloat16),
        in_specs=[pl.BlockSpec(memory_space=pl.ANY)],
        out_specs=pl.BlockSpec(memory_space=pl.ANY),
        scratch_shapes=[pltpu.SemaphoreType.DMA((3, 3, 4)), pltpu.SemaphoreType.DMA((3, 3, 4)),
                        pltpu.SemaphoreType.DMA((3, 10)), pltpu.SemaphoreType.DMA((3, 10)), pltpu.SemaphoreType.DMA],
        compiler_params=pltpu.CompilerParams(collective_id=0, has_side_effects=True),
    )(own)


EIGHTH = 16 * 433
W_QKV = (24, 768, 18)
W_OUT = (13866, 768, 6)
W_UP = (18480, 768, 24)
W_DOWN = (36936, 3072, 6)
VECTORS = {"ln1_gain": (0, 6), "ln1_shift": (6, 6), "ln2_gain": (12, 6), "ln2_shift": (18, 6),
           "b_qkv": (13848, 18), "b_out": (18474, 6), "b_up": (36912, 24), "b_down": (55368, 6)}


HEADS = 12
TILE = 1024
KEYS = 1024


def exchange_kernel(to_heads, in_ref, out_ref, send, recv, local):
    x, core = lax.axis_index("dp_0"), lax.axis_index("dp_1")
    me = lax.axis_index("seq_0") * 4 + lax.axis_index("seq_1")
    barrier = pltpu.get_barrier_semaphore()
    others = [lax.rem(me + k, 16) for k in range(1, 16)]
    where = lambda t: (x, core, lax.div(t, 4), lax.rem(t, 4))
    for t in others:
        pl.semaphore_signal(barrier, inc=1, device_id=where(t), device_id_type=MESH)
    pl.semaphore_wait(barrier, 15)

    def copy(t):
        return pltpu.make_async_remote_copy(in_ref.at[t], out_ref.at[me], send.at[t], recv.at[me],
                                            device_id=where(t), device_id_type=MESH)

    def arrival(t):
        return pltpu.make_async_remote_copy(out_ref.at[t], out_ref.at[t], send.at[t], recv.at[t],
                                            device_id=where(t), device_id_type=MESH)

    own = pltpu.make_async_copy(in_ref.at[me], out_ref.at[me], local)
    if to_heads:
        for t in others:
            pl.when(t < HEADS)(lambda t=t: copy(t).start())

        @pl.when(me < HEADS)
        def _():
            own.start()
            for t in others:
                arrival(t).wait_recv()
            own.wait()
        for t in others:
            pl.when(t < HEADS)(lambda t=t: copy(t).wait_send())
    else:
        @pl.when(me < HEADS)
        def _():
            for t in others:
                copy(t).start()
            own.start()
        for t in others:
            pl.when(t < HEADS)(lambda t=t: arrival(t).wait_recv())

        @pl.when(me < HEADS)
        def _():
            for t in others:
                copy(t).wait_send()
            own.wait()


def exchange(blocks, to_heads):
    count = 16 if to_heads else HEADS
    return pl.pallas_call(
        functools.partial(exchange_kernel, to_heads),
        out_shape=jax.ShapeDtypeStruct((count,) + blocks.shape[1:], blocks.dtype),
        in_specs=[pl.BlockSpec(memory_space=pl.ANY)],
        out_specs=pl.BlockSpec(memory_space=pl.ANY),
        scratch_shapes=[pltpu.SemaphoreType.DMA((16,)), pltpu.SemaphoreType.DMA((16,)), pltpu.SemaphoreType.DMA],
        compiler_params=pltpu.CompilerParams(collective_id=2 if to_heads else 3, has_side_effects=True),
    )(blocks)


NT = (((1,), (1,)), ((), ()))


def product(a, b, dims=(((1,), (0,)), ((), ()))):
    return lax.dot_general(a, b, dims, preferred_element_type=jnp.float32)


def head_kernel(in_ref, out_ref, k, v, kt, vt, scores, dk, dv):
    blocks = 2048 // TILE
    per = TILE // 128

    def rows(which, i):
        return jnp.concatenate([in_ref[i * per + p, which] for p in range(per)], 0)

    @pl.loop(0, blocks)
    def _(i):
        at = pl.ds(pl.multiple_of(i * TILE, TILE), TILE)
        key = rows(0, i)[:, 64:]
        value = rows(1, i)[:, :64]
        k[at, :] = key
        v[at, :] = value
        kt[:, at] = key.T
        vt[:, at] = value.T
        dk[at, :] = jnp.zeros((TILE, 64), jnp.float32)
        dv[at, :] = jnp.zeros((TILE, 64), jnp.float32)

    @pl.loop(0, blocks)
    def _(i):
        query = rows(0, i)[:, :64] * jnp.bfloat16(0.125)
        grad = rows(1, i)[:, 64:]

        def tile(j):
            return pl.ds(pl.multiple_of(j * KEYS, KEYS), KEYS)

        last = lax.div(i * TILE, KEYS)

        def first(j, top):
            s = product(k[tile(j), :], query, NT)
            scores[tile(j), :] = s
            return jnp.maximum(top, jnp.max(s, 0, keepdims=True))

        top = lax.fori_loop(0, last, first, jnp.full((1, TILE), -1e30, jnp.float32))
        s = product(k[tile(last), :], query, NT)
        keep = lax.broadcasted_iota(jnp.int32, (KEYS, TILE), 0) - lax.broadcasted_iota(jnp.int32, (KEYS, TILE), 1) <= i * TILE - last * KEYS
        s = jnp.where(keep, s, -1e30)
        scores[tile(last), :] = s
        top = jnp.maximum(top, jnp.max(s, 0, keepdims=True))

        def second(j, carry):
            total, out = carry
            e = jnp.exp(scores[tile(j), :] - top)
            scores[tile(j), :] = e
            return total + jnp.sum(e, 0, keepdims=True), out + product(vt[:, tile(j)], e.astype(jnp.bfloat16))

        total, out = lax.fori_loop(0, last + 1, second, (jnp.zeros((1, TILE), jnp.float32), jnp.zeros((64, TILE), jnp.float32)))
        scale = 1.0 / total
        out = out * scale
        inner = jnp.sum(out * grad.astype(jnp.float32).T, 0, keepdims=True)

        def third(j, dq):
            p = scores[tile(j), :] * scale
            dp = product(v[tile(j), :], grad, NT)
            ds = (p * (dp - inner)).astype(jnp.bfloat16)
            dv[tile(j), :] += product(p.astype(jnp.bfloat16), grad)
            dk[tile(j), :] += product(ds, query)
            return dq + product(kt[:, tile(j)], ds)

        dq = lax.fori_loop(0, last + 1, third, jnp.zeros((64, TILE), jnp.float32)) * 0.125
        both = jnp.concatenate([out, dq], 0).T.astype(jnp.bfloat16)
        for p in range(per):
            out_ref[i * per + p, 0] = both[128 * p:128 * (p + 1)]

    @pl.loop(0, blocks)
    def _(i):
        at = pl.ds(pl.multiple_of(i * TILE, TILE), TILE)
        both = jnp.concatenate([dk[at, :], dv[at, :]], 1).astype(jnp.bfloat16)
        for p in range(per):
            out_ref[i * per + p, 1] = both[128 * p:128 * (p + 1)]


def heads(blocks):
    return pl.pallas_call(
        head_kernel,
        out_shape=jax.ShapeDtypeStruct((16, 2, 128, 128), jnp.bfloat16),
        in_specs=[pl.BlockSpec(memory_space=pltpu.VMEM)],
        out_specs=pl.BlockSpec(memory_space=pltpu.VMEM),
        scratch_shapes=[pltpu.VMEM((2048, 64), jnp.bfloat16), pltpu.VMEM((2048, 64), jnp.bfloat16),
                        pltpu.VMEM((64, 2048), jnp.bfloat16), pltpu.VMEM((64, 2048), jnp.bfloat16),
                        pltpu.VMEM((2048, TILE), jnp.float32),
                        pltpu.VMEM((2048, 64), jnp.float32), pltpu.VMEM((2048, 64), jnp.float32)],
        compiler_params=pltpu.CompilerParams(vmem_limit_bytes=32 * 2**20),
    )(blocks)


EPS = 1e-05
ORDER = ("ln1_gain", "ln1_shift", "ln2_gain", "ln2_shift", "b_qkv", "b_out", "b_up", "b_down")


def widen(g_ref, flat, step):
    @pl.loop(0, 16)
    def _(k):
        base = (step * 16 + k) * 433
        flat[pl.ds(base, 440), :] = g_ref[k, 0:440, :].astype(jnp.float32)


def unpack_matrix(flat, first, where, out, size=64):
    offset, rows, blocks = where
    start = offset - first * EIGHTH

    @pl.loop(0, rows // size)
    def _(i):
        for j in range(blocks):
            piece = flat[pl.ds(start + j + i * (size * blocks), size, stride=blocks), :]
            out[pl.ds(pl.multiple_of(i * size, size), size), 128 * j:128 * (j + 1)] = piece.astype(jnp.bfloat16)


def as_row(ref, start, count):
    return jnp.concatenate([ref[start + n:start + n + 1, :] for n in range(count)], 1)


def to_rows(ref, start, row):
    for n in range(row.shape[1] // 128):
        ref[start + n:start + n + 1, :] = row[:, 128 * n:128 * (n + 1)]


def normalized(values):
    center = jnp.mean(values, -1, keepdims=True)
    centered = values - center
    factor = lax.rsqrt(jnp.mean(centered * centered, -1, keepdims=True) + EPS)
    return centered * factor, factor


def turn(x, tables, sign):
    return x * tables[0] + (pltpu.roll(x, 120, 1) * tables[1] + pltpu.roll(x, 8, 1) * tables[2]) * sign


def first_kernel(g_ref, tokens_ref, grad_ref, tables_ref, w_qkv, w_out, blocks_ref, h1t_ref, h2_ref, h2t_ref, vec_ref, flat, wide):
    step = pl.program_id(0)
    widen(g_ref, flat, step)

    @pl.when(step == 1)
    def _():
        unpack_matrix(flat, 0, W_QKV, w_qkv)

    @pl.when(step == 2)
    def _():
        unpack_matrix(flat, 0, W_OUT, w_out)
        vec_ref[0:24, :] = flat[0:24, :]
        start = VECTORS["b_out"][0]
        vec_ref[24:30, :] = flat[start:start + 6, :]
        normal, _ = normalized(tokens_ref[...].astype(jnp.float32))
        h1 = (normal * as_row(flat, 0, 6) + as_row(flat, 6, 6)).astype(jnp.bfloat16)
        h2 = (normal * as_row(flat, 12, 6) + as_row(flat, 18, 6)).astype(jnp.bfloat16)
        h1t_ref[...] = h1.T
        h2_ref[...] = h2
        h2t_ref[...] = h2.T
        for n in range(9):
            start = VECTORS["b_qkv"][0] + 2 * n
            wide[:, 256 * n:256 * (n + 1)] = product(h1, w_qkv[:, 256 * n:256 * (n + 1)]) + as_row(flat, start, 2)
        low = lax.broadcasted_iota(jnp.int32, (128, 128), 1) < 64
        for m in range(6):
            q, k, v = (wide[:, 768 * p + 128 * m:768 * p + 128 * (m + 1)] for p in range(3))
            q = turn(q, tables_ref, 1.0)
            k = turn(k, tables_ref, 1.0)
            a = product(grad_ref[...], w_out[128 * m:128 * (m + 1), :], NT)
            swap = lambda t: pltpu.roll(t, 64, 1)
            blocks_ref[2 * m, 0] = jnp.where(low, q, swap(k)).astype(jnp.bfloat16)
            blocks_ref[2 * m + 1, 0] = jnp.where(low, swap(q), k).astype(jnp.bfloat16)
            blocks_ref[2 * m, 1] = jnp.where(low, v, swap(a)).astype(jnp.bfloat16)
            blocks_ref[2 * m + 1, 1] = jnp.where(low, swap(v), a).astype(jnp.bfloat16)


def const(*shape):
    return pl.BlockSpec(shape, lambda e: (0,) * len(shape))


def first_part(gathered, tokens, grad, tables):
    bf = lambda *s: jax.ShapeDtypeStruct(s, jnp.bfloat16)
    outs = [bf(768, 2304), bf(768, 768), bf(HEADS, 2, 128, 128), bf(768, 128), bf(128, 768), bf(768, 128),
            jax.ShapeDtypeStruct((32, 128), jnp.float32)]
    return pl.pallas_call(
        first_kernel,
        grid=(3,),
        out_shape=outs,
        in_specs=[pl.BlockSpec((16, 448, 128), lambda e: (e, 0, 0)), const(128, 768), const(128, 768), const(3, 128, 128)],
        out_specs=[const(*o.shape) for o in outs],
        scratch_shapes=[pltpu.VMEM((3 * EIGHTH + 16, 128), jnp.float32), pltpu.VMEM((128, 2304), jnp.float32)],
        compiler_params=pltpu.CompilerParams(vmem_limit_bytes=48 * 2**20),
    )(gathered, tokens, grad, tables)


def gelu_pair(u):
    inside = 0.5 * (1.0 + lax.erf(u * 0.7071067811865476))
    return u * inside, inside + u * jnp.exp(-0.5 * u * u) * 0.3989422804014327


def second_kernel(g_ref, h2_ref, grad_ref, mlp_ref, dh2_ref, act_t_ref, dup_ref, bias_ref, flat, w_up, w_down, act, slope):
    step = pl.program_id(0)
    widen(g_ref, flat, step)

    @pl.when(step == 3)
    def _():
        unpack_matrix(flat, 2, W_UP, w_up)
        start = VECTORS["b_up"][0] - 2 * EIGHTH
        for n in range(12):
            at = slice(256 * n, 256 * (n + 1))
            up = product(h2_ref[...], w_up[:, at]) + as_row(flat, start + 2 * n, 2)
            value, slope[:, at] = gelu_pair(up)
            value = value.astype(jnp.bfloat16)
            act[:, at] = value
            act_t_ref[at, :] = value.T

    @pl.when(step == 5)
    def _():
        unpack_matrix(flat, 2, W_DOWN, w_down, 128)
        start = VECTORS["b_down"][0] - 2 * EIGHTH
        for n in range(3):
            at = slice(256 * n, 256 * (n + 1))
            mlp_ref[:, at] = product(act[...], w_down[:, at]) + as_row(flat, start + 2 * n, 2)
        for n in range(12):
            at = slice(256 * n, 256 * (n + 1))
            dup = (product(grad_ref[...], w_down[at, :], NT) * slope[:, at]).astype(jnp.bfloat16)
            dup_ref[:, at] = dup
            to_rows(bias_ref, 2 * n, jnp.sum(dup.astype(jnp.float32), 0, keepdims=True))
        for n in range(3):
            at = slice(256 * n, 256 * (n + 1))
            dh2_ref[:, at] = product(dup_ref[...], w_up[at, :], NT)


def second_part(gathered, h2, grad):
    bf = lambda *s: jax.ShapeDtypeStruct(s, jnp.bfloat16)
    f32 = lambda *s: jax.ShapeDtypeStruct(s, jnp.float32)
    outs = [f32(128, 768), f32(128, 768), bf(3072, 128), bf(128, 3072), f32(24, 128)]
    return pl.pallas_call(
        second_kernel,
        grid=(6,),
        out_shape=outs,
        in_specs=[pl.BlockSpec((16, 448, 128), lambda e: (e + 2, 0, 0)), const(128, 768), const(128, 768)],
        out_specs=[const(*o.shape) for o in outs],
        scratch_shapes=[pltpu.VMEM((6 * EIGHTH + 16, 128), jnp.float32), pltpu.VMEM((768, 3072), jnp.bfloat16),
                        pltpu.VMEM((3072, 768), jnp.bfloat16), pltpu.VMEM((128, 3072), jnp.bfloat16),
                        pltpu.VMEM((128, 3072), jnp.float32)],
        compiler_params=pltpu.CompilerParams(vmem_limit_bytes=56 * 2**20),
    )(gathered, h2, grad)


def third_kernel(back_ref, tokens_ref, grad_ref, tables_ref, w_qkv, w_out, mlp_ref, dh2_ref, bias_ref, in_vec,
                 layer_ref, input_ref, att_t_ref, dqkv_ref, vec_ref):
    low = lax.broadcasted_iota(jnp.int32, (128, 128), 1) < 64
    swap = lambda t: pltpu.roll(t, 64, 1)
    f32 = lambda t: t.astype(jnp.float32)
    attended = []
    for m in range(6):
        a, b = f32(back_ref[2 * m, 0]), f32(back_ref[2 * m + 1, 0])
        c, d = f32(back_ref[2 * m, 1]), f32(back_ref[2 * m + 1, 1])
        attended.append(jnp.where(low, a, swap(b)).astype(jnp.bfloat16))
        dq = turn(jnp.where(low, swap(a), b), tables_ref, -1.0)
        dk = turn(jnp.where(low, c, swap(d)), tables_ref, -1.0)
        dv = jnp.where(low, swap(c), d)
        for p, part in enumerate((dq, dk, dv)):
            dqkv_ref[:, 768 * p + 128 * m:768 * p + 128 * (m + 1)] = part.astype(jnp.bfloat16)
    attended = jnp.concatenate(attended, 1)
    att_t_ref[...] = attended.T
    tokens = f32(tokens_ref[...])
    grad = f32(grad_ref[...])
    layer_ref[...] = (tokens + (product(attended, w_out[...]) + as_row(in_vec, 24, 6)) + mlp_ref[...]).astype(jnp.bfloat16)
    normal, factor = normalized(tokens)
    total = grad
    row = 0
    for gain_at, dh in ((0, product(dqkv_ref[...], w_qkv[...], NT)), (12, dh2_ref[...])):
        to_rows(vec_ref, row, jnp.sum(dh * normal, 0, keepdims=True))
        to_rows(vec_ref, row + 6, jnp.sum(dh, 0, keepdims=True))
        row += 12
        scaled = dh * as_row(in_vec, gain_at, 6)
        inner = scaled - jnp.mean(scaled, -1, keepdims=True) - normal * jnp.mean(scaled * normal, -1, keepdims=True)
        total = total + factor * inner
    input_ref[...] = total
    to_rows(vec_ref, 24, jnp.sum(f32(dqkv_ref[...]), 0, keepdims=True))
    shift = jnp.sum(grad, 0, keepdims=True)
    to_rows(vec_ref, 42, shift)
    vec_ref[48:72, :] = bias_ref[...]
    to_rows(vec_ref, 72, shift)
    vec_ref[78:80, :] = jnp.zeros((2, 128), jnp.float32)


def third_part(*args):
    bf = lambda *s: jax.ShapeDtypeStruct(s, jnp.bfloat16)
    f32 = lambda *s: jax.ShapeDtypeStruct(s, jnp.float32)
    outs = [bf(128, 768), f32(128, 768), bf(768, 128), bf(128, 2304), f32(80, 128)]
    whole = pl.BlockSpec(memory_space=pltpu.VMEM)
    return pl.pallas_call(
        third_kernel,
        out_shape=outs,
        in_specs=[whole] * len(args),
        out_specs=[whole] * len(outs),
        compiler_params=pltpu.CompilerParams(vmem_limit_bytes=32 * 2**20),
    )(*args)


def rotary_tables(positions):
    lane = jnp.arange(128) % 64
    freq = jnp.tile(10000.0 ** (-jnp.arange(8).astype(jnp.float32) * 2.0 / 16), 16)
    angles = positions.astype(jnp.float32)[:, None] * freq[None, :]
    cosine, sine = jnp.cos(angles), jnp.sin(angles)
    return jnp.stack([jnp.where(lane < 16, cosine, 1.0), jnp.where(lane < 8, -sine, 0.0),
                      jnp.where((lane >= 8) & (lane < 16), sine, 0.0)])


MARGIN = 384
CHUNK = 128


def weight_kernel(core_ref, vec_ref, *refs):
    mine, theirs, (out_ref, flat), pair = refs[:7], refs[7:14], refs[14:16], refs[16:]
    step = pl.program_id(0)
    core = core_ref[0]

    @pl.when(step == 0)
    def _():
        for n in range(7):
            if n < 4:
                pair[n][:, :128] = mine[n][...]
                pair[n][:, 128:] = theirs[n][...]
            else:
                pair[n][:128, :] = mine[n][...]
                pair[n][128:, :] = theirs[n][...]

    h1_ref, att_ref, h2_ref, act_ref, dqkv_ref, g_ref, dup_ref = pair
    pairs = ((W_QKV, h1_ref, dqkv_ref), (W_OUT, att_ref, g_ref), (W_UP, h2_ref, dup_ref), (W_DOWN, act_ref, g_ref))

    def eighth(number):
        low, high = number * EIGHTH, (number + 1) * EIGHTH
        at = MARGIN - low
        for (offset, rows, blocks), left, right in pairs:
            first = max(0, (low - offset) // blocks) // 16 * 16
            last = min(rows, -(-(high - offset) // blocks))
            last = -(-last // 16) * 16
            if last <= first:
                continue
            size = min(CHUNK, last - first)
            count = -(-(last - first) // size)
            base = offset + at

            @pl.loop(0, count)
            def _(i, first=first, last=last, size=size, blocks=blocks, base=base, left=left, right=right):
                row = pl.multiple_of(jnp.minimum(first + i * size, last - size), 16)
                lhs = left[pl.ds(row, size), :]

                @pl.loop(0, blocks // 2, unroll=3)
                def _(j):
                    rhs = right[:, pl.ds(pl.multiple_of(j * 256, 256), 256)]
                    product = jnp.dot(lhs, rhs, preferred_element_type=jnp.float32)
                    start = base + row * blocks + 2 * j
                    flat[pl.ds(start, size, stride=blocks), :] = product[:, :128]
                    flat[pl.ds(start + 1, size, stride=blocks), :] = product[:, 128:]

        row = 0
        for name in ORDER:
            start, count = VECTORS[name]
            lo, hi = max(start, low), min(start + count, high)
            if lo < hi:
                flat[lo + at:hi + at, :] = vec_ref[row + lo - start:row + hi - start, :]
            row += count
        end = 55374
        if high > end:
            flat[end + at:high + at, :] = jnp.zeros((high - end, 128), jnp.float32)

    for t in range(4):
        for c in range(2):
            pl.when((step == t) & (core == c))(lambda number=2 * t + c: eighth(number))

    @pl.loop(0, 16)
    def _(k):
        out_ref[0, k] = flat[pl.ds(MARGIN + 433 * k, 448), :].astype(jnp.bfloat16)


def weight_grads(core, vec, mine, theirs):
    whole = pl.BlockSpec(memory_space=pltpu.VMEM)
    pairs = [(r, 256) for r in (768, 768, 768, 3072)] + [(256, c) for c in (2304, 768, 3072)]
    return pl.pallas_call(
        weight_kernel,
        grid=(4,),
        out_shape=jax.ShapeDtypeStruct((4, 16, 448, 128), jnp.bfloat16),
        in_specs=[pl.BlockSpec(memory_space=pltpu.SMEM)] + [whole] * 15,
        out_specs=pl.BlockSpec((1, 16, 448, 128), lambda e: (e, 0, 0, 0)),
        scratch_shapes=[pltpu.VMEM((EIGHTH + 2 * MARGIN, 128), jnp.float32)] + [pltpu.VMEM(p, jnp.bfloat16) for p in pairs],
        compiler_params=pltpu.CompilerParams(vmem_limit_bytes=48 * 2**20),
    )(core, vec, *mine, *theirs)


def halves(size):
    half = size // 32 * 16
    return half, size - half


def pick(ref, axes, axis, index, start, size):
    idx = tuple(index if a == axis else slice(None) for a in axes)
    return ref.at[idx + (pl.ds(start, size), slice(None))]


def each(count, body):
    if count == 0:
        body(())
        return
    @pl.loop(0, 4 ** count)
    def _(n):
        body(tuple(lax.rem(lax.div(n, 4 ** (count - 1 - d)), 4) for d in range(count)))


def scatter_kernel(in_ref, out_ref, *scratch):
    send, recv = scratch[-2:]
    bufs = list(scratch[:-2])
    pos, core = place()
    greet(pos, core, sibling=False)
    take = iter(bufs)
    got = {}
    for part in range(3):
        for phase in range(3):
            got[part, phase] = [next(take) for _ in range(9 if phase < 2 else 8)]

    def push(part, phase, number, src, dst, axis, by):
        copy = pltpu.make_async_remote_copy(src, dst, send.at[part, phase, number], recv.at[part, phase, number],
                                            device_id=device(moved(pos, axis, by), core), device_id_type=MESH)
        copy.start()
        return copy

    def current(part, phase):
        start, size, order = PARTS[part]
        axes = [0, 1, 2]
        for a in order[::-1][:phase]:
            axes.remove(a)
        if phase == 0:
            return in_ref, axes, start
        return got[part, phase - 1][8], axes, 0

    copies = {}

    def begin(part, phase):
        ref, axes, base = current(part, phase)
        start, size, order = PARTS[part]
        axis = order[2 - phase]
        h0, h1 = halves(size)
        q = pos[axis]
        far, right, left = (lax.rem(q + k, 4) for k in (2, 1, 3))
        b = got[part, phase]
        copies[part, phase] = [
            push(part, phase, 0, pick(ref, axes, axis, far, base, h0), b[0], axis, 1),
            push(part, phase, 1, pick(ref, axes, axis, far, base + h0, h1), b[1], axis, 3),
            push(part, phase, 2, pick(ref, axes, axis, right, base + h0, h1), b[2], axis, 1),
            push(part, phase, 3, pick(ref, axes, axis, left, base, h0), b[3], axis, 3),
        ]

    def add(ref, axes, axis, index, base, size, others, put):
        rest = [a for a in axes if a != axis]

        def body(at):
            full = dict(zip(rest, at))
            idx = tuple(index if a == axis else full[a] for a in axes)
            total = ref[idx + (pl.ds(base, size), slice(None))].astype(jnp.float32)
            for other in others:
                total = total + other[at + (slice(None), slice(None))].astype(jnp.float32)
            put(at, total)

        each(len(rest), body)

    def middle(part, phase):
        ref, axes, base = current(part, phase)
        start, size, order = PARTS[part]
        axis = order[2 - phase]
        h0, h1 = halves(size)
        q = pos[axis]
        right, left = (lax.rem(q + k, 4) for k in (1, 3))
        b = got[part, phase]
        c = copies[part, phase]

        def to(ref):
            def put(at, total):
                ref[at + (slice(None), slice(None))] = total.astype(jnp.bfloat16)
            return put

        c[0].wait_recv()
        add(ref, axes, axis, right, base, h0, [b[0]], to(b[6]))
        c.append(push(part, phase, 4, b[6], b[4], axis, 1))
        c[1].wait_recv()
        add(ref, axes, axis, left, base + h0, h1, [b[1]], to(b[7]))
        c.append(push(part, phase, 5, b[7], b[5], axis, 3))

    def finish(part, phase):
        ref, axes, base = current(part, phase)
        start, size, order = PARTS[part]
        axis = order[2 - phase]
        h0, h1 = halves(size)
        q = pos[axis]
        b = got[part, phase]
        c = copies[part, phase]
        for copy in c[2:]:
            copy.wait_recv()
        for lo, n, others in ((0, h0, [b[3], b[4]]), (h0, h1, [b[2], b[5]])):
            def put(at, total, lo=lo, n=n):
                if phase == 2:
                    out_ref[start + lo:start + lo + n, :] = total
                else:
                    b[8][at + (pl.ds(lo, n), slice(None))] = total.astype(jnp.bfloat16)
            add(ref, axes, axis, q, base + lo, n, others, put)

    for phase in range(3):
        for part in range(3):
            if phase == 0:
                begin(part, 0)
        for part in range(3):
            middle(part, phase)
        for part in range(3):
            finish(part, phase)
            if phase < 2:
                begin(part, phase + 1)
    for c in copies.values():
        for copy in c:
            copy.wait_send()


def scatter(parts):
    scratch = []
    for part in range(3):
        _, size, _ = PARTS[part]
        h0, h1 = halves(size)
        for phase in range(3):
            lead = (4,) * (2 - phase)
            sizes = [h0, h1, h1, h0, h0, h1, h0, h1] + ([size] if phase < 2 else [])
            scratch += [pltpu.VMEM(lead + (n, 128), jnp.bfloat16) for n in sizes]
    scratch += [pltpu.SemaphoreType.DMA((3, 3, 6)), pltpu.SemaphoreType.DMA((3, 3, 6))]
    return pl.pallas_call(
        scatter_kernel,
        out_shape=jax.ShapeDtypeStruct((ROWS, 128), jnp.float32),
        in_specs=[pl.BlockSpec(memory_space=pltpu.VMEM)],
        out_specs=pl.BlockSpec(memory_space=pltpu.VMEM),
        scratch_shapes=scratch,
        compiler_params=pltpu.CompilerParams(collective_id=1, has_side_effects=True, vmem_limit_bytes=40 * 2**20),
    )(parts)


def twin(array):
    return lax.ppermute(array, "dp_1", [(0, 1), (1, 0)])


def body(tokens, params, out_grad):
    piece = tokens.shape[1]
    x, grad = tokens[0], out_grad[0]
    own = jnp.pad(params.reshape(433, 128), ((0, ROWS - 433), (0, 0)))
    gathered = gather(own).reshape(128, ROWS, 128)
    tables = rotary_tables(lax.axis_index(SEQ) * piece + jnp.arange(piece))
    w_qkv, w_out, blocks, h1t, h2, h2t, in_vec = first_part(gathered, x, grad, tables)
    back = exchange(heads(exchange(blocks, True)), False)
    mlp, dh2, act_t, dup, bias = second_part(gathered, h2, grad)
    layer_out, input_grad, att_t, dqkv, vec = third_part(
        back, x, grad, tables, w_qkv, w_out, mlp, dh2, bias, in_vec
    )
    vec = vec + twin(vec)
    core = lax.axis_index("dp_1").astype(jnp.int32).reshape(1)
    mine = (h1t, att_t, h2t, act_t, dqkv, grad, dup)
    halves_sum = weight_grads(core, vec, mine, tuple(twin(a) for a in mine))
    param_grad = scatter(halves_sum.reshape(4, 4, 4, ROWS, 128))[:433].reshape(-1)
    return layer_out[None], input_grad[None], param_grad


def solution(mesh):
    finer = Mesh(mesh.devices.reshape(4, 2, 4, 4), DP_SEQ)
    in_specs = (P(DP, SEQ, None), P(DP_SEQ), P(DP, SEQ, None))
    out_specs = (P(DP, SEQ, None), P(DP, SEQ, None), P(DP_SEQ))
    return jax.shard_map(body, mesh=finer, in_specs=in_specs, out_specs=out_specs, check_vma=False)
```

```python
import functools

import jax
import jax.numpy as jnp
from jax import lax
from jax.experimental import pallas as pl
from jax.experimental.pallas import tpu as pltpu
from jax.sharding import Mesh
from jax.sharding import PartitionSpec as P

DP_SEQ = ("dp_0", "dp_1", "seq_0", "seq_1")
SEQ = ("seq_0", "seq_1")
DP = ("dp_0", "dp_1")
VMEM_LIMIT = 60 * 2**20
MESH = pl.DeviceIdType.MESH
ROWS = 448
PARTS = ((0, 144, (0, 2, 1)), (144, 144, (2, 1, 0)), (288, 160, (1, 0, 2)))


def place():
    return [lax.axis_index("dp_0"), lax.axis_index("seq_0"), lax.axis_index("seq_1")], lax.axis_index("dp_1")


def device(pos, core):
    return (pos[0], core, pos[1], pos[2])


def moved(pos, axis, by):
    out = list(pos)
    out[axis] = lax.rem(pos[axis] + by, 4)
    return out


def greet(pos, core, sibling=True):
    barrier = pltpu.get_barrier_semaphore()
    others = [device(moved(pos, a, by), core) for a in range(3) for by in (1, 3)]
    if sibling:
        others.append(device(pos, 1 - core))
    for other in others:
        pl.semaphore_signal(barrier, inc=1, device_id=other, device_id_type=MESH)
    pl.semaphore_wait(barrier, len(others))


def gather_kernel(own_ref, out_ref, send, recv, sib_send, sib_recv, local):
    pos, core = place()
    greet(pos, core)

    def region(part, where, c, start, size):
        idx = [slice(None) if w is None else w for w in where]
        return out_ref.at[idx[0], c, idx[1], idx[2], pl.ds(start, size), :]

    own = pltpu.make_async_copy(own_ref, out_ref.at[pos[0], core, pos[1], pos[2]], local)
    own.start()
    own.wait()
    sibs = []

    def to_sibling(number, part, where):
        start, size, _ = PARTS[part]
        ref = region(part, where, core, start, size)
        copy = pltpu.make_async_remote_copy(ref, ref, sib_send.at[part, number], sib_recv.at[part, number],
                                            device_id=device(pos, 1 - core), device_id_type=MESH)
        copy.start()
        sibs.append(copy)

    def push(part, phase, number, where, start, size, axis, by):
        ref = region(part, where, core, start, size)
        copy = pltpu.make_async_remote_copy(ref, ref, send.at[part, phase, number], recv.at[part, phase, number],
                                            device_id=device(moved(pos, axis, by), core), device_id_type=MESH)
        copy.start()
        return copy

    def before(order, phase):
        where = [pos[0], pos[1], pos[2]]
        for a in order[:phase]:
            where[a] = None
        return where

    for part in range(3):
        to_sibling(0, part, before(PARTS[part][2], 0))
    for phase in range(3):
        firsts, seconds = [], []
        for part in range(3):
            start, size, order = PARTS[part]
            axis = order[phase]
            where = before(order, phase)
            firsts.append((push(part, phase, 0, where, start, size, axis, 1), push(part, phase, 1, where, start, size, axis, 3)))
        for part in range(3):
            start, size, order = PARTS[part]
            axis = order[phase]
            up, down = firsts[part]
            half = size // 32 * 16
            left = before(order, phase)
            left[axis] = lax.rem(pos[axis] + 3, 4)
            right = before(order, phase)
            right[axis] = lax.rem(pos[axis] + 1, 4)
            up.wait_recv()
            one = push(part, phase, 2, left, start, half, axis, 1)
            to_sibling(1 + 3 * phase, part, left)
            down.wait_recv()
            two = push(part, phase, 3, right, start + half, size - half, axis, 3)
            to_sibling(2 + 3 * phase, part, right)
            seconds.append((one, two))
        for part in range(3):
            start, size, order = PARTS[part]
            axis = order[phase]
            one, two = seconds[part]
            one.wait_recv()
            two.wait_recv()
            far = before(order, phase)
            far[axis] = lax.rem(pos[axis] + 2, 4)
            to_sibling(3 + 3 * phase, part, far)
        for copy in [c for pair in firsts + seconds for c in pair]:
            copy.wait_send()
    for copy in sibs:
        copy.wait_send()
        copy.wait_recv()


def gather(own):
    return pl.pallas_call(
        gather_kernel,
        out_shape=jax.ShapeDtypeStruct((4, 2, 4, 4, ROWS, 128), jnp.bfloat16),
        in_specs=[pl.BlockSpec(memory_space=pl.ANY)],
        out_specs=pl.BlockSpec(memory_space=pl.ANY),
        scratch_shapes=[pltpu.SemaphoreType.DMA((3, 3, 4)), pltpu.SemaphoreType.DMA((3, 3, 4)),
                        pltpu.SemaphoreType.DMA((3, 10)), pltpu.SemaphoreType.DMA((3, 10)), pltpu.SemaphoreType.DMA],
        compiler_params=pltpu.CompilerParams(collective_id=0, has_side_effects=True),
    )(own)


EIGHTH = 16 * 433
W_QKV = (24, 768, 18)
W_OUT = (13866, 768, 6)
W_UP = (18480, 768, 24)
W_DOWN = (36936, 3072, 6)
VECTORS = {"ln1_gain": (0, 6), "ln1_shift": (6, 6), "ln2_gain": (12, 6), "ln2_shift": (18, 6),
           "b_qkv": (13848, 18), "b_out": (18474, 6), "b_up": (36912, 24), "b_down": (55368, 6)}


HEADS = 12
TILE = 1024
KEYS = 1024


class Exchange:
    scratch = [pltpu.SemaphoreType.DMA((16,)), pltpu.SemaphoreType.DMA((16,)), pltpu.SemaphoreType.DMA]

    def __init__(self, to_heads, in_ref, out_ref, send, recv, local):
        self.to_heads, self.in_ref, self.out_ref = to_heads, in_ref, out_ref
        self.send, self.recv, self.local = send, recv, local
        self.x, self.core = lax.axis_index("dp_0"), lax.axis_index("dp_1")
        self.me = lax.axis_index("seq_0") * 4 + lax.axis_index("seq_1")
        self.others = [lax.rem(self.me + k, 16) for k in range(1, 16)]

    def where(self, t):
        return (self.x, self.core, lax.div(t, 4), lax.rem(t, 4))

    def copy(self, t):
        return pltpu.make_async_remote_copy(
            self.in_ref.at[t], self.out_ref.at[self.me], self.send.at[t], self.recv.at[self.me],
            device_id=self.where(t), device_id_type=MESH)

    def arrival(self, t):
        return pltpu.make_async_remote_copy(
            self.out_ref.at[t], self.out_ref.at[t], self.send.at[t], self.recv.at[t],
            device_id=self.where(t), device_id_type=MESH)

    def own(self):
        return pltpu.make_async_copy(self.in_ref.at[self.me], self.out_ref.at[self.me], self.local)

    def start(self):
        barrier = pltpu.get_barrier_semaphore()
        for t in self.others:
            pl.semaphore_signal(barrier, inc=1, device_id=self.where(t), device_id_type=MESH)
        pl.semaphore_wait(barrier, 15)
        if self.to_heads:
            for t in self.others:
                pl.when(t < HEADS)(lambda t=t: self.copy(t).start())
            pl.when(self.me < HEADS)(lambda: self.own().start())
        else:
            @pl.when(self.me < HEADS)
            def _():
                for t in self.others:
                    self.copy(t).start()
                self.own().start()

    def wait(self):
        if self.to_heads:
            @pl.when(self.me < HEADS)
            def _():
                for t in self.others:
                    self.arrival(t).wait_recv()
                self.own().wait()
            for t in self.others:
                pl.when(t < HEADS)(lambda t=t: self.copy(t).wait_send())
        else:
            for t in self.others:
                pl.when(t < HEADS)(lambda t=t: self.arrival(t).wait_recv())

            @pl.when(self.me < HEADS)
            def _():
                for t in self.others:
                    self.copy(t).wait_send()
                self.own().wait()


NT = (((1,), (1,)), ((), ()))


def product(a, b, dims=(((1,), (0,)), ((), ()))):
    return lax.dot_general(a, b, dims, preferred_element_type=jnp.float32)


def head_kernel(in_ref, out_ref, k, v, kt, vt, scores, dk, dv):
    blocks = 2048 // TILE
    per = TILE // 128

    def rows(which, i):
        return jnp.concatenate([in_ref[i * per + p, which] for p in range(per)], 0)

    @pl.loop(0, blocks)
    def _(i):
        at = pl.ds(pl.multiple_of(i * TILE, TILE), TILE)
        key = rows(0, i)[:, 64:]
        value = rows(1, i)[:, :64]
        k[at, :] = key
        v[at, :] = value
        kt[:, at] = key.T
        vt[:, at] = value.T
        dk[at, :] = jnp.zeros((TILE, 64), jnp.float32)
        dv[at, :] = jnp.zeros((TILE, 64), jnp.float32)

    @pl.loop(0, blocks)
    def _(i):
        query = rows(0, i)[:, :64] * jnp.bfloat16(0.125)
        grad = rows(1, i)[:, 64:]

        def tile(j):
            return pl.ds(pl.multiple_of(j * KEYS, KEYS), KEYS)

        last = lax.div(i * TILE, KEYS)

        def first(j, top):
            s = product(k[tile(j), :], query, NT)
            scores[tile(j), :] = s
            return jnp.maximum(top, jnp.max(s, 0, keepdims=True))

        top = lax.fori_loop(0, last, first, jnp.full((1, TILE), -1e30, jnp.float32))
        s = product(k[tile(last), :], query, NT)
        keep = lax.broadcasted_iota(jnp.int32, (KEYS, TILE), 0) - lax.broadcasted_iota(jnp.int32, (KEYS, TILE), 1) <= i * TILE - last * KEYS
        s = jnp.where(keep, s, -1e30)
        scores[tile(last), :] = s
        top = jnp.maximum(top, jnp.max(s, 0, keepdims=True))

        def second(j, carry):
            total, out = carry
            e = jnp.exp(scores[tile(j), :] - top)
            scores[tile(j), :] = e
            return total + jnp.sum(e, 0, keepdims=True), out + product(vt[:, tile(j)], e.astype(jnp.bfloat16))

        total, out = lax.fori_loop(0, last + 1, second, (jnp.zeros((1, TILE), jnp.float32), jnp.zeros((64, TILE), jnp.float32)))
        scale = 1.0 / total
        out = out * scale
        inner = jnp.sum(out * grad.astype(jnp.float32).T, 0, keepdims=True)

        def third(j, dq):
            p = scores[tile(j), :] * scale
            dp = product(v[tile(j), :], grad, NT)
            ds = (p * (dp - inner)).astype(jnp.bfloat16)
            dv[tile(j), :] += product(p.astype(jnp.bfloat16), grad)
            dk[tile(j), :] += product(ds, query)
            return dq + product(kt[:, tile(j)], ds)

        dq = lax.fori_loop(0, last + 1, third, jnp.zeros((64, TILE), jnp.float32)) * 0.125
        both = jnp.concatenate([out, dq], 0).T.astype(jnp.bfloat16)
        for p in range(per):
            out_ref[i * per + p, 0] = both[128 * p:128 * (p + 1)]

    @pl.loop(0, blocks)
    def _(i):
        at = pl.ds(pl.multiple_of(i * TILE, TILE), TILE)
        both = jnp.concatenate([dk[at, :], dv[at, :]], 1).astype(jnp.bfloat16)
        for p in range(per):
            out_ref[i * per + p, 1] = both[128 * p:128 * (p + 1)]


def heads(blocks):
    return pl.pallas_call(
        head_kernel,
        out_shape=jax.ShapeDtypeStruct((16, 2, 128, 128), jnp.bfloat16),
        grid=(1,),
        in_specs=[pl.BlockSpec((16, 2, 128, 128), lambda e: (0, 0, 0, 0))],
        out_specs=pl.BlockSpec((16, 2, 128, 128), lambda e: (0, 0, 0, 0)),
        scratch_shapes=[pltpu.VMEM((2048, 64), jnp.bfloat16), pltpu.VMEM((2048, 64), jnp.bfloat16),
                        pltpu.VMEM((64, 2048), jnp.bfloat16), pltpu.VMEM((64, 2048), jnp.bfloat16),
                        pltpu.VMEM((2048, TILE), jnp.float32),
                        pltpu.VMEM((2048, 64), jnp.float32), pltpu.VMEM((2048, 64), jnp.float32)],
        compiler_params=pltpu.CompilerParams(vmem_limit_bytes=VMEM_LIMIT),
    )(blocks)


EPS = 1e-05
ORDER = ("ln1_gain", "ln1_shift", "ln2_gain", "ln2_shift", "b_qkv", "b_out", "b_up", "b_down")


def widen(g_ref, flat, step):
    @pl.loop(0, 16)
    def _(k):
        base = (step * 16 + k) * 433
        flat[pl.ds(base, 440), :] = g_ref[k, 0:440, :].astype(jnp.float32)


def unpack_matrix(flat, first, where, out, size=64):
    offset, rows, blocks = where
    start = offset - first * EIGHTH

    @pl.loop(0, rows // size)
    def _(i):
        for j in range(blocks):
            piece = flat[pl.ds(start + j + i * (size * blocks), size, stride=blocks), :]
            out[pl.ds(pl.multiple_of(i * size, size), size), 128 * j:128 * (j + 1)] = piece.astype(jnp.bfloat16)


def as_row(ref, start, count):
    return jnp.concatenate([ref[start + n:start + n + 1, :] for n in range(count)], 1)


def to_rows(ref, start, row):
    for n in range(row.shape[1] // 128):
        ref[start + n:start + n + 1, :] = row[:, 128 * n:128 * (n + 1)]


def normalized(values):
    center = jnp.mean(values, -1, keepdims=True)
    centered = values - center
    factor = lax.rsqrt(jnp.mean(centered * centered, -1, keepdims=True) + EPS)
    return centered * factor, factor


def turn(x, tables, sign):
    return x * tables[0] + (pltpu.roll(x, 120, 1) * tables[1] + pltpu.roll(x, 8, 1) * tables[2]) * sign


def first_kernel(g_ref, tokens_ref, grad_ref, tables_ref, w_qkv, w_out, blocks_ref, h1t_ref, h2_ref, h2t_ref, vec_ref, flat, wide):
    step = pl.program_id(0)
    widen(g_ref, flat, step)

    @pl.when(step == 1)
    def _():
        unpack_matrix(flat, 0, W_QKV, w_qkv)

    @pl.when(step == 2)
    def _():
        unpack_matrix(flat, 0, W_OUT, w_out)
        vec_ref[0:24, :] = flat[0:24, :]
        start = VECTORS["b_out"][0]
        vec_ref[24:30, :] = flat[start:start + 6, :]
        normal, _ = normalized(tokens_ref[...].astype(jnp.float32))
        h1 = (normal * as_row(flat, 0, 6) + as_row(flat, 6, 6)).astype(jnp.bfloat16)
        h2 = (normal * as_row(flat, 12, 6) + as_row(flat, 18, 6)).astype(jnp.bfloat16)
        h1t_ref[...] = h1.T
        h2_ref[...] = h2
        h2t_ref[...] = h2.T
        for n in range(9):
            start = VECTORS["b_qkv"][0] + 2 * n
            wide[:, 256 * n:256 * (n + 1)] = product(h1, w_qkv[:, 256 * n:256 * (n + 1)]) + as_row(flat, start, 2)
        low = lax.broadcasted_iota(jnp.int32, (128, 128), 1) < 64
        for m in range(6):
            q, k, v = (wide[:, 768 * p + 128 * m:768 * p + 128 * (m + 1)] for p in range(3))
            q = turn(q, tables_ref, 1.0)
            k = turn(k, tables_ref, 1.0)
            a = product(grad_ref[...], w_out[128 * m:128 * (m + 1), :], NT)
            swap = lambda t: pltpu.roll(t, 64, 1)
            blocks_ref[2 * m, 0] = jnp.where(low, q, swap(k)).astype(jnp.bfloat16)
            blocks_ref[2 * m + 1, 0] = jnp.where(low, swap(q), k).astype(jnp.bfloat16)
            blocks_ref[2 * m, 1] = jnp.where(low, v, swap(a)).astype(jnp.bfloat16)
            blocks_ref[2 * m + 1, 1] = jnp.where(low, swap(v), a).astype(jnp.bfloat16)


def const(*shape):
    return pl.BlockSpec(shape, lambda e: (0,) * len(shape))


def first_part(gathered, tokens, grad, tables):
    bf = lambda *s: jax.ShapeDtypeStruct(s, jnp.bfloat16)
    outs = [bf(768, 2304), bf(768, 768), bf(HEADS, 2, 128, 128), bf(768, 128), bf(128, 768), bf(768, 128),
            jax.ShapeDtypeStruct((32, 128), jnp.float32)]
    return pl.pallas_call(
        first_kernel,
        grid=(3,),
        out_shape=outs,
        in_specs=[pl.BlockSpec((16, 448, 128), lambda e: (e, 0, 0)), const(128, 768), const(128, 768), const(3, 128, 128)],
        out_specs=[const(*o.shape) for o in outs],
        scratch_shapes=[pltpu.VMEM((3 * EIGHTH + 16, 128), jnp.float32), pltpu.VMEM((128, 2304), jnp.float32)],
        compiler_params=pltpu.CompilerParams(vmem_limit_bytes=VMEM_LIMIT),
    )(gathered, tokens, grad, tables)


def gelu_pair(u):
    inside = 0.5 * (1.0 + lax.erf(u * 0.7071067811865476))
    return u * inside, inside + u * jnp.exp(-0.5 * u * u) * 0.3989422804014327


def second_kernel(g_ref, h2_ref, grad_ref, blocks_ref, mlp_ref, dh2_ref, act_t_ref, dup_ref, bias_ref, heads_ref,
                  flat, w_up, w_down, act, slope, *sems):
    step = pl.program_id(0)
    swap = Exchange(True, blocks_ref, heads_ref, *sems)
    pl.when(step == 0)(swap.start)
    widen(g_ref, flat, step)

    @pl.when(step == 3)
    def _():
        unpack_matrix(flat, 2, W_UP, w_up)
        start = VECTORS["b_up"][0] - 2 * EIGHTH
        for n in range(12):
            at = slice(256 * n, 256 * (n + 1))
            up = product(h2_ref[...], w_up[:, at]) + as_row(flat, start + 2 * n, 2)
            value, slope[:, at] = gelu_pair(up)
            value = value.astype(jnp.bfloat16)
            act[:, at] = value
            act_t_ref[at, :] = value.T

    @pl.when(step == 5)
    def _():
        unpack_matrix(flat, 2, W_DOWN, w_down, 128)
        start = VECTORS["b_down"][0] - 2 * EIGHTH
        for n in range(3):
            at = slice(256 * n, 256 * (n + 1))
            mlp_ref[:, at] = product(act[...], w_down[:, at]) + as_row(flat, start + 2 * n, 2)
        for n in range(12):
            at = slice(256 * n, 256 * (n + 1))
            dup = (product(grad_ref[...], w_down[at, :], NT) * slope[:, at]).astype(jnp.bfloat16)
            dup_ref[:, at] = dup
            to_rows(bias_ref, 2 * n, jnp.sum(dup.astype(jnp.float32), 0, keepdims=True))
        for n in range(3):
            at = slice(256 * n, 256 * (n + 1))
            dh2_ref[:, at] = product(dup_ref[...], w_up[at, :], NT)
        swap.wait()


def second_part(gathered, h2, grad, blocks):
    bf = lambda *s: jax.ShapeDtypeStruct(s, jnp.bfloat16)
    f32 = lambda *s: jax.ShapeDtypeStruct(s, jnp.float32)
    outs = [f32(128, 768), f32(128, 768), bf(3072, 128), bf(128, 3072), f32(24, 128)]
    anywhere = pl.BlockSpec(memory_space=pl.ANY)
    return pl.pallas_call(
        second_kernel,
        grid=(6,),
        out_shape=outs + [bf(16, 2, 128, 128)],
        in_specs=[pl.BlockSpec((16, 448, 128), lambda e: (e + 2, 0, 0)), const(128, 768), const(128, 768), anywhere],
        out_specs=[const(*o.shape) for o in outs] + [anywhere],
        scratch_shapes=[pltpu.VMEM((6 * EIGHTH + 16, 128), jnp.float32), pltpu.VMEM((768, 3072), jnp.bfloat16),
                        pltpu.VMEM((3072, 768), jnp.bfloat16), pltpu.VMEM((128, 3072), jnp.bfloat16),
                        pltpu.VMEM((128, 3072), jnp.float32)] + Exchange.scratch,
        compiler_params=pltpu.CompilerParams(collective_id=2, has_side_effects=True, vmem_limit_bytes=VMEM_LIMIT),
    )(gathered, h2, grad, blocks)


def third_kernel(back_ref, tokens_ref, grad_ref, tables_ref, w_qkv, w_out, mlp_ref, dh2_ref, bias_ref, in_vec,
                 layer_ref, input_ref, att_t_ref, dqkv_ref, vec_ref):
    low = lax.broadcasted_iota(jnp.int32, (128, 128), 1) < 64
    swap = lambda t: pltpu.roll(t, 64, 1)
    f32 = lambda t: t.astype(jnp.float32)
    attended = []
    for m in range(6):
        a, b = f32(back_ref[2 * m, 0]), f32(back_ref[2 * m + 1, 0])
        c, d = f32(back_ref[2 * m, 1]), f32(back_ref[2 * m + 1, 1])
        attended.append(jnp.where(low, a, swap(b)).astype(jnp.bfloat16))
        dq = turn(jnp.where(low, swap(a), b), tables_ref, -1.0)
        dk = turn(jnp.where(low, c, swap(d)), tables_ref, -1.0)
        dv = jnp.where(low, swap(c), d)
        for p, part in enumerate((dq, dk, dv)):
            dqkv_ref[:, 768 * p + 128 * m:768 * p + 128 * (m + 1)] = part.astype(jnp.bfloat16)
    attended = jnp.concatenate(attended, 1)
    att_t_ref[...] = attended.T
    tokens = f32(tokens_ref[...])
    grad = f32(grad_ref[...])
    layer_ref[...] = (tokens + (product(attended, w_out[...]) + as_row(in_vec, 24, 6)) + mlp_ref[...]).astype(jnp.bfloat16)
    normal, factor = normalized(tokens)
    total = grad
    row = 0
    for gain_at, dh in ((0, product(dqkv_ref[...], w_qkv[...], NT)), (12, dh2_ref[...])):
        to_rows(vec_ref, row, jnp.sum(dh * normal, 0, keepdims=True))
        to_rows(vec_ref, row + 6, jnp.sum(dh, 0, keepdims=True))
        row += 12
        scaled = dh * as_row(in_vec, gain_at, 6)
        inner = scaled - jnp.mean(scaled, -1, keepdims=True) - normal * jnp.mean(scaled * normal, -1, keepdims=True)
        total = total + factor * inner
    input_ref[...] = total
    to_rows(vec_ref, 24, jnp.sum(f32(dqkv_ref[...]), 0, keepdims=True))
    shift = jnp.sum(grad, 0, keepdims=True)
    to_rows(vec_ref, 42, shift)
    vec_ref[48:72, :] = bias_ref[...]
    to_rows(vec_ref, 72, shift)
    vec_ref[78:80, :] = jnp.zeros((2, 128), jnp.float32)


def third_part(*args):
    bf = lambda *s: jax.ShapeDtypeStruct(s, jnp.bfloat16)
    f32 = lambda *s: jax.ShapeDtypeStruct(s, jnp.float32)
    outs = [bf(128, 768), f32(128, 768), bf(768, 128), bf(128, 2304), f32(80, 128)]
    return pl.pallas_call(
        third_kernel,
        grid=(1,),
        out_shape=outs,
        in_specs=[const(*a.shape) for a in args],
        out_specs=[const(*o.shape) for o in outs],
        compiler_params=pltpu.CompilerParams(vmem_limit_bytes=VMEM_LIMIT),
    )(*args)


def rotary_tables(positions):
    lane = jnp.arange(128) % 64
    freq = jnp.tile(10000.0 ** (-jnp.arange(8).astype(jnp.float32) * 2.0 / 16), 16)
    angles = positions.astype(jnp.float32)[:, None] * freq[None, :]
    cosine, sine = jnp.cos(angles), jnp.sin(angles)
    return jnp.stack([jnp.where(lane < 16, cosine, 1.0), jnp.where(lane < 8, -sine, 0.0),
                      jnp.where((lane >= 8) & (lane < 16), sine, 0.0)])


MARGIN = 384
CHUNK = 128


def weight_eighth(number, pairs, vec_ref, flat):
    low, high = number * EIGHTH, (number + 1) * EIGHTH
    at = MARGIN - low
    for (offset, rows, blocks), left, right in pairs:
        first = max(0, (low - offset) // blocks) // 16 * 16
        last = min(rows, -(-(high - offset) // blocks))
        last = -(-last // 16) * 16
        if last <= first:
            continue
        size = min(CHUNK, last - first)
        count = -(-(last - first) // size)
        base = offset + at

        @pl.loop(0, count)
        def _(i, first=first, last=last, size=size, blocks=blocks, base=base, left=left, right=right):
            row = pl.multiple_of(jnp.minimum(first + i * size, last - size), 16)
            lhs = left[pl.ds(row, size), :]

            @pl.loop(0, blocks // 2, unroll=3)
            def _(j):
                rhs = right[:, pl.ds(pl.multiple_of(j * 256, 256), 256)]
                result = product(lhs, rhs)
                start = base + row * blocks + 2 * j
                flat[pl.ds(start, size, stride=blocks), :] = result[:, :128]
                flat[pl.ds(start + 1, size, stride=blocks), :] = result[:, 128:]

    row = 0
    for name in ORDER:
        start, count = VECTORS[name]
        lo, hi = max(start, low), min(start + count, high)
        if lo < hi:
            flat[lo + at:hi + at, :] = vec_ref[row + lo - start:row + hi - start, :]
        row += count
    end = 55374
    if high > end:
        flat[end + at:high + at, :] = jnp.zeros((high - end, 128), jnp.float32)


def join(pair, mine, theirs, lanes):
    if lanes:
        pair[:, :128] = mine[...]
        pair[:, 128:] = theirs[...]
    else:
        pair[:128, :] = mine[...]
        pair[128:, :] = theirs[...]


def pack(flat, out_ref):
    @pl.loop(0, 16)
    def _(k):
        out_ref[0, k] = flat[pl.ds(MARGIN + 433 * k, 448), :].astype(jnp.bfloat16)


def eighths(steps, step, core, pairs, vec_ref, flat):
    for n, t in enumerate(steps):
        for c in range(2):
            pl.when((step == n) & (core == c))(lambda number=2 * t + c: weight_eighth(number, pairs, vec_ref, flat))


HALVES = jax.ShapeDtypeStruct((4, 16, 448, 128), jnp.bfloat16)


def late_kernel(vec_ref, act_ref, act2_ref, g_ref, g2_ref, dup_ref, dup2_ref, h2_ref, h22_ref, heads_ref,
                out_ref, back_ref, flat, act, g, dup, h2, *sems):
    step = pl.program_id(0)
    swap = Exchange(False, heads_ref, back_ref, *sems)

    @pl.when(step == 0)
    def _():
        swap.start()
        join(act, act_ref, act2_ref, True)
        join(h2, h2_ref, h22_ref, True)
        join(g, g_ref, g2_ref, False)
        join(dup, dup_ref, dup2_ref, False)

    eighths((2, 3), step, lax.axis_index("dp_1"), ((W_UP, h2, dup), (W_DOWN, act, g)), vec_ref, flat)
    pack(flat, out_ref)
    pl.when(step == 1)(swap.wait)


def late_grads(vec, act, act2, g, g2, dup, dup2, h2, h22, heads_out):
    args = (vec, act, act2, g, g2, dup, dup2, h2, h22)
    anywhere = pl.BlockSpec(memory_space=pl.ANY)
    pairs = [(3072, 256), (256, 768), (256, 3072), (768, 256)]
    return pl.pallas_call(
        late_kernel,
        grid=(2,),
        out_shape=[HALVES, jax.ShapeDtypeStruct((HEADS, 2, 128, 128), jnp.bfloat16)],
        in_specs=[const(*a.shape) for a in args] + [anywhere],
        out_specs=[pl.BlockSpec((1, 16, 448, 128), lambda e: (e + 2, 0, 0, 0)), anywhere],
        scratch_shapes=[pltpu.VMEM((EIGHTH + 2 * MARGIN, 128), jnp.float32)]
        + [pltpu.VMEM(p, jnp.bfloat16) for p in pairs] + Exchange.scratch,
        compiler_params=pltpu.CompilerParams(collective_id=3, has_side_effects=True, vmem_limit_bytes=VMEM_LIMIT),
    )(*args, heads_out)


def early_kernel(core_ref, vec_ref, h1_ref, h12_ref, att_ref, att2_ref, h2_ref, h22_ref, dqkv_ref, dqkv2_ref,
                 g_ref, g2_ref, dup_ref, dup2_ref, halves_ref, out_ref, flat, h1, att, h2, dqkv, g, dup):
    step = pl.program_id(0)

    @pl.when(step == 0)
    def _():
        join(h1, h1_ref, h12_ref, True)
        join(att, att_ref, att2_ref, True)
        join(h2, h2_ref, h22_ref, True)
        join(dqkv, dqkv_ref, dqkv2_ref, False)
        join(g, g_ref, g2_ref, False)
        join(dup, dup_ref, dup2_ref, False)

    eighths((0, 1), step, core_ref[0], ((W_QKV, h1, dqkv), (W_OUT, att, g), (W_UP, h2, dup)), vec_ref, flat)
    pack(flat, out_ref)


def early_grads(core, vec, h1, h12, att, att2, h2, h22, dqkv, dqkv2, g, g2, dup, dup2, halves):
    args = (vec, h1, h12, att, att2, h2, h22, dqkv, dqkv2, g, g2, dup, dup2)
    pairs = [(768, 256)] * 3 + [(256, 2304), (256, 768), (256, 3072)]
    return pl.pallas_call(
        early_kernel,
        grid=(2,),
        out_shape=HALVES,
        in_specs=[pl.BlockSpec(memory_space=pltpu.SMEM)] + [const(*a.shape) for a in args] + [pl.BlockSpec(memory_space=pl.ANY)],
        out_specs=pl.BlockSpec((1, 16, 448, 128), lambda e: (e, 0, 0, 0)),
        scratch_shapes=[pltpu.VMEM((EIGHTH + 2 * MARGIN, 128), jnp.float32)] + [pltpu.VMEM(p, jnp.bfloat16) for p in pairs],
        input_output_aliases={14: 0},
        compiler_params=pltpu.CompilerParams(vmem_limit_bytes=VMEM_LIMIT),
    )(core, *args, halves)


def halves(size):
    half = size // 32 * 16
    return half, size - half


def pick(ref, axes, axis, index, start, size):
    idx = tuple(index if a == axis else slice(None) for a in axes)
    return ref.at[idx + (pl.ds(start, size), slice(None))]


def each(count, body):
    if count == 0:
        body(())
        return
    @pl.loop(0, 4 ** count)
    def _(n):
        body(tuple(lax.rem(lax.div(n, 4 ** (count - 1 - d)), 4) for d in range(count)))


def scatter_kernel(in_ref, out_ref, *scratch):
    send, recv = scratch[-2:]
    bufs = list(scratch[:-2])
    pos, core = place()
    greet(pos, core, sibling=False)
    take = iter(bufs)
    got = {}
    for part in range(3):
        for phase in range(3):
            got[part, phase] = [next(take) for _ in range(9 if phase < 2 else 8)]

    def push(part, phase, number, src, dst, axis, by):
        copy = pltpu.make_async_remote_copy(src, dst, send.at[part, phase, number], recv.at[part, phase, number],
                                            device_id=device(moved(pos, axis, by), core), device_id_type=MESH)
        copy.start()
        return copy

    def current(part, phase):
        start, size, order = PARTS[part]
        axes = [0, 1, 2]
        for a in order[::-1][:phase]:
            axes.remove(a)
        if phase == 0:
            return in_ref, axes, start
        return got[part, phase - 1][8], axes, 0

    copies = {}

    def begin(part, phase):
        ref, axes, base = current(part, phase)
        start, size, order = PARTS[part]
        axis = order[2 - phase]
        h0, h1 = halves(size)
        q = pos[axis]
        far, right, left = (lax.rem(q + k, 4) for k in (2, 1, 3))
        b = got[part, phase]
        copies[part, phase] = [
            push(part, phase, 0, pick(ref, axes, axis, far, base, h0), b[0], axis, 1),
            push(part, phase, 1, pick(ref, axes, axis, far, base + h0, h1), b[1], axis, 3),
            push(part, phase, 2, pick(ref, axes, axis, right, base + h0, h1), b[2], axis, 1),
            push(part, phase, 3, pick(ref, axes, axis, left, base, h0), b[3], axis, 3),
        ]

    def add(ref, axes, axis, index, base, size, others, put):
        rest = [a for a in axes if a != axis]

        def body(at):
            full = dict(zip(rest, at))
            idx = tuple(index if a == axis else full[a] for a in axes)
            total = ref[idx + (pl.ds(base, size), slice(None))].astype(jnp.float32)
            for other in others:
                total = total + other[at + (slice(None), slice(None))].astype(jnp.float32)
            put(at, total)

        each(len(rest), body)

    def middle(part, phase):
        ref, axes, base = current(part, phase)
        start, size, order = PARTS[part]
        axis = order[2 - phase]
        h0, h1 = halves(size)
        q = pos[axis]
        right, left = (lax.rem(q + k, 4) for k in (1, 3))
        b = got[part, phase]
        c = copies[part, phase]

        def to(ref):
            def put(at, total):
                ref[at + (slice(None), slice(None))] = total.astype(jnp.bfloat16)
            return put

        c[0].wait_recv()
        add(ref, axes, axis, right, base, h0, [b[0]], to(b[6]))
        c.append(push(part, phase, 4, b[6], b[4], axis, 1))
        c[1].wait_recv()
        add(ref, axes, axis, left, base + h0, h1, [b[1]], to(b[7]))
        c.append(push(part, phase, 5, b[7], b[5], axis, 3))

    def finish(part, phase):
        ref, axes, base = current(part, phase)
        start, size, order = PARTS[part]
        axis = order[2 - phase]
        h0, h1 = halves(size)
        q = pos[axis]
        b = got[part, phase]
        c = copies[part, phase]
        for copy in c[2:]:
            copy.wait_recv()
        for lo, n, others in ((0, h0, [b[3], b[4]]), (h0, h1, [b[2], b[5]])):
            def put(at, total, lo=lo, n=n):
                if phase == 2:
                    out_ref[start + lo:start + lo + n, :] = total
                else:
                    b[8][at + (pl.ds(lo, n), slice(None))] = total.astype(jnp.bfloat16)
            add(ref, axes, axis, q, base + lo, n, others, put)

    for phase in range(3):
        for part in range(3):
            if phase == 0:
                begin(part, 0)
        for part in range(3):
            middle(part, phase)
        for part in range(3):
            finish(part, phase)
            if phase < 2:
                begin(part, phase + 1)
    for c in copies.values():
        for copy in c:
            copy.wait_send()


def scatter(parts):
    scratch = []
    for part in range(3):
        _, size, _ = PARTS[part]
        h0, h1 = halves(size)
        for phase in range(3):
            lead = (4,) * (2 - phase)
            sizes = [h0, h1, h1, h0, h0, h1, h0, h1] + ([size] if phase < 2 else [])
            scratch += [pltpu.VMEM(lead + (n, 128), jnp.bfloat16) for n in sizes]
    scratch += [pltpu.SemaphoreType.DMA((3, 3, 6)), pltpu.SemaphoreType.DMA((3, 3, 6))]
    return pl.pallas_call(
        scatter_kernel,
        out_shape=jax.ShapeDtypeStruct((ROWS, 128), jnp.float32),
        grid=(1,),
        in_specs=[pl.BlockSpec((4, 4, 4, ROWS, 128), lambda e: (0, 0, 0, 0, 0))],
        out_specs=pl.BlockSpec((ROWS, 128), lambda e: (0, 0)),
        scratch_shapes=scratch,
        compiler_params=pltpu.CompilerParams(collective_id=1, has_side_effects=True, vmem_limit_bytes=VMEM_LIMIT),
    )(parts)


def twin(array):
    return lax.ppermute(array, "dp_1", [(0, 1), (1, 0)])


def body(tokens, params, out_grad):
    piece = tokens.shape[1]
    x, grad = tokens[0], out_grad[0]
    own = jnp.pad(params.reshape(433, 128), ((0, ROWS - 433), (0, 0)))
    gathered = gather(own).reshape(128, ROWS, 128)
    tables = rotary_tables(lax.axis_index(SEQ) * piece + jnp.arange(piece))
    w_qkv, w_out, blocks, h1t, h2, h2t, in_vec = first_part(gathered, x, grad, tables)
    mlp, dh2, act_t, dup, bias, at_heads = second_part(gathered, h2, grad, blocks)
    shift = jnp.sum(grad.astype(jnp.float32), 0).reshape(6, 128)
    late_vec = jnp.concatenate([jnp.zeros((48, 128), jnp.float32), bias, shift, jnp.zeros((2, 128), jnp.float32)])
    late_vec = late_vec + twin(late_vec)
    act2, g2, dup2, h22, h12 = (twin(a) for a in (act_t, grad, dup, h2t, h1t))
    halves_sum, back = late_grads(late_vec, act_t, act2, grad, g2, dup, dup2, h2t, h22, heads(at_heads))
    layer_out, input_grad, att_t, dqkv, vec = third_part(
        back, x, grad, tables, w_qkv, w_out, mlp, dh2, bias, in_vec
    )
    vec = vec + twin(vec)
    core = lax.axis_index("dp_1").astype(jnp.int32).reshape(1)
    halves_sum = early_grads(
        core, vec, h1t, h12, att_t, twin(att_t), h2t, h22, dqkv, twin(dqkv), grad, g2, dup, dup2, halves_sum
    )
    param_grad = scatter(halves_sum.reshape(4, 4, 4, ROWS, 128))[:433].reshape(-1)
    return layer_out[None], input_grad[None], param_grad


def solution(mesh):
    finer = Mesh(mesh.devices.reshape(4, 2, 4, 4), DP_SEQ)
    in_specs = (P(DP, SEQ, None), P(DP_SEQ), P(DP, SEQ, None))
    out_specs = (P(DP, SEQ, None), P(DP, SEQ, None), P(DP_SEQ))
    return jax.shard_map(body, mesh=finer, in_specs=in_specs, out_specs=out_specs, check_vma=False)
```

```python
import functools

import jax
import jax.numpy as jnp
from jax import lax
from jax.experimental import pallas as pl
from jax.experimental.pallas import tpu as pltpu
from jax.sharding import Mesh
from jax.sharding import PartitionSpec as P

DP_SEQ = ("dp_0", "dp_1", "seq_0", "seq_1")
SEQ = ("seq_0", "seq_1")
DP = ("dp_0", "dp_1")
VMEM_LIMIT = 60 * 2**20
MESH = pl.DeviceIdType.MESH
ROWS = 448
PARTS = ((0, 144, (0, 2, 1)), (144, 144, (2, 1, 0)), (288, 160, (1, 0, 2)))


def place():
    return [lax.axis_index("dp_0"), lax.axis_index("seq_0"), lax.axis_index("seq_1")], lax.axis_index("dp_1")


def device(pos, core):
    return (pos[0], core, pos[1], pos[2])


def moved(pos, axis, by):
    out = list(pos)
    out[axis] = lax.rem(pos[axis] + by, 4)
    return out


def greet(pos, core, sibling=True):
    barrier = pltpu.get_barrier_semaphore()
    others = [device(moved(pos, a, by), core) for a in range(3) for by in (1, 3)]
    if sibling:
        others.append(device(pos, 1 - core))
    for other in others:
        pl.semaphore_signal(barrier, inc=1, device_id=other, device_id_type=MESH)
    pl.semaphore_wait(barrier, len(others))


class Gather:
    scratch = [pltpu.SemaphoreType.DMA((3, 9, 4)), pltpu.SemaphoreType.DMA((3, 9, 4)),
               pltpu.SemaphoreType.DMA((3, 19)), pltpu.SemaphoreType.DMA((3, 19)), pltpu.SemaphoreType.DMA]
    rings = ("a", "b0", "b1", "b2", "b3", "c0", "c1", "c2", "c3")

    def __init__(self, own_ref, out_ref, send, recv, sib_send, sib_recv, local):
        self.own_ref, self.out_ref, self.local = own_ref, out_ref, local
        self.send_sem, self.recv_sem, self.sib_send, self.sib_recv = send, recv, sib_send, sib_recv
        self.pos, self.core = place()
        self.copies, self.sibs = {}, [[], [], []]

    def near(self, axis):
        q = self.pos[axis]
        return [q] + [lax.rem(q + k, 4) for k in (3, 1, 2)]

    def region(self, where, start, size):
        return self.out_ref.at[where[0], self.core, where[1], where[2], pl.ds(start, size), :]

    def base(self, part, ring):
        a, b, c = PARTS[part][2]
        where = list(self.pos)
        if ring == "a":
            return a, where
        number = int(ring[1])
        if ring[0] == "b":
            where[a] = self.near(a)[number]
            return b, where
        where[a] = slice(None)
        where[b] = self.near(b)[number]
        return c, where

    def at(self, part, ring, which):
        axis, where = self.base(part, ring)
        where[axis] = self.near(axis)[which]
        return where

    def push(self, part, ring, number, which, by, start, size, src=None):
        axis, _ = self.base(part, ring)
        n = self.rings.index(ring)
        ref = self.region(self.at(part, ring, which), start, size)
        copy = pltpu.make_async_remote_copy(
            ref if src is None else src, ref, self.send_sem.at[part, n, number], self.recv_sem.at[part, n, number],
            device_id=device(moved(self.pos, axis, by), self.core), device_id_type=MESH)
        copy.start()
        self.copies[part, ring, number] = copy

    def begin(self, part, ring):
        start, size, _ = PARTS[part]
        src = self.own_ref.at[pl.ds(start, size), :] if ring in ("a", "b0") else None
        self.push(part, ring, 0, 0, 1, start, size, src)
        self.push(part, ring, 1, 0, 3, start, size, src)

    def onward(self, part, ring, left=None, right=None):
        start, size, _ = PARTS[part]
        half = size // 32 * 16
        self.copies[part, ring, 0].wait_recv()
        self.push(part, ring, 2, 1, 1, start, half)
        if left:
            left()
        self.copies[part, ring, 1].wait_recv()
        self.push(part, ring, 3, 2, 3, start + half, size - half)
        if right:
            right()

    def end(self, part, ring):
        self.copies[part, ring, 2].wait_recv()
        self.copies[part, ring, 3].wait_recv()

    def sibling(self, part, where, src=None):
        start, size, _ = PARTS[part]
        number = len(self.sibs[part])
        ref = self.region(where, start, size)
        copy = pltpu.make_async_remote_copy(
            ref if src is None else src, ref, self.sib_send.at[part, number], self.sib_recv.at[part, number],
            device_id=device(self.pos, 1 - self.core), device_id_type=MESH)
        copy.start()
        self.sibs[part].append(copy)

    def share(self, part, ring, which):
        return lambda: self.sibling(part, self.at(part, ring, which))

    def row(self, part, number):
        a, b, _ = PARTS[part][2]
        where = list(self.pos)
        where[a] = slice(None)
        where[b] = self.near(b)[number]
        return where

    def run(self):
        parts = range(3)
        own = pltpu.make_async_copy(self.own_ref, self.out_ref.at[self.pos[0], self.core, self.pos[1], self.pos[2]], self.local)
        own.start()
        greet(self.pos, self.core)
        for p in parts:
            self.begin(p, "a")
        for p in parts:
            self.begin(p, "b0")
        for p in parts:
            start, size, _ = PARTS[p]
            self.sibling(p, self.pos, self.own_ref.at[pl.ds(start, size), :])
        own.wait()
        for p in parts:
            def arrived(which, p=p):
                self.begin(p, "b" + str(which))
                self.sibling(p, self.at(p, "a", which))
            self.onward(p, "a", lambda: arrived(1), lambda: arrived(2))
        for p in parts:
            self.onward(p, "b0")
        for p in parts:
            self.end(p, "a")
            self.begin(p, "b3")
            self.begin(p, "c0")
            self.sibling(p, self.at(p, "a", 3))
        for p in parts:
            self.onward(p, "b1")
            self.onward(p, "b2")
        for p in parts:
            self.end(p, "b0")
            self.onward(p, "b3")
            self.begin(p, "c1")
            self.begin(p, "c2")
            self.sibling(p, self.row(p, 1))
            self.sibling(p, self.row(p, 2))
        for p in parts:
            self.onward(p, "c0", self.share(p, "c0", 1), self.share(p, "c0", 2))
        for p in parts:
            for ring in ("b1", "b2", "b3"):
                self.end(p, ring)
            self.begin(p, "c3")
            self.sibling(p, self.row(p, 3))
        for ring in ("c1", "c2", "c3"):
            for p in parts:
                self.onward(p, ring, self.share(p, ring, 1), self.share(p, ring, 2))
            for p in parts:
                before = {"c1": "c0", "c2": "c1", "c3": "c2"}[ring]
                self.end(p, before)
                self.sibling(p, self.at(p, before, 3))
        for p in parts:
            self.end(p, "c3")
            self.sibling(p, self.at(p, "c3", 3))
        for copy in self.copies.values():
            copy.wait_send()
        for copies in self.sibs:
            for copy in copies:
                copy.wait_send()
                copy.wait_recv()


def gather_kernel(*refs):
    Gather(*refs).run()


def gather(own):
    return pl.pallas_call(
        gather_kernel,
        out_shape=jax.ShapeDtypeStruct((4, 2, 4, 4, ROWS, 128), jnp.bfloat16),
        in_specs=[pl.BlockSpec(memory_space=pl.ANY)],
        out_specs=pl.BlockSpec(memory_space=pl.ANY),
        scratch_shapes=Gather.scratch,
        compiler_params=pltpu.CompilerParams(collective_id=0, has_side_effects=True),
    )(own)


EIGHTH = 16 * 433
W_QKV = (24, 768, 18)
W_OUT = (13866, 768, 6)
W_UP = (18480, 768, 24)
W_DOWN = (36936, 3072, 6)
VECTORS = {"ln1_gain": (0, 6), "ln1_shift": (6, 6), "ln2_gain": (12, 6), "ln2_shift": (18, 6),
           "b_qkv": (13848, 18), "b_out": (18474, 6), "b_up": (36912, 24), "b_down": (55368, 6)}


HEADS = 12
TILE = 1024
KEYS = 1024


class Exchange:
    scratch = [pltpu.SemaphoreType.DMA((16,)), pltpu.SemaphoreType.DMA((16,)), pltpu.SemaphoreType.DMA]

    def __init__(self, to_heads, in_ref, out_ref, send, recv, local):
        self.to_heads, self.in_ref, self.out_ref = to_heads, in_ref, out_ref
        self.send, self.recv, self.local = send, recv, local
        self.x, self.core = lax.axis_index("dp_0"), lax.axis_index("dp_1")
        self.me = lax.axis_index("seq_0") * 4 + lax.axis_index("seq_1")
        self.others = [lax.rem(self.me + k, 16) for k in range(1, 16)]

    def where(self, t):
        return (self.x, self.core, lax.div(t, 4), lax.rem(t, 4))

    def copy(self, t):
        return pltpu.make_async_remote_copy(
            self.in_ref.at[t], self.out_ref.at[self.me], self.send.at[t], self.recv.at[self.me],
            device_id=self.where(t), device_id_type=MESH)

    def arrival(self, t):
        return pltpu.make_async_remote_copy(
            self.out_ref.at[t], self.out_ref.at[t], self.send.at[t], self.recv.at[t],
            device_id=self.where(t), device_id_type=MESH)

    def own(self):
        return pltpu.make_async_copy(self.in_ref.at[self.me], self.out_ref.at[self.me], self.local)

    def start(self):
        barrier = pltpu.get_barrier_semaphore()
        for t in self.others:
            pl.semaphore_signal(barrier, inc=1, device_id=self.where(t), device_id_type=MESH)
        pl.semaphore_wait(barrier, 15)
        if self.to_heads:
            for t in self.others:
                pl.when(t < HEADS)(lambda t=t: self.copy(t).start())
            pl.when(self.me < HEADS)(lambda: self.own().start())
        else:
            @pl.when(self.me < HEADS)
            def _():
                for t in self.others:
                    self.copy(t).start()
                self.own().start()

    def wait(self):
        if self.to_heads:
            @pl.when(self.me < HEADS)
            def _():
                for t in self.others:
                    self.arrival(t).wait_recv()
                self.own().wait()
            for t in self.others:
                pl.when(t < HEADS)(lambda t=t: self.copy(t).wait_send())
        else:
            for t in self.others:
                pl.when(t < HEADS)(lambda t=t: self.arrival(t).wait_recv())

            @pl.when(self.me < HEADS)
            def _():
                for t in self.others:
                    self.copy(t).wait_send()
                self.own().wait()


NT = (((1,), (1,)), ((), ()))


def product(a, b, dims=(((1,), (0,)), ((), ()))):
    return lax.dot_general(a, b, dims, preferred_element_type=jnp.float32)


def head_kernel(in_ref, out_ref, k, v, kt, vt, scores, dk, dv):
    blocks = 2048 // TILE
    per = TILE // 128

    def rows(which, i):
        return jnp.concatenate([in_ref[i * per + p, which] for p in range(per)], 0)

    @pl.loop(0, blocks)
    def _(i):
        at = pl.ds(pl.multiple_of(i * TILE, TILE), TILE)
        key = rows(0, i)[:, 64:]
        value = rows(1, i)[:, :64]
        k[at, :] = key
        v[at, :] = value
        kt[:, at] = key.T
        vt[:, at] = value.T
        dk[at, :] = jnp.zeros((TILE, 64), jnp.float32)
        dv[at, :] = jnp.zeros((TILE, 64), jnp.float32)

    @pl.loop(0, blocks)
    def _(i):
        query = rows(0, i)[:, :64] * jnp.bfloat16(0.125)
        grad = rows(1, i)[:, 64:]

        def tile(j):
            return pl.ds(pl.multiple_of(j * KEYS, KEYS), KEYS)

        last = lax.div(i * TILE, KEYS)

        def first(j, top):
            s = product(k[tile(j), :], query, NT)
            scores[tile(j), :] = s
            return jnp.maximum(top, jnp.max(s, 0, keepdims=True))

        top = lax.fori_loop(0, last, first, jnp.full((1, TILE), -1e30, jnp.float32))
        s = product(k[tile(last), :], query, NT)
        keep = lax.broadcasted_iota(jnp.int32, (KEYS, TILE), 0) - lax.broadcasted_iota(jnp.int32, (KEYS, TILE), 1) <= i * TILE - last * KEYS
        s = jnp.where(keep, s, -1e30)
        scores[tile(last), :] = s
        top = jnp.maximum(top, jnp.max(s, 0, keepdims=True))

        def second(j, carry):
            total, out = carry
            e = jnp.exp(scores[tile(j), :] - top)
            scores[tile(j), :] = e
            return total + jnp.sum(e, 0, keepdims=True), out + product(vt[:, tile(j)], e.astype(jnp.bfloat16))

        total, out = lax.fori_loop(0, last + 1, second, (jnp.zeros((1, TILE), jnp.float32), jnp.zeros((64, TILE), jnp.float32)))
        scale = 1.0 / total
        out = out * scale
        inner = jnp.sum(out * grad.astype(jnp.float32).T, 0, keepdims=True)

        def third(j, dq):
            p = scores[tile(j), :] * scale
            dp = product(v[tile(j), :], grad, NT)
            ds = (p * (dp - inner)).astype(jnp.bfloat16)
            dv[tile(j), :] += product(p.astype(jnp.bfloat16), grad)
            dk[tile(j), :] += product(ds, query)
            return dq + product(kt[:, tile(j)], ds)

        dq = lax.fori_loop(0, last + 1, third, jnp.zeros((64, TILE), jnp.float32)) * 0.125
        both = jnp.concatenate([out, dq], 0).T.astype(jnp.bfloat16)
        for p in range(per):
            out_ref[i * per + p, 0] = both[128 * p:128 * (p + 1)]

    @pl.loop(0, blocks)
    def _(i):
        at = pl.ds(pl.multiple_of(i * TILE, TILE), TILE)
        both = jnp.concatenate([dk[at, :], dv[at, :]], 1).astype(jnp.bfloat16)
        for p in range(per):
            out_ref[i * per + p, 1] = both[128 * p:128 * (p + 1)]


def heads(blocks):
    return pl.pallas_call(
        head_kernel,
        out_shape=jax.ShapeDtypeStruct((16, 2, 128, 128), jnp.bfloat16),
        grid=(1,),
        in_specs=[pl.BlockSpec((16, 2, 128, 128), lambda e: (0, 0, 0, 0))],
        out_specs=pl.BlockSpec((16, 2, 128, 128), lambda e: (0, 0, 0, 0)),
        scratch_shapes=[pltpu.VMEM((2048, 64), jnp.bfloat16), pltpu.VMEM((2048, 64), jnp.bfloat16),
                        pltpu.VMEM((64, 2048), jnp.bfloat16), pltpu.VMEM((64, 2048), jnp.bfloat16),
                        pltpu.VMEM((2048, TILE), jnp.float32),
                        pltpu.VMEM((2048, 64), jnp.float32), pltpu.VMEM((2048, 64), jnp.float32)],
        compiler_params=pltpu.CompilerParams(vmem_limit_bytes=VMEM_LIMIT),
    )(blocks)


EPS = 1e-05
ORDER = ("ln1_gain", "ln1_shift", "ln2_gain", "ln2_shift", "b_qkv", "b_out", "b_up", "b_down")


def widen(g_ref, flat, step):
    @pl.loop(0, 16)
    def _(k):
        base = (step * 16 + k) * 433
        flat[pl.ds(base, 440), :] = g_ref[k, 0:440, :].astype(jnp.float32)


def unpack_matrix(flat, first, where, out, size=64):
    offset, rows, blocks = where
    start = offset - first * EIGHTH

    @pl.loop(0, rows // size)
    def _(i):
        for j in range(blocks):
            piece = flat[pl.ds(start + j + i * (size * blocks), size, stride=blocks), :]
            out[pl.ds(pl.multiple_of(i * size, size), size), 128 * j:128 * (j + 1)] = piece.astype(jnp.bfloat16)


def as_row(ref, start, count):
    return jnp.concatenate([ref[start + n:start + n + 1, :] for n in range(count)], 1)


def to_rows(ref, start, row):
    for n in range(row.shape[1] // 128):
        ref[start + n:start + n + 1, :] = row[:, 128 * n:128 * (n + 1)]


def normalized(values):
    center = jnp.mean(values, -1, keepdims=True)
    centered = values - center
    factor = lax.rsqrt(jnp.mean(centered * centered, -1, keepdims=True) + EPS)
    return centered * factor, factor


def turn(x, tables, sign):
    return x * tables[0] + (pltpu.roll(x, 120, 1) * tables[1] + pltpu.roll(x, 8, 1) * tables[2]) * sign


def first_kernel(g_ref, tokens_ref, grad_ref, tables_ref, w_qkv, w_out, blocks_ref, h1t_ref, h2_ref, h2t_ref, vec_ref, flat, wide):
    step = pl.program_id(0)
    widen(g_ref, flat, step)

    @pl.when(step == 1)
    def _():
        unpack_matrix(flat, 0, W_QKV, w_qkv)

    @pl.when(step == 2)
    def _():
        unpack_matrix(flat, 0, W_OUT, w_out)
        vec_ref[0:24, :] = flat[0:24, :]
        start = VECTORS["b_out"][0]
        vec_ref[24:30, :] = flat[start:start + 6, :]
        normal, _ = normalized(tokens_ref[...].astype(jnp.float32))
        h1 = (normal * as_row(flat, 0, 6) + as_row(flat, 6, 6)).astype(jnp.bfloat16)
        h2 = (normal * as_row(flat, 12, 6) + as_row(flat, 18, 6)).astype(jnp.bfloat16)
        h1t_ref[...] = h1.T
        h2_ref[...] = h2
        h2t_ref[...] = h2.T
        for n in range(9):
            start = VECTORS["b_qkv"][0] + 2 * n
            wide[:, 256 * n:256 * (n + 1)] = product(h1, w_qkv[:, 256 * n:256 * (n + 1)]) + as_row(flat, start, 2)
        low = lax.broadcasted_iota(jnp.int32, (128, 128), 1) < 64
        for m in range(6):
            q, k, v = (wide[:, 768 * p + 128 * m:768 * p + 128 * (m + 1)] for p in range(3))
            q = turn(q, tables_ref, 1.0)
            k = turn(k, tables_ref, 1.0)
            a = product(grad_ref[...], w_out[128 * m:128 * (m + 1), :], NT)
            swap = lambda t: pltpu.roll(t, 64, 1)
            blocks_ref[2 * m, 0] = jnp.where(low, q, swap(k)).astype(jnp.bfloat16)
            blocks_ref[2 * m + 1, 0] = jnp.where(low, swap(q), k).astype(jnp.bfloat16)
            blocks_ref[2 * m, 1] = jnp.where(low, v, swap(a)).astype(jnp.bfloat16)
            blocks_ref[2 * m + 1, 1] = jnp.where(low, swap(v), a).astype(jnp.bfloat16)


def const(*shape):
    return pl.BlockSpec(shape, lambda e: (0,) * len(shape))


def first_part(gathered, tokens, grad, tables):
    bf = lambda *s: jax.ShapeDtypeStruct(s, jnp.bfloat16)
    outs = [bf(768, 2304), bf(768, 768), bf(HEADS, 2, 128, 128), bf(768, 128), bf(128, 768), bf(768, 128),
            jax.ShapeDtypeStruct((32, 128), jnp.float32)]
    return pl.pallas_call(
        first_kernel,
        grid=(3,),
        out_shape=outs,
        in_specs=[pl.BlockSpec((16, 448, 128), lambda e: (e, 0, 0)), const(128, 768), const(128, 768), const(3, 128, 128)],
        out_specs=[const(*o.shape) for o in outs],
        scratch_shapes=[pltpu.VMEM((3 * EIGHTH + 16, 128), jnp.float32), pltpu.VMEM((128, 2304), jnp.float32)],
        compiler_params=pltpu.CompilerParams(vmem_limit_bytes=VMEM_LIMIT),
    )(gathered, tokens, grad, tables)


def gelu_pair(u):
    inside = 0.5 * (1.0 + lax.erf(u * 0.7071067811865476))
    return u * inside, inside + u * jnp.exp(-0.5 * u * u) * 0.3989422804014327


def second_kernel(g_ref, h2_ref, grad_ref, blocks_ref, mlp_ref, dh2_ref, act_t_ref, dup_ref, bias_ref, heads_ref,
                  flat, w_up, w_down, act, slope, *sems):
    step = pl.program_id(0)
    swap = Exchange(True, blocks_ref, heads_ref, *sems)
    pl.when(step == 0)(swap.start)
    widen(g_ref, flat, step)

    @pl.when(step == 3)
    def _():
        unpack_matrix(flat, 2, W_UP, w_up)
        start = VECTORS["b_up"][0] - 2 * EIGHTH
        for n in range(12):
            at = slice(256 * n, 256 * (n + 1))
            up = product(h2_ref[...], w_up[:, at]) + as_row(flat, start + 2 * n, 2)
            value, slope[:, at] = gelu_pair(up)
            value = value.astype(jnp.bfloat16)
            act[:, at] = value
            act_t_ref[at, :] = value.T

    @pl.when(step == 5)
    def _():
        unpack_matrix(flat, 2, W_DOWN, w_down, 128)
        start = VECTORS["b_down"][0] - 2 * EIGHTH
        for n in range(3):
            at = slice(256 * n, 256 * (n + 1))
            mlp_ref[:, at] = product(act[...], w_down[:, at]) + as_row(flat, start + 2 * n, 2)
        for n in range(12):
            at = slice(256 * n, 256 * (n + 1))
            dup = (product(grad_ref[...], w_down[at, :], NT) * slope[:, at]).astype(jnp.bfloat16)
            dup_ref[:, at] = dup
            to_rows(bias_ref, 2 * n, jnp.sum(dup.astype(jnp.float32), 0, keepdims=True))
        for n in range(3):
            at = slice(256 * n, 256 * (n + 1))
            dh2_ref[:, at] = product(dup_ref[...], w_up[at, :], NT)
        swap.wait()


def second_part(gathered, h2, grad, blocks):
    bf = lambda *s: jax.ShapeDtypeStruct(s, jnp.bfloat16)
    f32 = lambda *s: jax.ShapeDtypeStruct(s, jnp.float32)
    outs = [f32(128, 768), f32(128, 768), bf(3072, 128), bf(128, 3072), f32(24, 128)]
    anywhere = pl.BlockSpec(memory_space=pl.ANY)
    return pl.pallas_call(
        second_kernel,
        grid=(6,),
        out_shape=outs + [bf(16, 2, 128, 128)],
        in_specs=[pl.BlockSpec((16, 448, 128), lambda e: (e + 2, 0, 0)), const(128, 768), const(128, 768), anywhere],
        out_specs=[const(*o.shape) for o in outs] + [anywhere],
        scratch_shapes=[pltpu.VMEM((6 * EIGHTH + 16, 128), jnp.float32), pltpu.VMEM((768, 3072), jnp.bfloat16),
                        pltpu.VMEM((3072, 768), jnp.bfloat16), pltpu.VMEM((128, 3072), jnp.bfloat16),
                        pltpu.VMEM((128, 3072), jnp.float32)] + Exchange.scratch,
        compiler_params=pltpu.CompilerParams(collective_id=2, has_side_effects=True, vmem_limit_bytes=VMEM_LIMIT),
    )(gathered, h2, grad, blocks)


def third_kernel(back_ref, tokens_ref, grad_ref, tables_ref, w_qkv, w_out, mlp_ref, dh2_ref, bias_ref, in_vec,
                 layer_ref, input_ref, att_t_ref, dqkv_ref, vec_ref):
    low = lax.broadcasted_iota(jnp.int32, (128, 128), 1) < 64
    swap = lambda t: pltpu.roll(t, 64, 1)
    f32 = lambda t: t.astype(jnp.float32)
    attended = []
    for m in range(6):
        a, b = f32(back_ref[2 * m, 0]), f32(back_ref[2 * m + 1, 0])
        c, d = f32(back_ref[2 * m, 1]), f32(back_ref[2 * m + 1, 1])
        attended.append(jnp.where(low, a, swap(b)).astype(jnp.bfloat16))
        dq = turn(jnp.where(low, swap(a), b), tables_ref, -1.0)
        dk = turn(jnp.where(low, c, swap(d)), tables_ref, -1.0)
        dv = jnp.where(low, swap(c), d)
        for p, part in enumerate((dq, dk, dv)):
            dqkv_ref[:, 768 * p + 128 * m:768 * p + 128 * (m + 1)] = part.astype(jnp.bfloat16)
    attended = jnp.concatenate(attended, 1)
    att_t_ref[...] = attended.T
    tokens = f32(tokens_ref[...])
    grad = f32(grad_ref[...])
    layer_ref[...] = (tokens + (product(attended, w_out[...]) + as_row(in_vec, 24, 6)) + mlp_ref[...]).astype(jnp.bfloat16)
    normal, factor = normalized(tokens)
    total = grad
    row = 0
    for gain_at, dh in ((0, product(dqkv_ref[...], w_qkv[...], NT)), (12, dh2_ref[...])):
        to_rows(vec_ref, row, jnp.sum(dh * normal, 0, keepdims=True))
        to_rows(vec_ref, row + 6, jnp.sum(dh, 0, keepdims=True))
        row += 12
        scaled = dh * as_row(in_vec, gain_at, 6)
        inner = scaled - jnp.mean(scaled, -1, keepdims=True) - normal * jnp.mean(scaled * normal, -1, keepdims=True)
        total = total + factor * inner
    input_ref[...] = total
    to_rows(vec_ref, 24, jnp.sum(f32(dqkv_ref[...]), 0, keepdims=True))
    shift = jnp.sum(grad, 0, keepdims=True)
    to_rows(vec_ref, 42, shift)
    vec_ref[48:72, :] = bias_ref[...]
    to_rows(vec_ref, 72, shift)
    vec_ref[78:80, :] = jnp.zeros((2, 128), jnp.float32)


def third_part(*args):
    bf = lambda *s: jax.ShapeDtypeStruct(s, jnp.bfloat16)
    f32 = lambda *s: jax.ShapeDtypeStruct(s, jnp.float32)
    outs = [bf(128, 768), f32(128, 768), bf(768, 128), bf(128, 2304), f32(80, 128)]
    return pl.pallas_call(
        third_kernel,
        grid=(1,),
        out_shape=outs,
        in_specs=[const(*a.shape) for a in args],
        out_specs=[const(*o.shape) for o in outs],
        compiler_params=pltpu.CompilerParams(vmem_limit_bytes=VMEM_LIMIT),
    )(*args)


def rotary_tables(positions):
    lane = jnp.arange(128) % 64
    freq = jnp.tile(10000.0 ** (-jnp.arange(8).astype(jnp.float32) * 2.0 / 16), 16)
    angles = positions.astype(jnp.float32)[:, None] * freq[None, :]
    cosine, sine = jnp.cos(angles), jnp.sin(angles)
    return jnp.stack([jnp.where(lane < 16, cosine, 1.0), jnp.where(lane < 8, -sine, 0.0),
                      jnp.where((lane >= 8) & (lane < 16), sine, 0.0)])


MARGIN = 384
CHUNK = 128


def weight_eighth(number, pairs, vec_ref, flat):
    low, high = number * EIGHTH, (number + 1) * EIGHTH
    at = MARGIN - low
    for (offset, rows, blocks), left, right in pairs:
        first = max(0, (low - offset) // blocks) // 16 * 16
        last = min(rows, -(-(high - offset) // blocks))
        last = -(-last // 16) * 16
        if last <= first:
            continue
        size = min(CHUNK, last - first)
        count = -(-(last - first) // size)
        base = offset + at

        @pl.loop(0, count)
        def _(i, first=first, last=last, size=size, blocks=blocks, base=base, left=left, right=right):
            row = pl.multiple_of(jnp.minimum(first + i * size, last - size), 16)
            lhs = left[pl.ds(row, size), :]

            @pl.loop(0, blocks // 2, unroll=3)
            def _(j):
                rhs = right[:, pl.ds(pl.multiple_of(j * 256, 256), 256)]
                result = product(lhs, rhs)
                start = base + row * blocks + 2 * j
                flat[pl.ds(start, size, stride=blocks), :] = result[:, :128]
                flat[pl.ds(start + 1, size, stride=blocks), :] = result[:, 128:]

    row = 0
    for name in ORDER:
        start, count = VECTORS[name]
        lo, hi = max(start, low), min(start + count, high)
        if lo < hi:
            flat[lo + at:hi + at, :] = vec_ref[row + lo - start:row + hi - start, :]
        row += count
    end = 55374
    if high > end:
        flat[end + at:high + at, :] = jnp.zeros((high - end, 128), jnp.float32)


def join(pair, mine, theirs, lanes):
    if lanes:
        pair[:, :128] = mine[...]
        pair[:, 128:] = theirs[...]
    else:
        pair[:128, :] = mine[...]
        pair[128:, :] = theirs[...]


def pack(flat, out_ref):
    @pl.loop(0, 16)
    def _(k):
        out_ref[0, k] = flat[pl.ds(MARGIN + 433 * k, 448), :].astype(jnp.bfloat16)


def eighths(steps, step, core, pairs, vec_ref, flat):
    for n, t in enumerate(steps):
        for c in range(2):
            pl.when((step == n) & (core == c))(lambda number=2 * t + c: weight_eighth(number, pairs, vec_ref, flat))


HALVES = jax.ShapeDtypeStruct((4, 16, 448, 128), jnp.bfloat16)


def late_kernel(vec_ref, act_ref, act2_ref, g_ref, g2_ref, dup_ref, dup2_ref, h2_ref, h22_ref, heads_ref,
                out_ref, back_ref, flat, act, g, dup, h2, *sems):
    step = pl.program_id(0)
    swap = Exchange(False, heads_ref, back_ref, *sems)

    @pl.when(step == 0)
    def _():
        swap.start()
        join(act, act_ref, act2_ref, True)
        join(h2, h2_ref, h22_ref, True)
        join(g, g_ref, g2_ref, False)
        join(dup, dup_ref, dup2_ref, False)

    eighths((2, 3), step, lax.axis_index("dp_1"), ((W_UP, h2, dup), (W_DOWN, act, g)), vec_ref, flat)
    pack(flat, out_ref)
    pl.when(step == 1)(swap.wait)


def late_grads(vec, act, act2, g, g2, dup, dup2, h2, h22, heads_out):
    args = (vec, act, act2, g, g2, dup, dup2, h2, h22)
    anywhere = pl.BlockSpec(memory_space=pl.ANY)
    pairs = [(3072, 256), (256, 768), (256, 3072), (768, 256)]
    return pl.pallas_call(
        late_kernel,
        grid=(2,),
        out_shape=[HALVES, jax.ShapeDtypeStruct((HEADS, 2, 128, 128), jnp.bfloat16)],
        in_specs=[const(*a.shape) for a in args] + [anywhere],
        out_specs=[pl.BlockSpec((1, 16, 448, 128), lambda e: (e + 2, 0, 0, 0)), anywhere],
        scratch_shapes=[pltpu.VMEM((EIGHTH + 2 * MARGIN, 128), jnp.float32)]
        + [pltpu.VMEM(p, jnp.bfloat16) for p in pairs] + Exchange.scratch,
        compiler_params=pltpu.CompilerParams(collective_id=3, has_side_effects=True, vmem_limit_bytes=VMEM_LIMIT),
    )(*args, heads_out)


def early_kernel(core_ref, vec_ref, h1_ref, h12_ref, att_ref, att2_ref, h2_ref, h22_ref, dqkv_ref, dqkv2_ref,
                 g_ref, g2_ref, dup_ref, dup2_ref, halves_ref, out_ref, flat, h1, att, h2, dqkv, g, dup):
    step = pl.program_id(0)

    @pl.when(step == 0)
    def _():
        join(h1, h1_ref, h12_ref, True)
        join(att, att_ref, att2_ref, True)
        join(h2, h2_ref, h22_ref, True)
        join(dqkv, dqkv_ref, dqkv2_ref, False)
        join(g, g_ref, g2_ref, False)
        join(dup, dup_ref, dup2_ref, False)

    eighths((0, 1), step, core_ref[0], ((W_QKV, h1, dqkv), (W_OUT, att, g), (W_UP, h2, dup)), vec_ref, flat)
    pack(flat, out_ref)


def early_grads(core, vec, h1, h12, att, att2, h2, h22, dqkv, dqkv2, g, g2, dup, dup2, halves):
    args = (vec, h1, h12, att, att2, h2, h22, dqkv, dqkv2, g, g2, dup, dup2)
    pairs = [(768, 256)] * 3 + [(256, 2304), (256, 768), (256, 3072)]
    return pl.pallas_call(
        early_kernel,
        grid=(2,),
        out_shape=HALVES,
        in_specs=[pl.BlockSpec(memory_space=pltpu.SMEM)] + [const(*a.shape) for a in args] + [pl.BlockSpec(memory_space=pl.ANY)],
        out_specs=pl.BlockSpec((1, 16, 448, 128), lambda e: (e, 0, 0, 0)),
        scratch_shapes=[pltpu.VMEM((EIGHTH + 2 * MARGIN, 128), jnp.float32)] + [pltpu.VMEM(p, jnp.bfloat16) for p in pairs],
        input_output_aliases={14: 0},
        compiler_params=pltpu.CompilerParams(vmem_limit_bytes=VMEM_LIMIT),
    )(core, *args, halves)


def halves(size):
    half = size // 32 * 16
    return half, size - half


class Scatter:
    names = ("c0", "c1", "c2", "c3", "b", "a")
    count = 3 * (6 * 8 + 2)

    @staticmethod
    def scratch():
        out = []
        for _, size, _ in PARTS:
            h0, h1 = halves(size)
            for name in Scatter.names:
                lead = () if name == "a" else (4,)
                out += [pltpu.VMEM(lead + (n, 128), jnp.bfloat16) for n in (h0, h1, h1, h0, h0, h1, h0, h1)]
            out += [pltpu.VMEM((4, 4, size, 128), jnp.bfloat16), pltpu.VMEM((4, size, 128), jnp.bfloat16)]
        return out + [pltpu.SemaphoreType.DMA((3, 6, 6)), pltpu.SemaphoreType.DMA((3, 6, 6))]

    def __init__(self, in_ref, out_ref, *scratch):
        self.in_ref, self.out_ref = in_ref, out_ref
        self.send, self.recv = scratch[-2:]
        take = iter(scratch[:-2])
        self.buf, self.rows, self.line = {}, [], []
        for p in range(3):
            for name in self.names:
                self.buf[p, name] = [next(take) for _ in range(8)]
            self.rows.append(next(take))
            self.line.append(next(take))
        self.pos, self.core = place()
        self.copies = {}

    def near(self, axis):
        q = self.pos[axis]
        return [q] + [lax.rem(q + k, 4) for k in (3, 1, 2)]

    def axis(self, p, name):
        return PARTS[p][2]["abc".index(name[0])]

    def source(self, p, name, which, lo, n):
        a, b, c = PARTS[p][2]
        if name == "a":
            return self.line[p].at[self.near(a)[which], pl.ds(lo, n), :]
        if name == "b":
            return self.rows[p].at[which, :, pl.ds(lo, n), :]
        where = [slice(None)] * 3
        where[b] = self.near(b)[int(name[1])]
        where[c] = self.near(c)[which]
        return self.in_ref.at[where[0], where[1], where[2], pl.ds(PARTS[p][0] + lo, n), :]

    def push(self, p, name, number, src, by):
        n = self.names.index(name)
        copy = pltpu.make_async_remote_copy(
            src, self.buf[p, name][number], self.send.at[p, n, number], self.recv.at[p, n, number],
            device_id=device(moved(self.pos, self.axis(p, name), by), self.core), device_id_type=MESH)
        copy.start()
        self.copies[p, name, number] = copy

    def far(self, p, name):
        h0, h1 = halves(PARTS[p][1])
        self.push(p, name, 0, self.source(p, name, 3, 0, h0), 1)
        self.push(p, name, 1, self.source(p, name, 3, h0, h1), 3)

    def raw_right(self, p, name):
        h0, h1 = halves(PARTS[p][1])
        self.push(p, name, 2, self.source(p, name, 2, h0, h1), 1)

    def raw_left(self, p, name):
        h0, h1 = halves(PARTS[p][1])
        self.push(p, name, 3, self.source(p, name, 1, 0, h0), 3)

    def begin(self, p, name):
        self.far(p, name)
        self.raw_right(p, name)
        self.raw_left(p, name)

    def add(self, name, mine, others, put):
        def one(*at):
            total = mine[at + (slice(None), slice(None))].astype(jnp.float32)
            for other in others:
                total = total + other[at + (slice(None), slice(None))].astype(jnp.float32)
            put(at, total)

        if name == "a":
            one()
        else:
            pl.loop(0, 4)(lambda i: one(i))

    def onward(self, p, name):
        h0, h1 = halves(PARTS[p][1])
        b = self.buf[p, name]

        def to(ref):
            def put(at, total):
                ref[at + (slice(None), slice(None))] = total.astype(jnp.bfloat16)
            return put

        self.copies[p, name, 0].wait_recv()
        self.add(name, self.source(p, name, 2, 0, h0), [b[0]], to(b[6]))
        self.push(p, name, 4, b[6], 1)
        self.copies[p, name, 1].wait_recv()
        self.add(name, self.source(p, name, 1, h0, h1), [b[1]], to(b[7]))
        self.push(p, name, 5, b[7], 3)

    def end(self, p, name):
        start, size, _ = PARTS[p]
        h0, h1 = halves(size)
        b = self.buf[p, name]
        for number in (3, 2, 4, 5):
            self.copies[p, name, number].wait_recv()
        for lo, n, others in ((0, h0, [b[3], b[4]]), (h0, h1, [b[2], b[5]])):
            def put(at, total, lo=lo, n=n):
                if name == "a":
                    self.out_ref[start + lo:start + lo + n, :] = total
                elif name == "b":
                    self.line[p][at + (pl.ds(lo, n), slice(None))] = total.astype(jnp.bfloat16)
                else:
                    self.rows[p][(int(name[1]),) + at + (pl.ds(lo, n), slice(None))] = total.astype(jnp.bfloat16)
            self.add(name, self.source(p, name, 0, lo, n), others, put)

    def run(self):
        parts = range(3)

        def each(step, name):
            for p in parts:
                step(p, name)

        greet(self.pos, self.core, sibling=False)
        each(self.begin, "c3")
        each(self.begin, "c1")
        each(self.onward, "c3")
        each(self.begin, "c2")
        each(self.onward, "c1")
        each(self.end, "c3")
        each(self.far, "b")
        each(self.begin, "c0")
        each(self.onward, "c2")
        each(self.end, "c1")
        each(self.raw_left, "b")
        each(self.onward, "c0")
        each(self.end, "c2")
        each(self.raw_right, "b")
        each(self.onward, "b")
        for p in parts:
            self.end(p, "c0")
            self.end(p, "b")
            self.begin(p, "a")
        each(self.onward, "a")
        each(self.end, "a")
        for copy in self.copies.values():
            copy.wait_send()


def scatter_kernel(*refs):
    Scatter(*refs).run()


def scatter(parts):
    return pl.pallas_call(
        scatter_kernel,
        grid=(1,),
        out_shape=jax.ShapeDtypeStruct((ROWS, 128), jnp.float32),
        in_specs=[pl.BlockSpec((4, 4, 4, ROWS, 128), lambda e: (0, 0, 0, 0, 0))],
        out_specs=pl.BlockSpec((ROWS, 128), lambda e: (0, 0)),
        scratch_shapes=Scatter.scratch(),
        compiler_params=pltpu.CompilerParams(collective_id=1, has_side_effects=True, vmem_limit_bytes=VMEM_LIMIT),
    )(parts)


def twin(array):
    return lax.ppermute(array, "dp_1", [(0, 1), (1, 0)])


def body(tokens, params, out_grad):
    piece = tokens.shape[1]
    x, grad = tokens[0], out_grad[0]
    own = jnp.pad(params.reshape(433, 128), ((0, ROWS - 433), (0, 0)))
    gathered = gather(own).reshape(128, ROWS, 128)
    tables = rotary_tables(lax.axis_index(SEQ) * piece + jnp.arange(piece))
    w_qkv, w_out, blocks, h1t, h2, h2t, in_vec = first_part(gathered, x, grad, tables)
    mlp, dh2, act_t, dup, bias, at_heads = second_part(gathered, h2, grad, blocks)
    shift = jnp.sum(grad.astype(jnp.float32), 0).reshape(6, 128)
    late_vec = jnp.concatenate([jnp.zeros((48, 128), jnp.float32), bias, shift, jnp.zeros((2, 128), jnp.float32)])
    late_vec = late_vec + twin(late_vec)
    act2, g2, dup2, h22, h12 = (twin(a) for a in (act_t, grad, dup, h2t, h1t))
    halves_sum, back = late_grads(late_vec, act_t, act2, grad, g2, dup, dup2, h2t, h22, heads(at_heads))
    layer_out, input_grad, att_t, dqkv, vec = third_part(
        back, x, grad, tables, w_qkv, w_out, mlp, dh2, bias, in_vec
    )
    vec = vec + twin(vec)
    core = lax.axis_index("dp_1").astype(jnp.int32).reshape(1)
    halves_sum = early_grads(
        core, vec, h1t, h12, att_t, twin(att_t), h2t, h22, dqkv, twin(dqkv), grad, g2, dup, dup2, halves_sum
    )
    param_grad = scatter(halves_sum.reshape(4, 4, 4, ROWS, 128))[:433].reshape(-1)
    return layer_out[None], input_grad[None], param_grad


def solution(mesh):
    finer = Mesh(mesh.devices.reshape(4, 2, 4, 4), DP_SEQ)
    in_specs = (P(DP, SEQ, None), P(DP_SEQ), P(DP, SEQ, None))
    out_specs = (P(DP, SEQ, None), P(DP, SEQ, None), P(DP_SEQ))
    return jax.shard_map(body, mesh=finer, in_specs=in_specs, out_specs=out_specs, check_vma=False)
```

```python
import functools

import jax
import jax.numpy as jnp
from jax import lax
from jax.experimental import pallas as pl
from jax.experimental.pallas import tpu as pltpu
from jax.sharding import Mesh
from jax.sharding import PartitionSpec as P

DP_SEQ = ("dp_0", "dp_1", "seq_0", "seq_1")
SEQ = ("seq_0", "seq_1")
DP = ("dp_0", "dp_1")
VMEM_LIMIT = 60 * 2**20
MESH = pl.DeviceIdType.MESH
ROWS = 448
PARTS = ((0, 144, (0, 2, 1)), (144, 144, (2, 1, 0)), (288, 160, (1, 0, 2)))


def place():
    return [lax.axis_index("dp_0"), lax.axis_index("seq_0"), lax.axis_index("seq_1")], lax.axis_index("dp_1")


def device(pos, core):
    return (pos[0], core, pos[1], pos[2])


def moved(pos, axis, by):
    out = list(pos)
    out[axis] = lax.rem(pos[axis] + by, 4)
    return out


def greet(pos, core, sibling=True):
    barrier = pltpu.get_barrier_semaphore()
    others = [device(moved(pos, a, by), core) for a in range(3) for by in (1, 3)]
    if sibling:
        others.append(device(pos, 1 - core))
    for other in others:
        pl.semaphore_signal(barrier, inc=1, device_id=other, device_id_type=MESH)
    pl.semaphore_wait(barrier, len(others))


class Gather:
    scratch = [pltpu.SemaphoreType.DMA((3, 9, 4)), pltpu.SemaphoreType.DMA((3, 9, 4)),
               pltpu.SemaphoreType.DMA((3, 19)), pltpu.SemaphoreType.DMA((3, 19)), pltpu.SemaphoreType.DMA]
    rings = ("a", "b0", "b1", "b2", "b3", "c0", "c1", "c2", "c3")

    def __init__(self, own_ref, out_ref, send, recv, sib_send, sib_recv, local):
        self.own_ref, self.out_ref, self.local = own_ref, out_ref, local
        self.send_sem, self.recv_sem, self.sib_send, self.sib_recv = send, recv, sib_send, sib_recv
        self.pos, self.core = place()
        self.copies, self.sibs = {}, [[], [], []]

    def near(self, axis):
        q = self.pos[axis]
        return [q] + [lax.rem(q + k, 4) for k in (3, 1, 2)]

    def region(self, where, start, size):
        return self.out_ref.at[where[0], self.core, where[1], where[2], pl.ds(start, size), :]

    def base(self, part, ring):
        a, b, c = PARTS[part][2]
        where = list(self.pos)
        if ring == "a":
            return a, where
        number = int(ring[1])
        if ring[0] == "b":
            where[a] = self.near(a)[number]
            return b, where
        where[a] = slice(None)
        where[b] = self.near(b)[number]
        return c, where

    def at(self, part, ring, which):
        axis, where = self.base(part, ring)
        where[axis] = self.near(axis)[which]
        return where

    def push(self, part, ring, number, which, by, start, size, src=None):
        axis, _ = self.base(part, ring)
        n = self.rings.index(ring)
        ref = self.region(self.at(part, ring, which), start, size)
        copy = pltpu.make_async_remote_copy(
            ref if src is None else src, ref, self.send_sem.at[part, n, number], self.recv_sem.at[part, n, number],
            device_id=device(moved(self.pos, axis, by), self.core), device_id_type=MESH)
        copy.start()
        self.copies[part, ring, number] = copy

    def begin(self, part, ring):
        start, size, _ = PARTS[part]
        src = self.own_ref.at[pl.ds(start, size), :] if ring in ("a", "b0") else None
        self.push(part, ring, 0, 0, 1, start, size, src)
        self.push(part, ring, 1, 0, 3, start, size, src)

    def onward(self, part, ring, left=None, right=None):
        start, size, _ = PARTS[part]
        half = size // 32 * 16
        self.copies[part, ring, 0].wait_recv()
        self.push(part, ring, 2, 1, 1, start, half)
        if left:
            left()
        self.copies[part, ring, 1].wait_recv()
        self.push(part, ring, 3, 2, 3, start + half, size - half)
        if right:
            right()

    def end(self, part, ring):
        self.copies[part, ring, 2].wait_recv()
        self.copies[part, ring, 3].wait_recv()

    def sibling(self, part, where, src=None):
        start, size, _ = PARTS[part]
        number = len(self.sibs[part])
        ref = self.region(where, start, size)
        copy = pltpu.make_async_remote_copy(
            ref if src is None else src, ref, self.sib_send.at[part, number], self.sib_recv.at[part, number],
            device_id=device(self.pos, 1 - self.core), device_id_type=MESH)
        copy.start()
        self.sibs[part].append(copy)

    def share(self, part, ring, which):
        return lambda: self.sibling(part, self.at(part, ring, which))

    def row(self, part, number):
        a, b, _ = PARTS[part][2]
        where = list(self.pos)
        where[a] = slice(None)
        where[b] = self.near(b)[number]
        return where

    def run(self):
        parts = range(3)
        own = pltpu.make_async_copy(self.own_ref, self.out_ref.at[self.pos[0], self.core, self.pos[1], self.pos[2]], self.local)
        own.start()
        greet(self.pos, self.core)
        for p in parts:
            self.begin(p, "a")
        for p in parts:
            self.begin(p, "b0")
        for p in parts:
            start, size, _ = PARTS[p]
            self.sibling(p, self.pos, self.own_ref.at[pl.ds(start, size), :])
        own.wait()
        for p in parts:
            def arrived(which, p=p):
                self.begin(p, "b" + str(which))
                self.sibling(p, self.at(p, "a", which))
            self.onward(p, "a", lambda: arrived(1), lambda: arrived(2))
        for p in parts:
            self.onward(p, "b0")
        for p in parts:
            self.end(p, "a")
            self.begin(p, "b3")
            self.begin(p, "c0")
            self.sibling(p, self.at(p, "a", 3))
        for p in parts:
            self.onward(p, "b1")
            self.onward(p, "b2")
        for p in parts:
            self.end(p, "b0")
            self.onward(p, "b3")
            self.begin(p, "c1")
            self.begin(p, "c2")
            self.sibling(p, self.row(p, 1))
            self.sibling(p, self.row(p, 2))
        for p in parts:
            self.onward(p, "c0", self.share(p, "c0", 1), self.share(p, "c0", 2))
        for p in parts:
            for ring in ("b1", "b2", "b3"):
                self.end(p, ring)
            self.begin(p, "c3")
            self.sibling(p, self.row(p, 3))
        for ring in ("c1", "c2", "c3"):
            for p in parts:
                self.onward(p, ring, self.share(p, ring, 1), self.share(p, ring, 2))
            for p in parts:
                before = {"c1": "c0", "c2": "c1", "c3": "c2"}[ring]
                self.end(p, before)
                self.sibling(p, self.at(p, before, 3))
        for p in parts:
            self.end(p, "c3")
            self.sibling(p, self.at(p, "c3", 3))
        for copy in self.copies.values():
            copy.wait_send()
        for copies in self.sibs:
            for copy in copies:
                copy.wait_send()
                copy.wait_recv()


def gather_kernel(*refs):
    Gather(*refs).run()


def gather(own):
    return pl.pallas_call(
        gather_kernel,
        out_shape=jax.ShapeDtypeStruct((4, 2, 4, 4, ROWS, 128), jnp.bfloat16),
        in_specs=[pl.BlockSpec(memory_space=pl.ANY)],
        out_specs=pl.BlockSpec(memory_space=pl.ANY),
        scratch_shapes=Gather.scratch,
        compiler_params=pltpu.CompilerParams(collective_id=0, has_side_effects=True),
    )(own)


EIGHTH = 16 * 433
W_QKV = (24, 768, 18)
W_OUT = (13866, 768, 6)
W_UP = (18480, 768, 24)
W_DOWN = (36936, 3072, 6)
VECTORS = {"ln1_gain": (0, 6), "ln1_shift": (6, 6), "ln2_gain": (12, 6), "ln2_shift": (18, 6),
           "b_qkv": (13848, 18), "b_out": (18474, 6), "b_up": (36912, 24), "b_down": (55368, 6)}


HEADS = 12
TILE = 1024
KEYS = 1024


class Exchange:
    scratch = [pltpu.SemaphoreType.DMA((16,)), pltpu.SemaphoreType.DMA((16,)), pltpu.SemaphoreType.DMA]

    def __init__(self, to_heads, in_ref, out_ref, send, recv, local):
        self.to_heads, self.in_ref, self.out_ref = to_heads, in_ref, out_ref
        self.send, self.recv, self.local = send, recv, local
        self.x, self.core = lax.axis_index("dp_0"), lax.axis_index("dp_1")
        self.me = lax.axis_index("seq_0") * 4 + lax.axis_index("seq_1")
        self.others = [lax.rem(self.me + k, 16) for k in range(1, 16)]

    def where(self, t):
        return (self.x, self.core, lax.div(t, 4), lax.rem(t, 4))

    def copy(self, t):
        return pltpu.make_async_remote_copy(
            self.in_ref.at[t], self.out_ref.at[self.me], self.send.at[t], self.recv.at[self.me],
            device_id=self.where(t), device_id_type=MESH)

    def arrival(self, t):
        return pltpu.make_async_remote_copy(
            self.out_ref.at[t], self.out_ref.at[t], self.send.at[t], self.recv.at[t],
            device_id=self.where(t), device_id_type=MESH)

    def own(self):
        return pltpu.make_async_copy(self.in_ref.at[self.me], self.out_ref.at[self.me], self.local)

    def greet(self):
        barrier = pltpu.get_barrier_semaphore()
        for t in self.others:
            pl.semaphore_signal(barrier, inc=1, device_id=self.where(t), device_id_type=MESH)
        twin = (self.x, 1 - self.core, lax.div(self.me, 4), lax.rem(self.me, 4))
        pl.semaphore_signal(barrier, inc=1, device_id=twin, device_id_type=MESH)
        pl.semaphore_wait(barrier, 16)

    def start(self):
        if self.to_heads:
            for t in self.others:
                pl.when(t < HEADS)(lambda t=t: self.copy(t).start())
            pl.when(self.me < HEADS)(lambda: self.own().start())
        else:
            @pl.when(self.me < HEADS)
            def _():
                for t in self.others:
                    self.copy(t).start()
                self.own().start()

    def wait(self):
        if self.to_heads:
            @pl.when(self.me < HEADS)
            def _():
                for t in self.others:
                    self.arrival(t).wait_recv()
                self.own().wait()
        else:
            for t in self.others:
                pl.when(t < HEADS)(lambda t=t: self.arrival(t).wait_recv())

            @pl.when(self.me < HEADS)
            def _():
                for t in self.others:
                    self.copy(t).wait_send()
                self.own().wait()

    def wait_send(self):
        for t in self.others:
            pl.when(t < HEADS)(lambda t=t: self.copy(t).wait_send())


NT = (((1,), (1,)), ((), ()))


def product(a, b, dims=(((1,), (0,)), ((), ()))):
    return lax.dot_general(a, b, dims, preferred_element_type=jnp.float32)


def head_kernel(in_ref, out_ref, k, v, kt, vt, scores, dk, dv):
    blocks = 2048 // TILE
    per = TILE // 128

    def rows(which, i):
        return jnp.concatenate([in_ref[i * per + p, which] for p in range(per)], 0)

    @pl.loop(0, blocks)
    def _(i):
        at = pl.ds(pl.multiple_of(i * TILE, TILE), TILE)
        key = rows(0, i)[:, 64:]
        value = rows(1, i)[:, :64]
        k[at, :] = key
        v[at, :] = value
        kt[:, at] = key.T
        vt[:, at] = value.T
        dk[at, :] = jnp.zeros((TILE, 64), jnp.float32)
        dv[at, :] = jnp.zeros((TILE, 64), jnp.float32)

    @pl.loop(0, blocks)
    def _(i):
        query = rows(0, i)[:, :64] * jnp.bfloat16(0.125)
        grad = rows(1, i)[:, 64:]

        def tile(j):
            return pl.ds(pl.multiple_of(j * KEYS, KEYS), KEYS)

        def put(j, s):
            for n in range(TILE // 128):
                scores[pl.ds(pl.multiple_of(j * KEYS, KEYS) + n * 2048, KEYS), :] = s[:, 128 * n:128 * (n + 1)]

        def get(j):
            return jnp.concatenate(
                [scores[pl.ds(pl.multiple_of(j * KEYS, KEYS) + n * 2048, KEYS), :] for n in range(TILE // 128)], 1)

        last = lax.div(i * TILE, KEYS)

        def first(j, top):
            s = product(k[tile(j), :], query, NT)
            put(j, s)
            return jnp.maximum(top, jnp.max(s, 0, keepdims=True))

        top = lax.fori_loop(0, last, first, jnp.full((1, TILE), -1e30, jnp.float32))
        s = product(k[tile(last), :], query, NT)
        keep = lax.broadcasted_iota(jnp.int32, (KEYS, TILE), 0) - lax.broadcasted_iota(jnp.int32, (KEYS, TILE), 1) <= i * TILE - last * KEYS
        s = jnp.where(keep, s, -1e30)
        put(last, s)
        top = jnp.maximum(top, jnp.max(s, 0, keepdims=True))

        def second(j, carry):
            total, out = carry
            e = jnp.exp(get(j) - top)
            put(j, e)
            return total + jnp.sum(e, 0, keepdims=True), out + product(vt[:, tile(j)], e.astype(jnp.bfloat16))

        total, out = lax.fori_loop(0, last + 1, second, (jnp.zeros((1, TILE), jnp.float32), jnp.zeros((64, TILE), jnp.float32)))
        scale = 1.0 / total
        out = out * scale
        inner = jnp.sum(out * grad.astype(jnp.float32).T, 0, keepdims=True)

        def third(j, dq):
            p = get(j) * scale
            dp = product(v[tile(j), :], grad, NT)
            ds = (p * (dp - inner)).astype(jnp.bfloat16)
            dv[tile(j), :] += product(p.astype(jnp.bfloat16), grad)
            dk[tile(j), :] += product(ds, query)
            return dq + product(kt[:, tile(j)], ds)

        dq = lax.fori_loop(0, last + 1, third, jnp.zeros((64, TILE), jnp.float32)) * 0.125
        both = jnp.concatenate([out, dq], 0).T.astype(jnp.bfloat16)
        for p in range(per):
            out_ref[i * per + p, 0] = both[128 * p:128 * (p + 1)]

    @pl.loop(0, blocks)
    def _(i):
        at = pl.ds(pl.multiple_of(i * TILE, TILE), TILE)
        both = jnp.concatenate([dk[at, :], dv[at, :]], 1).astype(jnp.bfloat16)
        for p in range(per):
            out_ref[i * per + p, 1] = both[128 * p:128 * (p + 1)]


HEAD_SCRATCH = [pltpu.VMEM((2048, 64), jnp.bfloat16), pltpu.VMEM((2048, 64), jnp.bfloat16),
                pltpu.VMEM((64, 2048), jnp.bfloat16), pltpu.VMEM((64, 2048), jnp.bfloat16),
                pltpu.VMEM((2048, 64), jnp.float32), pltpu.VMEM((2048, 64), jnp.float32)]


MARGIN = 384
CHUNK = 128


def weight_eighth(number, pairs, vec_ref, flat):
    low, high = number * EIGHTH, (number + 1) * EIGHTH
    at = MARGIN - low
    for (offset, rows, blocks), left, right in pairs:
        first = max(0, (low - offset) // blocks) // 16 * 16
        last = min(rows, -(-(high - offset) // blocks))
        last = -(-last // 16) * 16
        if last <= first:
            continue
        size = min(CHUNK, last - first)
        count = -(-(last - first) // size)
        base = offset + at

        @pl.loop(0, count)
        def _(i, first=first, last=last, size=size, blocks=blocks, base=base, left=left, right=right):
            row = pl.multiple_of(jnp.minimum(first + i * size, last - size), 16)
            lhs = left[pl.ds(row, size), :]

            @pl.loop(0, blocks // 2, unroll=3)
            def _(j):
                rhs = right[:, pl.ds(pl.multiple_of(j * 256, 256), 256)]
                result = product(lhs, rhs)
                start = base + row * blocks + 2 * j
                flat[pl.ds(start, size, stride=blocks), :] = result[:, :128]
                flat[pl.ds(start + 1, size, stride=blocks), :] = result[:, 128:]

    row = 0
    for name in ORDER:
        start, count = VECTORS[name]
        lo, hi = max(start, low), min(start + count, high)
        if lo < hi:
            flat[lo + at:hi + at, :] = vec_ref[row + lo - start:row + hi - start, :]
        row += count
    end = 55374
    if high > end:
        flat[end + at:high + at, :] = jnp.zeros((high - end, 128), jnp.float32)


def halves(size):
    half = size // 32 * 16
    return half, size - half


class Scatter:
    names = ("c0", "c1", "c2", "c3", "b", "a")
    count = 3 * (6 * 8 + 2)

    @staticmethod
    def scratch():
        out = []
        for _, size, _ in PARTS:
            h0, h1 = halves(size)
            for name in Scatter.names:
                lead = () if name == "a" else (4,)
                out += [pltpu.VMEM(lead + (n, 128), jnp.bfloat16) for n in (h0, h1, h1, h0, h0, h1, h0, h1)]
            out += [pltpu.VMEM((4, 4, size, 128), jnp.bfloat16), pltpu.VMEM((4, size, 128), jnp.bfloat16)]
        return out + [pltpu.SemaphoreType.DMA((3, 6, 6)), pltpu.SemaphoreType.DMA((3, 6, 6))]

    def __init__(self, in_ref, out_ref, *scratch):
        self.in_ref, self.out_ref = in_ref, out_ref
        self.send, self.recv = scratch[-2:]
        take = iter(scratch[:-2])
        self.buf, self.rows, self.line = {}, [], []
        for p in range(3):
            for name in self.names:
                self.buf[p, name] = [next(take) for _ in range(8)]
            self.rows.append(next(take))
            self.line.append(next(take))
        self.pos, self.core = place()
        self.copies = {}

    def near(self, axis):
        q = self.pos[axis]
        return [q] + [lax.rem(q + k, 4) for k in (3, 1, 2)]

    def axis(self, p, name):
        return PARTS[p][2]["abc".index(name[0])]

    def source(self, p, name, which, lo, n):
        a, b, c = PARTS[p][2]
        if name == "a":
            return self.line[p].at[self.near(a)[which], pl.ds(lo, n), :]
        if name == "b":
            return self.rows[p].at[which, :, pl.ds(lo, n), :]
        where = [slice(None)] * 3
        where[b] = self.near(b)[int(name[1])]
        where[c] = self.near(c)[which]
        return self.in_ref.at[where[0], where[1], where[2], pl.ds(PARTS[p][0] + lo, n), :]

    def push(self, p, name, number, src, by):
        n = self.names.index(name)
        copy = pltpu.make_async_remote_copy(
            src, self.buf[p, name][number], self.send.at[p, n, number], self.recv.at[p, n, number],
            device_id=device(moved(self.pos, self.axis(p, name), by), self.core), device_id_type=MESH)
        copy.start()
        self.copies[p, name, number] = copy

    def far(self, p, name):
        h0, h1 = halves(PARTS[p][1])
        self.push(p, name, 0, self.source(p, name, 3, 0, h0), 1)
        self.push(p, name, 1, self.source(p, name, 3, h0, h1), 3)

    def raw_right(self, p, name):
        h0, h1 = halves(PARTS[p][1])
        self.push(p, name, 2, self.source(p, name, 2, h0, h1), 1)

    def raw_left(self, p, name):
        h0, h1 = halves(PARTS[p][1])
        self.push(p, name, 3, self.source(p, name, 1, 0, h0), 3)

    def begin(self, p, name):
        self.far(p, name)
        self.raw_right(p, name)
        self.raw_left(p, name)

    def add(self, name, mine, others, put):
        def one(*at):
            total = mine[at + (slice(None), slice(None))].astype(jnp.float32)
            for other in others:
                total = total + other[at + (slice(None), slice(None))].astype(jnp.float32)
            put(at, total)

        if name == "a":
            one()
        else:
            pl.loop(0, 4)(lambda i: one(i))

    def onward(self, p, name):
        h0, h1 = halves(PARTS[p][1])
        b = self.buf[p, name]

        def to(ref):
            def put(at, total):
                ref[at + (slice(None), slice(None))] = total.astype(jnp.bfloat16)
            return put

        self.copies[p, name, 0].wait_recv()
        self.add(name, self.source(p, name, 2, 0, h0), [b[0]], to(b[6]))
        self.push(p, name, 4, b[6], 1)
        self.copies[p, name, 1].wait_recv()
        self.add(name, self.source(p, name, 1, h0, h1), [b[1]], to(b[7]))
        self.push(p, name, 5, b[7], 3)

    def end(self, p, name):
        start, size, _ = PARTS[p]
        h0, h1 = halves(size)
        b = self.buf[p, name]
        for number in (3, 2, 4, 5):
            self.copies[p, name, number].wait_recv()
        for lo, n, others in ((0, h0, [b[3], b[4]]), (h0, h1, [b[2], b[5]])):
            def put(at, total, lo=lo, n=n):
                if name == "a":
                    self.out_ref[start + lo:start + lo + n, :] = total
                elif name == "b":
                    self.line[p][at + (pl.ds(lo, n), slice(None))] = total.astype(jnp.bfloat16)
                else:
                    self.rows[p][(int(name[1]),) + at + (pl.ds(lo, n), slice(None))] = total.astype(jnp.bfloat16)
            self.add(name, self.source(p, name, 0, lo, n), others, put)

    def run(self):
        parts = range(3)

        def each(step, name):
            for p in parts:
                step(p, name)

        each(self.begin, "c3")
        each(self.begin, "c1")
        each(self.onward, "c3")
        each(self.begin, "c2")
        each(self.onward, "c1")
        each(self.end, "c3")
        each(self.far, "b")
        each(self.begin, "c0")
        each(self.onward, "c2")
        each(self.end, "c1")
        each(self.raw_left, "b")
        each(self.onward, "c0")
        each(self.end, "c2")
        each(self.raw_right, "b")
        each(self.onward, "b")
        for p in parts:
            self.end(p, "c0")
            self.end(p, "b")
            self.begin(p, "a")
        each(self.onward, "a")
        each(self.end, "a")
        for copy in self.copies.values():
            copy.wait_send()


EPS = 1e-05
ORDER = ("ln1_gain", "ln1_shift", "ln2_gain", "ln2_shift", "b_qkv", "b_out", "b_up", "b_down")


def widen(g_ref, flat, step):
    @pl.loop(0, 16)
    def _(k):
        base = (step * 16 + k) * 433
        flat[pl.ds(base, 440), :] = g_ref[k, 0:440, :].astype(jnp.float32)


def unpack_matrix(flat, first, where, out, size=64):
    offset, rows, blocks = where
    start = offset - first * EIGHTH

    @pl.loop(0, rows // size)
    def _(i):
        for j in range(blocks):
            piece = flat[pl.ds(start + j + i * (size * blocks), size, stride=blocks), :]
            out[pl.ds(pl.multiple_of(i * size, size), size), 128 * j:128 * (j + 1)] = piece.astype(jnp.bfloat16)


def as_row(ref, start, count):
    return jnp.concatenate([ref[start + n:start + n + 1, :] for n in range(count)], 1)


def to_rows(ref, start, row):
    for n in range(row.shape[1] // 128):
        ref[start + n:start + n + 1, :] = row[:, 128 * n:128 * (n + 1)]


def normalized(values):
    center = jnp.mean(values, -1, keepdims=True)
    centered = values - center
    factor = lax.rsqrt(jnp.mean(centered * centered, -1, keepdims=True) + EPS)
    return centered * factor, factor


def turn(x, tables, sign):
    return x * tables[0] + (pltpu.roll(x, 120, 1) * tables[1] + pltpu.roll(x, 8, 1) * tables[2]) * sign


def first_kernel(g_ref, tokens_ref, grad_ref, tables_ref, w_qkv, w_out, blocks_ref, h1t_ref, h2_ref, h2t_ref, vec_ref, flat, wide):
    step = pl.program_id(0)
    widen(g_ref, flat, step)

    @pl.when(step == 1)
    def _():
        unpack_matrix(flat, 0, W_QKV, w_qkv)

    @pl.when(step == 2)
    def _():
        unpack_matrix(flat, 0, W_OUT, w_out)
        vec_ref[0:24, :] = flat[0:24, :]
        start = VECTORS["b_out"][0]
        vec_ref[24:30, :] = flat[start:start + 6, :]
        normal, _ = normalized(tokens_ref[...].astype(jnp.float32))
        h1 = (normal * as_row(flat, 0, 6) + as_row(flat, 6, 6)).astype(jnp.bfloat16)
        h2 = (normal * as_row(flat, 12, 6) + as_row(flat, 18, 6)).astype(jnp.bfloat16)
        h1t_ref[...] = h1.T
        h2_ref[...] = h2
        h2t_ref[...] = h2.T
        for n in range(9):
            start = VECTORS["b_qkv"][0] + 2 * n
            wide[:, 256 * n:256 * (n + 1)] = product(h1, w_qkv[:, 256 * n:256 * (n + 1)]) + as_row(flat, start, 2)
        low = lax.broadcasted_iota(jnp.int32, (128, 128), 1) < 64
        for m in range(6):
            q, k, v = (wide[:, 768 * p + 128 * m:768 * p + 128 * (m + 1)] for p in range(3))
            q = turn(q, tables_ref, 1.0)
            k = turn(k, tables_ref, 1.0)
            a = product(grad_ref[...], w_out[128 * m:128 * (m + 1), :], NT)
            swap = lambda t: pltpu.roll(t, 64, 1)
            blocks_ref[2 * m, 0] = jnp.where(low, q, swap(k)).astype(jnp.bfloat16)
            blocks_ref[2 * m + 1, 0] = jnp.where(low, swap(q), k).astype(jnp.bfloat16)
            blocks_ref[2 * m, 1] = jnp.where(low, v, swap(a)).astype(jnp.bfloat16)
            blocks_ref[2 * m + 1, 1] = jnp.where(low, swap(v), a).astype(jnp.bfloat16)


def const(*shape):
    return pl.BlockSpec(shape, lambda e: (0,) * len(shape))


def first_part(gathered, tokens, grad, tables):
    bf = lambda *s: jax.ShapeDtypeStruct(s, jnp.bfloat16)
    outs = [bf(768, 2304), bf(768, 768), bf(HEADS, 2, 128, 128), bf(768, 128), bf(128, 768), bf(768, 128),
            jax.ShapeDtypeStruct((32, 128), jnp.float32)]
    return pl.pallas_call(
        first_kernel,
        grid=(3,),
        out_shape=outs,
        in_specs=[pl.BlockSpec((16, 448, 128), lambda e: (e, 0, 0)), const(128, 768), const(128, 768), const(3, 128, 128)],
        out_specs=[const(*o.shape) for o in outs],
        scratch_shapes=[pltpu.VMEM((3 * EIGHTH + 16, 128), jnp.float32), pltpu.VMEM((128, 2304), jnp.float32)],
        compiler_params=pltpu.CompilerParams(vmem_limit_bytes=VMEM_LIMIT),
    )(gathered, tokens, grad, tables)


def gelu_pair(u):
    inside = 0.5 * (1.0 + lax.erf(u * 0.7071067811865476))
    return u * inside, inside + u * jnp.exp(-0.5 * u * u) * 0.3989422804014327


class Twin:
    def __init__(self, send, recv):
        self.send, self.recv, self.copies = send, recv, []
        self.pos, self.core = place()

    def push(self, src, dst):
        number = len(self.copies)
        copy = pltpu.make_async_remote_copy(src, dst, self.send.at[number], self.recv.at[number],
                                            device_id=device(self.pos, 1 - self.core), device_id_type=MESH)
        copy.start()
        self.copies.append(copy)
        return copy

    def wait_send(self):
        for copy in self.copies:
            copy.wait_send()


def middle_kernel(g_ref, h2_ref, grad_ref, h2t_ref, blocks_ref,
                  mlp_ref, dh2_ref, bias_ref, up_ref, halves_ref, back_ref,
                  gbuf, flat, w_up, w_down, act, slope, act_pair, h2_pair, g_pair, dup_pair, vec, vec2,
                  heads_in, heads_out, *rest):
    head_scratch, rest = rest[:6], rest[6:]
    there = Exchange(True, blocks_ref, heads_in, *rest[0:3])
    home = Exchange(False, heads_out, back_ref, *rest[3:6])
    twin = Twin(*rest[6:8])
    load, store = rest[8:10]
    core = lax.axis_index("dp_1")
    loads = [pltpu.make_async_copy(g_ref.at[pl.ds(32 + 16 * e, 16)], gbuf.at[pl.ds(16 * (e % 3), 16)], load.at[e]) for e in range(6)]
    for copy in loads[:3]:
        copy.start()
    there.greet()
    there.start()
    h2_pair[:, :128] = h2t_ref[...]
    g_pair[:128, :] = grad_ref[...]
    h2_copy = twin.push(h2_pair.at[:, pl.ds(0, 128)], h2_pair.at[:, pl.ds(128, 128)])
    g_copy = twin.push(g_pair.at[pl.ds(0, 128), :], g_pair.at[pl.ds(128, 128), :])

    def widen(eighth, at):
        @pl.loop(0, 16)
        def _(k):
            flat[pl.ds((at * 16 + k) * 433, 440), :] = gbuf[(eighth - 2) % 3 * 16 + k, 0:440, :].astype(jnp.float32)

    for e in range(4):
        loads[e].wait()
        widen(2 + e, e)
        if e < 3:
            loads[3 + e].start()
    unpack_matrix(flat, 2, W_UP, w_up)
    start = VECTORS["b_up"][0] - 2 * EIGHTH
    for n in range(12):
        at = slice(256 * n, 256 * (n + 1))
        up = product(h2_ref[...], w_up[:, at]) + as_row(flat, start + 2 * n, 2)
        value, slope[:, at] = gelu_pair(up)
        value = value.astype(jnp.bfloat16)
        act[:, at] = value
        act_pair[at, :128] = value.T
    act_copy = twin.push(act_pair.at[:, pl.ds(0, 128)], act_pair.at[:, pl.ds(128, 128)])
    for e in range(3):
        if e:
            loads[3 + e].wait()
        widen(5 + e, e)
    unpack_matrix(flat, 5, W_DOWN, w_down, 128)
    start = VECTORS["b_down"][0] - 5 * EIGHTH
    for n in range(12):
        at = slice(256 * n, 256 * (n + 1))
        dup = (product(grad_ref[...], w_down[at, :], NT) * slope[:, at]).astype(jnp.bfloat16)
        dup_pair[:128, at] = dup
        to_rows(vec, 48 + 2 * n, jnp.sum(dup.astype(jnp.float32), 0, keepdims=True))
    dup_copy = twin.push(dup_pair.at[pl.ds(0, 128), :], dup_pair.at[pl.ds(128, 128), :])
    bias_ref[...] = vec[48:72, :]
    shift = jnp.sum(grad_ref[...].astype(jnp.float32), 0, keepdims=True)
    to_rows(vec, 72, shift)
    vec[78:80, :] = jnp.zeros((2, 128), jnp.float32)
    vec_copy = twin.push(vec.at[pl.ds(48, 32), :], vec2)
    for n in range(3):
        at = slice(256 * n, 256 * (n + 1))
        mlp_ref[:, at] = product(act[...], w_down[:, at]) + as_row(flat, start + 2 * n, 2)
        dh2_ref[:, at] = product(dup_pair[:128, :], w_up[at, :], NT)
    there.wait()
    head_kernel(heads_in, heads_out, *head_scratch[:4], flat, *head_scratch[4:])
    home.start()
    for copy in (h2_copy, g_copy, act_copy, dup_copy, vec_copy):
        copy.wait_recv()
    vec_copy.wait_send()
    vec[48:80, :] = vec[48:80, :] + vec2[...]
    stores = []
    for t in (1, 2, 3):
        for c in range(2):
            if t > 1 or c == 1:
                pl.when(core == c)(
                    lambda number=2 * t + c: weight_eighth(number, ((W_UP, h2_pair, dup_pair), (W_DOWN, act_pair, g_pair)), vec, flat))

        @pl.loop(0, 16)
        def _(k):
            gbuf[16 * (t - 1) + k] = flat[pl.ds(MARGIN + 433 * k, 448), :].astype(jnp.bfloat16)

        copy = pltpu.make_async_copy(gbuf.at[pl.ds(16 * (t - 1), 16)], halves_ref.at[t - 1], store.at[t - 1])
        copy.start()
        stores.append(copy)

    @pl.when(core == 0)
    def _():
        @pl.loop(0, 12)
        def _(j):
            result = product(h2_pair[:96, :], dup_pair[:, pl.ds(pl.multiple_of(j * 256, 256), 256)])
            up_ref[pl.ds(2 * j, 96, stride=24), :] = result[:, :128]
            up_ref[pl.ds(2 * j + 1, 96, stride=24), :] = result[:, 128:]

    home.wait()
    there.wait_send()
    for copy in (h2_copy, g_copy, act_copy, dup_copy):
        copy.wait_send()
    for copy in stores:
        copy.wait()


def middle_part(gathered, h2, grad, h2t, blocks):
    f32 = lambda *s: jax.ShapeDtypeStruct(s, jnp.float32)
    bf = lambda *s: jax.ShapeDtypeStruct(s, jnp.bfloat16)
    vm = lambda *s: pltpu.VMEM(s, jnp.bfloat16)
    vf = lambda *s: pltpu.VMEM(s, jnp.float32)
    anywhere = pl.BlockSpec(memory_space=pl.ANY)
    outs = [f32(128, 768), f32(128, 768), f32(24, 128), f32(2304, 128)]
    dma = pltpu.SemaphoreType.DMA
    return pl.pallas_call(
        middle_kernel,
        grid=(1,),
        out_shape=outs + [bf(3, 16, 448, 128), bf(HEADS, 2, 128, 128)],
        in_specs=[anywhere, const(128, 768), const(128, 768), const(768, 128), anywhere],
        out_specs=[const(*o.shape) for o in outs] + [anywhere, anywhere],
        scratch_shapes=[vm(48, 448, 128), vf(4 * EIGHTH + 16, 128), vm(768, 3072), vm(3072, 768), vm(128, 3072),
                        vf(128, 3072), vm(3072, 256), vm(768, 256), vm(256, 768), vm(256, 3072), vf(80, 128), vf(32, 128),
                        vm(16, 2, 128, 128), vm(16, 2, 128, 128)]
        + HEAD_SCRATCH + Exchange.scratch + Exchange.scratch + [dma((5,)), dma((5,)), dma((6,)), dma((3,))],
        compiler_params=pltpu.CompilerParams(collective_id=2, has_side_effects=True, vmem_limit_bytes=VMEM_LIMIT),
    )(gathered, h2, grad, h2t, blocks)


def last_kernel(back_ref, tokens_ref, grad_ref, tables_ref, w_qkv, w_out, mlp_ref, dh2_ref, bias_ref, in_vec, h1t_ref,
                up_ref, halves_ref, layer_ref, input_ref, own_ref,
                sums, flat, h1_pair, att_pair, dqkv_pair, g_pair, vec, vec2, twin_send, twin_recv, load, *scratch):
    later = pltpu.make_async_copy(halves_ref, sums.at[pl.ds(1, 3)], load)
    later.start()
    scatter = Scatter(sums, own_ref, *scratch)
    greet(scatter.pos, scatter.core)
    twin = Twin(twin_send, twin_recv)
    h1_pair[:, :128] = h1t_ref[...]
    g_pair[:128, :] = grad_ref[...]
    lanes = lambda pair: twin.push(pair.at[:, pl.ds(0, 128)], pair.at[:, pl.ds(128, 128)])
    rows = lambda pair: twin.push(pair.at[pl.ds(0, 128), :], pair.at[pl.ds(128, 128), :])
    lanes(h1_pair)
    rows(g_pair)
    low = lax.broadcasted_iota(jnp.int32, (128, 128), 1) < 64
    swap = lambda t: pltpu.roll(t, 64, 1)
    f32 = lambda t: t.astype(jnp.float32)
    attended = []
    for m in range(6):
        a, b = f32(back_ref[2 * m, 0]), f32(back_ref[2 * m + 1, 0])
        c, d = f32(back_ref[2 * m, 1]), f32(back_ref[2 * m + 1, 1])
        attended.append(jnp.where(low, a, swap(b)).astype(jnp.bfloat16))
        dq = turn(jnp.where(low, swap(a), b), tables_ref, -1.0)
        dk = turn(jnp.where(low, c, swap(d)), tables_ref, -1.0)
        dv = jnp.where(low, swap(c), d)
        for p, part in enumerate((dq, dk, dv)):
            dqkv_pair[:128, 768 * p + 128 * m:768 * p + 128 * (m + 1)] = part.astype(jnp.bfloat16)
    rows(dqkv_pair)
    attended = jnp.concatenate(attended, 1)
    att_pair[:, :128] = attended.T
    lanes(att_pair)
    tokens = f32(tokens_ref[...])
    grad = f32(grad_ref[...])
    normal, factor = normalized(tokens)
    total = grad
    row = 0
    for gain_at, dh in ((0, product(dqkv_pair[:128, :], w_qkv[...], NT)), (12, dh2_ref[...])):
        to_rows(vec, row, jnp.sum(dh * normal, 0, keepdims=True))
        to_rows(vec, row + 6, jnp.sum(dh, 0, keepdims=True))
        row += 12
        scaled = dh * as_row(in_vec, gain_at, 6)
        inner = scaled - jnp.mean(scaled, -1, keepdims=True) - normal * jnp.mean(scaled * normal, -1, keepdims=True)
        total = total + factor * inner
    input_ref[...] = total
    to_rows(vec, 24, jnp.sum(f32(dqkv_pair[:128, :]), 0, keepdims=True))
    shift = jnp.sum(grad, 0, keepdims=True)
    to_rows(vec, 42, shift)
    vec[48:72, :] = bias_ref[...]
    to_rows(vec, 72, shift)
    vec[78:80, :] = jnp.zeros((2, 128), jnp.float32)
    twin.push(vec, vec2)
    layer_ref[...] = (tokens + (product(attended, w_out[...]) + as_row(in_vec, 24, 6)) + mlp_ref[...]).astype(jnp.bfloat16)
    for copy in twin.copies:
        copy.wait_recv()
    twin.copies[-1].wait_send()
    vec[...] = vec[...] + vec2[...]
    pairs = ((W_QKV, h1_pair, dqkv_pair), (W_OUT, att_pair, g_pair))

    def keep(t):
        for z in range(4):
            @pl.loop(0, 4)
            def _(y):
                sums[t, z, y] = flat[pl.ds(MARGIN + 433 * (4 * z + y), 448), :].astype(jnp.bfloat16)

    for c in range(2):
        pl.when(scatter.core == c)(lambda c=c: weight_eighth(c, pairs, vec, flat))
    keep(0)
    later.wait()

    @pl.when(scatter.core == 0)
    def _():
        weight_eighth(2, pairs, vec, flat)
        at = W_UP[0] - 2 * EIGHTH + MARGIN
        flat[at:at + 2304, :] = up_ref[...]
        keep(1)

    scatter.run()
    for copy in twin.copies[:-1]:
        copy.wait_send()


def last_part(*args):
    halves = args[-1].reshape(3, 4, 4, 448, 128)
    bf = lambda *s: jax.ShapeDtypeStruct(s, jnp.bfloat16)
    f32 = lambda *s: jax.ShapeDtypeStruct(s, jnp.float32)
    vm = lambda *s: pltpu.VMEM(s, jnp.bfloat16)
    vf = lambda *s: pltpu.VMEM(s, jnp.float32)
    dma = pltpu.SemaphoreType.DMA
    outs = [bf(128, 768), f32(128, 768), f32(448, 128)]
    return pl.pallas_call(
        last_kernel,
        grid=(1,),
        out_shape=outs,
        in_specs=[const(*a.shape) for a in args[:-1]] + [pl.BlockSpec(memory_space=pl.ANY)],
        out_specs=[const(*o.shape) for o in outs],
        scratch_shapes=[vm(4, 4, 4, 448, 128), vf(EIGHTH + 2 * MARGIN, 128), vm(768, 256), vm(768, 256), vm(256, 2304),
                        vm(256, 768), vf(80, 128), vf(80, 128), dma((5,)), dma((5,)), dma] + Scatter.scratch(),
        compiler_params=pltpu.CompilerParams(collective_id=1, has_side_effects=True, vmem_limit_bytes=VMEM_LIMIT),
    )(*args[:-1], halves)


def rotary_tables(positions):
    lane = jnp.arange(128) % 64
    freq = jnp.tile(10000.0 ** (-jnp.arange(8).astype(jnp.float32) * 2.0 / 16), 16)
    angles = positions.astype(jnp.float32)[:, None] * freq[None, :]
    cosine, sine = jnp.cos(angles), jnp.sin(angles)
    return jnp.stack([jnp.where(lane < 16, cosine, 1.0), jnp.where(lane < 8, -sine, 0.0),
                      jnp.where((lane >= 8) & (lane < 16), sine, 0.0)])


def body(tokens, params, out_grad):
    piece = tokens.shape[1]
    x, grad = tokens[0], out_grad[0]
    own = jnp.pad(params.reshape(433, 128), ((0, ROWS - 433), (0, 0)))
    gathered = gather(own).reshape(128, ROWS, 128)
    tables = rotary_tables(lax.axis_index(SEQ) * piece + jnp.arange(piece))
    w_qkv, w_out, blocks, h1t, h2, h2t, in_vec = first_part(gathered, x, grad, tables)
    mlp, dh2, bias, up_rows, halves_sum, back = middle_part(gathered, h2, grad, h2t, blocks)
    layer_out, input_grad, own_sum = last_part(
        back, x, grad, tables, w_qkv, w_out, mlp, dh2, bias, in_vec, h1t, up_rows, halves_sum
    )
    param_grad = own_sum[:433].reshape(-1)
    return layer_out[None], input_grad[None], param_grad


def solution(mesh):
    finer = Mesh(mesh.devices.reshape(4, 2, 4, 4), DP_SEQ)
    in_specs = (P(DP, SEQ, None), P(DP_SEQ), P(DP, SEQ, None))
    out_specs = (P(DP, SEQ, None), P(DP, SEQ, None), P(DP_SEQ))
    return jax.shard_map(body, mesh=finer, in_specs=in_specs, out_specs=out_specs, check_vma=False)
```

```python
import functools

import jax
import jax.numpy as jnp
from jax import lax
from jax.experimental import pallas as pl
from jax.experimental.pallas import tpu as pltpu
from jax.sharding import Mesh
from jax.sharding import PartitionSpec as P

DP_SEQ = ("dp_0", "dp_1", "seq_0", "seq_1")
SEQ = ("seq_0", "seq_1")
DP = ("dp_0", "dp_1")
VMEM_LIMIT = 60 * 2**20
MESH = pl.DeviceIdType.MESH
ROWS = 448
PARTS = ((0, 144, (0, 2, 1)), (144, 144, (2, 1, 0)), (288, 160, (1, 0, 2)))


def place():
    return [lax.axis_index("dp_0"), lax.axis_index("seq_0"), lax.axis_index("seq_1")], lax.axis_index("dp_1")


def device(pos, core):
    return (pos[0], core, pos[1], pos[2])


def moved(pos, axis, by):
    out = list(pos)
    out[axis] = lax.rem(pos[axis] + by, 4)
    return out


def greet(pos, core, sibling=True):
    barrier = pltpu.get_barrier_semaphore()
    others = [device(moved(pos, a, by), core) for a in range(3) for by in (1, 2, 3)]
    if sibling:
        others.append(device(pos, 1 - core))
    for other in others:
        pl.semaphore_signal(barrier, inc=1, device_id=other, device_id_type=MESH)
    pl.semaphore_wait(barrier, len(others))


class Gather:
    scratch = [pltpu.SemaphoreType.DMA((3, 9, 4)), pltpu.SemaphoreType.DMA((3, 9, 4)),
               pltpu.SemaphoreType.DMA((3, 19)), pltpu.SemaphoreType.DMA((3, 19)), pltpu.SemaphoreType.DMA]
    rings = ("a", "b0", "b1", "b2", "b3", "c0", "c1", "c2", "c3")

    def __init__(self, own_ref, out_ref, send, recv, sib_send, sib_recv, local):
        self.own_ref, self.out_ref, self.local = own_ref, out_ref, local
        self.send_sem, self.recv_sem, self.sib_send, self.sib_recv = send, recv, sib_send, sib_recv
        self.pos, self.core = place()
        self.copies, self.sibs = {}, [[], [], []]

    def near(self, axis):
        q = self.pos[axis]
        return [q] + [lax.rem(q + k, 4) for k in (3, 1, 2)]

    def region(self, where, start, size):
        return self.out_ref.at[where[0], self.core, where[1], where[2], pl.ds(start, size), :]

    def base(self, part, ring):
        a, b, c = PARTS[part][2]
        where = list(self.pos)
        if ring == "a":
            return a, where
        number = int(ring[1])
        if ring[0] == "b":
            where[a] = self.near(a)[number]
            return b, where
        where[a] = slice(None)
        where[b] = self.near(b)[number]
        return c, where

    def at(self, part, ring, which):
        axis, where = self.base(part, ring)
        where[axis] = self.near(axis)[which]
        return where

    def push(self, part, ring, number, which, by, start, size, src=None):
        axis, _ = self.base(part, ring)
        n = self.rings.index(ring)
        ref = self.region(self.at(part, ring, which), start, size)
        copy = pltpu.make_async_remote_copy(
            ref if src is None else src, ref, self.send_sem.at[part, n, number], self.recv_sem.at[part, n, number],
            device_id=device(moved(self.pos, axis, by), self.core), device_id_type=MESH)
        copy.start()
        self.copies[part, ring, number] = copy

    def begin(self, part, ring):
        start, size, _ = PARTS[part]
        src = self.own_ref.at[pl.ds(start, size), :] if ring in ("a", "b0") else None
        self.push(part, ring, 0, 0, 1, start, size, src)
        self.push(part, ring, 1, 0, 3, start, size, src)
        if ring == "a":
            self.push(part, ring, 2, 0, 2, start, size, src)

    def onward(self, part, ring, left=None, right=None):
        start, size, _ = PARTS[part]
        half = size // 32 * 16
        self.copies[part, ring, 0].wait_recv()
        if ring != "a":
            self.push(part, ring, 2, 1, 1, start, half)
        if left:
            left()
        self.copies[part, ring, 1].wait_recv()
        if ring != "a":
            self.push(part, ring, 3, 2, 3, start + half, size - half)
        if right:
            right()

    def end(self, part, ring):
        self.copies[part, ring, 2].wait_recv()
        if ring != "a":
            self.copies[part, ring, 3].wait_recv()

    def sibling(self, part, where, src=None):
        start, size, _ = PARTS[part]
        number = len(self.sibs[part])
        ref = self.region(where, start, size)
        copy = pltpu.make_async_remote_copy(
            ref if src is None else src, ref, self.sib_send.at[part, number], self.sib_recv.at[part, number],
            device_id=device(self.pos, 1 - self.core), device_id_type=MESH)
        copy.start()
        self.sibs[part].append(copy)

    def share(self, part, ring, which):
        return lambda: self.sibling(part, self.at(part, ring, which))

    def row(self, part, number):
        a, b, _ = PARTS[part][2]
        where = list(self.pos)
        where[a] = slice(None)
        where[b] = self.near(b)[number]
        return where

    def run(self):
        parts = range(3)
        own = pltpu.make_async_copy(self.own_ref, self.out_ref.at[self.pos[0], self.core, self.pos[1], self.pos[2]], self.local)
        own.start()
        greet(self.pos, self.core)
        for p in parts:
            self.begin(p, "a")
        for p in parts:
            self.begin(p, "b0")
        for p in parts:
            start, size, _ = PARTS[p]
            self.sibling(p, self.pos, self.own_ref.at[pl.ds(start, size), :])
        own.wait()
        for p in parts:
            def arrived(which, p=p):
                self.begin(p, "b" + str(which))
                self.sibling(p, self.at(p, "a", which))
            self.onward(p, "a", lambda: arrived(1), lambda: arrived(2))
        for p in parts:
            self.onward(p, "b0")
        for p in parts:
            self.end(p, "a")
            self.begin(p, "b3")
            self.begin(p, "c0")
            self.sibling(p, self.at(p, "a", 3))
        for p in parts:
            self.onward(p, "b1")
            self.onward(p, "b2")
        for p in parts:
            self.end(p, "b0")
            self.onward(p, "b3")
            self.begin(p, "c1")
            self.begin(p, "c2")
            self.sibling(p, self.row(p, 1))
            self.sibling(p, self.row(p, 2))
        for p in parts:
            self.onward(p, "c0", self.share(p, "c0", 1), self.share(p, "c0", 2))
        for p in parts:
            for ring in ("b1", "b2", "b3"):
                self.end(p, ring)
            self.begin(p, "c3")
            self.sibling(p, self.row(p, 3))
        for ring in ("c1", "c2", "c3"):
            for p in parts:
                self.onward(p, ring, self.share(p, ring, 1), self.share(p, ring, 2))
            for p in parts:
                before = {"c1": "c0", "c2": "c1", "c3": "c2"}[ring]
                self.end(p, before)
                self.sibling(p, self.at(p, before, 3))
        for p in parts:
            self.end(p, "c3")
            self.sibling(p, self.at(p, "c3", 3))
        for copy in self.copies.values():
            copy.wait_send()
        for copies in self.sibs:
            for copy in copies:
                copy.wait_send()
                copy.wait_recv()


def gather_kernel(params_ref, out_ref, own_ref, *sems):
    own_ref[0:432, :] = params_ref[0:432, :]
    own_ref[432:448, :] = jnp.zeros((16, 128), jnp.bfloat16)
    own_ref[432:433, :] = params_ref[432:433, :]
    Gather(own_ref, out_ref, *sems).run()


def gather(params):
    return pl.pallas_call(
        gather_kernel,
        grid=(1,),
        out_shape=jax.ShapeDtypeStruct((4, 2, 4, 4, ROWS, 128), jnp.bfloat16),
        in_specs=[pl.BlockSpec((433, 128), lambda e: (0, 0))],
        out_specs=pl.BlockSpec(memory_space=pl.ANY),
        scratch_shapes=[pltpu.VMEM((ROWS, 128), jnp.bfloat16)] + Gather.scratch,
        compiler_params=pltpu.CompilerParams(collective_id=0, has_side_effects=True),
    )(params)


EIGHTH = 16 * 433
W_QKV = (24, 768, 18)
W_OUT = (13866, 768, 6)
W_UP = (18480, 768, 24)
W_DOWN = (36936, 3072, 6)
VECTORS = {"ln1_gain": (0, 6), "ln1_shift": (6, 6), "ln2_gain": (12, 6), "ln2_shift": (18, 6),
           "b_qkv": (13848, 18), "b_out": (18474, 6), "b_up": (36912, 24), "b_down": (55368, 6)}


HEADS = 12
TILE = 512
KEYS = 512


class Exchange:
    scratch = [pltpu.SemaphoreType.DMA((16,)), pltpu.SemaphoreType.DMA((16,)), pltpu.SemaphoreType.DMA]

    def __init__(self, to_heads, in_ref, out_ref, send, recv, local):
        self.to_heads, self.in_ref, self.out_ref = to_heads, in_ref, out_ref
        self.send, self.recv, self.local = send, recv, local
        self.x, self.core = lax.axis_index("dp_0"), lax.axis_index("dp_1")
        self.me = lax.axis_index("seq_0") * 4 + lax.axis_index("seq_1")
        self.others = [lax.rem(self.me + k, 16) for k in range(1, 16)]

    def where(self, t):
        return (self.x, self.core, lax.div(t, 4), lax.rem(t, 4))

    def copy(self, t):
        return pltpu.make_async_remote_copy(
            self.in_ref.at[t], self.out_ref.at[self.me], self.send.at[t], self.recv.at[self.me],
            device_id=self.where(t), device_id_type=MESH)

    def arrival(self, t):
        return pltpu.make_async_remote_copy(
            self.out_ref.at[t], self.out_ref.at[t], self.send.at[t], self.recv.at[t],
            device_id=self.where(t), device_id_type=MESH)

    def own(self):
        return pltpu.make_async_copy(self.in_ref.at[self.me], self.out_ref.at[self.me], self.local)

    def greet(self):
        barrier = pltpu.get_barrier_semaphore()
        for t in self.others:
            pl.semaphore_signal(barrier, inc=1, device_id=self.where(t), device_id_type=MESH)
        twin = (self.x, 1 - self.core, lax.div(self.me, 4), lax.rem(self.me, 4))
        pl.semaphore_signal(barrier, inc=1, device_id=twin, device_id_type=MESH)
        pl.semaphore_wait(barrier, 16)

    def start(self):
        if self.to_heads:
            for t in self.others:
                pl.when(t < HEADS)(lambda t=t: self.copy(t).start())
            pl.when(self.me < HEADS)(lambda: self.own().start())
        else:
            @pl.when(self.me < HEADS)
            def _():
                for t in self.others:
                    self.copy(t).start()
                self.own().start()

    def wait(self):
        if self.to_heads:
            @pl.when(self.me < HEADS)
            def _():
                for t in self.others:
                    self.arrival(t).wait_recv()
                self.own().wait()
        else:
            for t in self.others:
                pl.when(t < HEADS)(lambda t=t: self.arrival(t).wait_recv())

            @pl.when(self.me < HEADS)
            def _():
                for t in self.others:
                    self.copy(t).wait_send()
                self.own().wait()

    def wait_send(self):
        for t in self.others:
            pl.when(t < HEADS)(lambda t=t: self.copy(t).wait_send())


NT = (((1,), (1,)), ((), ()))


def product(a, b, dims=(((1,), (0,)), ((), ()))):
    return lax.dot_general(a, b, dims, preferred_element_type=jnp.float32)


def unrolled(low, high, body, carry):
    for j in range(low, high):
        carry = body(j, carry)
    return carry


def head_kernel(in_ref, out_ref, k, v, kt, vt, scores, dk, dv):
    blocks = 2048 // TILE
    per = TILE // 128

    def rows(which, i):
        return jnp.concatenate([in_ref[i * per + p, which] for p in range(per)], 0)

    @pl.loop(0, blocks)
    def _(i):
        at = pl.ds(pl.multiple_of(i * TILE, TILE), TILE)
        key = rows(0, i)[:, 64:]
        value = rows(1, i)[:, :64]
        k[at, :] = key
        v[at, :] = value
        kt[:, at] = key.T
        vt[:, at] = value.T
        dk[at, :] = jnp.zeros((TILE, 64), jnp.float32)
        dv[at, :] = jnp.zeros((TILE, 64), jnp.float32)

    def block(i):
        query = rows(0, i)[:, :64] * jnp.bfloat16(0.125)
        grad = rows(1, i)[:, 64:]

        def tile(j):
            return pl.ds(j * KEYS, KEYS)

        def put(j, s):
            for n in range(TILE // 128):
                scores[pl.ds(j * KEYS + n * 2048, KEYS), :] = s[:, 128 * n:128 * (n + 1)]

        def get(j):
            return jnp.concatenate(
                [scores[pl.ds(j * KEYS + n * 2048, KEYS), :] for n in range(TILE // 128)], 1)

        last = i * TILE // KEYS

        def first(j, top):
            s = product(k[tile(j), :], query, NT)
            put(j, s)
            return jnp.maximum(top, jnp.max(s, 0, keepdims=True))

        top = unrolled(0, last, first, jnp.full((1, TILE), -1e30, jnp.float32))
        s = product(k[tile(last), :], query, NT)
        keep = lax.broadcasted_iota(jnp.int32, (KEYS, TILE), 0) - lax.broadcasted_iota(jnp.int32, (KEYS, TILE), 1) <= i * TILE - last * KEYS
        s = jnp.where(keep, s, -1e30)
        put(last, s)
        top = jnp.maximum(top, jnp.max(s, 0, keepdims=True))

        def second(j, carry):
            total, out = carry
            e = jnp.exp(get(j) - top)
            put(j, e)
            return total + jnp.sum(e, 0, keepdims=True), out + product(vt[:, tile(j)], e.astype(jnp.bfloat16))

        total, out = unrolled(0, last + 1, second, (jnp.zeros((1, TILE), jnp.float32), jnp.zeros((64, TILE), jnp.float32)))
        scale = 1.0 / total
        out = out * scale
        inner = jnp.sum(out * grad.astype(jnp.float32).T, 0, keepdims=True)

        def third(j, dq):
            p = get(j) * scale
            dp = product(v[tile(j), :], grad, NT)
            ds = (p * (dp - inner)).astype(jnp.bfloat16)
            dv[tile(j), :] += product(p.astype(jnp.bfloat16), grad)
            dk[tile(j), :] += product(ds, query)
            return dq + product(kt[:, tile(j)], ds)

        dq = unrolled(0, last + 1, third, jnp.zeros((64, TILE), jnp.float32)) * 0.125
        both = jnp.concatenate([out, dq], 0).T.astype(jnp.bfloat16)
        for p in range(per):
            out_ref[i * per + p, 0] = both[128 * p:128 * (p + 1)]

    for i in range(blocks):
        block(i)

    @pl.loop(0, blocks)
    def _(i):
        at = pl.ds(pl.multiple_of(i * TILE, TILE), TILE)
        both = jnp.concatenate([dk[at, :], dv[at, :]], 1).astype(jnp.bfloat16)
        for p in range(per):
            out_ref[i * per + p, 1] = both[128 * p:128 * (p + 1)]


HEAD_SCRATCH = [pltpu.VMEM((2048, 64), jnp.bfloat16), pltpu.VMEM((2048, 64), jnp.bfloat16),
                pltpu.VMEM((64, 2048), jnp.bfloat16), pltpu.VMEM((64, 2048), jnp.bfloat16),
                pltpu.VMEM((2048, 64), jnp.float32), pltpu.VMEM((2048, 64), jnp.float32)]


MARGIN = 384
CHUNK = 128


def weight_eighth(number, pairs, vec_ref, flat):
    low, high = number * EIGHTH, (number + 1) * EIGHTH
    at = MARGIN - low
    for (offset, rows, blocks), left, right in pairs:
        first = max(0, (low - offset) // blocks) // 16 * 16
        last = min(rows, -(-(high - offset) // blocks))
        last = -(-last // 16) * 16
        if last <= first:
            continue
        size = min(CHUNK, last - first)
        count = -(-(last - first) // size)
        base = offset + at

        @pl.loop(0, count)
        def _(i, first=first, last=last, size=size, blocks=blocks, base=base, left=left, right=right):
            row = pl.multiple_of(jnp.minimum(first + i * size, last - size), 16)
            lhs = left[pl.ds(row, size), :]

            @pl.loop(0, blocks // 2, unroll=3)
            def _(j):
                rhs = right[:, pl.ds(pl.multiple_of(j * 256, 256), 256)]
                result = product(lhs, rhs)
                start = base + row * blocks + 2 * j
                flat[pl.ds(start, size, stride=blocks), :] = result[:, :128]
                flat[pl.ds(start + 1, size, stride=blocks), :] = result[:, 128:]

    row = 0
    for name in ORDER:
        start, count = VECTORS[name]
        lo, hi = max(start, low), min(start + count, high)
        if lo < hi:
            flat[lo + at:hi + at, :] = vec_ref[row + lo - start:row + hi - start, :]
        row += count
    end = 55374
    if high > end:
        flat[end + at:high + at, :] = jnp.zeros((high - end, 128), jnp.float32)


def halves(size):
    half = size // 32 * 16
    return half, size - half


class Scatter:
    names = ("c0", "c1", "c2", "c3", "b", "a")
    @staticmethod
    def scratch():
        out = []
        for _, size, _ in PARTS:
            h0, h1 = halves(size)
            for name in Scatter.names:
                if name == "a":
                    out += [pltpu.VMEM((size, 128), jnp.bfloat16)] * 3
                else:
                    out += [pltpu.VMEM((4, n, 128), jnp.bfloat16) for n in (h0, h1, h1, h0, h0, h1, h0, h1)]
            out += [pltpu.VMEM((4, 4, size, 128), jnp.bfloat16), pltpu.VMEM((4, size, 128), jnp.bfloat16)]
        return out + [pltpu.SemaphoreType.DMA((3, 6, 10)), pltpu.SemaphoreType.DMA((3, 6, 10))]

    def __init__(self, in_ref, out_ref, *scratch):
        self.in_ref, self.out_ref = in_ref, out_ref
        self.send, self.recv = scratch[-2:]
        take = iter(scratch[:-2])
        self.buf, self.rows, self.line = {}, [], []
        for p in range(3):
            for name in self.names:
                self.buf[p, name] = [next(take) for _ in range(3 if name == "a" else 8)]
            self.rows.append(next(take))
            self.line.append(next(take))
        self.pos, self.core = place()
        self.copies = {}

    def near(self, axis):
        q = self.pos[axis]
        return [q] + [lax.rem(q + k, 4) for k in (3, 1, 2)]

    def axis(self, p, name):
        return PARTS[p][2]["abc".index(name[0])]

    def source(self, p, name, which, lo, n):
        a, b, c = PARTS[p][2]
        if name == "a":
            return self.line[p].at[self.near(a)[which], pl.ds(lo, n), :]
        if name == "b":
            return self.rows[p].at[which, :, pl.ds(lo, n), :]
        where = [slice(None)] * 3
        where[b] = self.near(b)[int(name[1])]
        where[c] = self.near(c)[which]
        return self.in_ref.at[where[0], where[1], where[2], pl.ds(PARTS[p][0] + lo, n), :]

    def push(self, p, name, number, src, by, when=None, dst=None, sem=None):
        n = self.names.index(name)
        sem = number if sem is None else sem
        copy = pltpu.make_async_remote_copy(
            src, self.buf[p, name][number] if dst is None else dst, self.send.at[p, n, sem], self.recv.at[p, n, sem],
            device_id=device(moved(self.pos, self.axis(p, name), by), self.core), device_id_type=MESH)
        if when is None:
            copy.start()
        else:
            pl.when(when)(copy.start)
        self.copies.setdefault((p, name, number), []).append(copy)

    def arrived(self, p, name, number):
        for copy in self.copies[p, name, number]:
            copy.wait_recv()

    def sends(self, p):
        h0, h1 = halves(PARTS[p][1])
        return ((0, 3, 0, h0, 1), (1, 3, h0, h1, 3), (2, 2, h0, h1, 1), (3, 1, 0, h0, 3))

    def begin(self, p, name, numbers=(0, 1, 2, 3)):
        for number, which, lo, n, by in self.sends(p):
            if number in numbers:
                self.push(p, name, number, self.source(p, name, which, lo, n), by)

    def ahead(self, name, later):
        for p in range(3):
            a, b, c = PARTS[p][2]
            for number, which, lo, n, by in self.sends(p):
                src = self.source(p, name, which, lo, n)
                if a == 0:
                    part = pl.ds(2 if later else 0, 2)
                    self.push(p, name, number, src.at[part], by, None, self.buf[p, name][number].at[part],
                              number if later else 6 + number)
                    continue
                x = self.near(0)[int(name[1])] if b == 0 else self.near(0)[which]
                if later:
                    self.push(p, name, number, src, by, x >= 2)
                else:
                    pl.when(x < 2)(self.copies[p, name, number][0].start)

    def direct(self, p):
        for number, (which, by) in enumerate(((1, 3), (2, 1), (3, 2))):
            self.push(p, "a", number, self.source(p, "a", which, 0, PARTS[p][1]), by)

    def total(self, p):
        start, size, _ = PARTS[p]
        for number in range(3):
            self.arrived(p, "a", number)
        value = self.source(p, "a", 0, 0, size)[...].astype(jnp.float32)
        for other in self.buf[p, "a"]:
            value = value + other[...].astype(jnp.float32)
        self.out_ref[start:start + size, :] = value

    def add(self, name, mine, others, put):
        def one(*at):
            total = mine[at + (slice(None), slice(None))].astype(jnp.float32)
            for other in others:
                total = total + other[at + (slice(None), slice(None))].astype(jnp.float32)
            put(at, total)

        pl.loop(0, 4)(lambda i: one(i))

    def onward(self, p, name):
        h0, h1 = halves(PARTS[p][1])
        b = self.buf[p, name]

        def to(ref):
            def put(at, total):
                ref[at + (slice(None), slice(None))] = total.astype(jnp.bfloat16)
            return put

        self.arrived(p, name, 0)
        self.add(name, self.source(p, name, 2, 0, h0), [b[0]], to(b[6]))
        self.push(p, name, 4, b[6], 1)
        self.arrived(p, name, 1)
        self.add(name, self.source(p, name, 1, h0, h1), [b[1]], to(b[7]))
        self.push(p, name, 5, b[7], 3)

    def end(self, p, name):
        h0, h1 = halves(PARTS[p][1])
        b = self.buf[p, name]
        for number in (3, 2, 4, 5):
            self.arrived(p, name, number)
        for lo, n, others in ((0, h0, [b[3], b[4]]), (h0, h1, [b[2], b[5]])):
            def put(at, total, lo=lo, n=n):
                if name == "b":
                    self.line[p][at + (pl.ds(lo, n), slice(None))] = total.astype(jnp.bfloat16)
                else:
                    self.rows[p][(int(name[1]),) + at + (pl.ds(lo, n), slice(None))] = total.astype(jnp.bfloat16)
            self.add(name, self.source(p, name, 0, lo, n), others, put)

    def before(self):
        for name in ("c3", "c1", "c2", "c0"):
            self.ahead(name, True)

    def run(self):
        parts = range(3)

        def each(step, name, *more):
            for p in parts:
                step(p, name, *more)

        self.ahead("c3", False)
        self.ahead("c1", False)
        each(self.onward, "c3")
        self.ahead("c2", False)
        each(self.onward, "c1")
        each(self.end, "c3")
        each(self.begin, "b", (0, 1))
        self.ahead("c0", False)
        each(self.onward, "c2")
        each(self.end, "c1")
        each(self.begin, "b", (3,))
        each(self.onward, "c0")
        each(self.end, "c2")
        each(self.begin, "b", (2,))
        each(self.onward, "b")
        for p in parts:
            self.end(p, "c0")
            self.end(p, "b")
            self.direct(p)
        for p in parts:
            self.total(p)
        for copies in self.copies.values():
            for copy in copies:
                copy.wait_send()


EPS = 1e-05
ORDER = ("ln1_gain", "ln1_shift", "ln2_gain", "ln2_shift", "b_qkv", "b_out", "b_up", "b_down")


def widen(g_ref, flat, step):
    @pl.loop(0, 16)
    def _(k):
        base = (step * 16 + k) * 433
        flat[pl.ds(base, 440), :] = g_ref[k, 0:440, :].astype(jnp.float32)


def unpack_matrix(flat, first, where, out, size=64):
    offset, rows, blocks = where
    start = offset - first * EIGHTH

    @pl.loop(0, rows // size)
    def _(i):
        for j in range(blocks):
            piece = flat[pl.ds(start + j + i * (size * blocks), size, stride=blocks), :]
            out[pl.ds(pl.multiple_of(i * size, size), size), 128 * j:128 * (j + 1)] = piece.astype(jnp.bfloat16)


def as_row(ref, start, count):
    return jnp.concatenate([ref[start + n:start + n + 1, :] for n in range(count)], 1)


def to_rows(ref, start, row):
    for n in range(row.shape[1] // 128):
        ref[start + n:start + n + 1, :] = row[:, 128 * n:128 * (n + 1)]


def normalized(values):
    center = jnp.mean(values, -1, keepdims=True)
    centered = values - center
    factor = lax.rsqrt(jnp.mean(centered * centered, -1, keepdims=True) + EPS)
    return centered * factor, factor


def turn(x, tables, sign):
    return x * tables[0] + (pltpu.roll(x, 120, 1) * tables[1] + pltpu.roll(x, 8, 1) * tables[2]) * sign


def first_kernel(g_ref, tokens_ref, grad_ref, tables_ref, w_qkv, w_out, blocks_ref, h1t_ref, h2_ref, h2t_ref, vec_ref, flat, wide):
    step = pl.program_id(0)
    widen(g_ref, flat, step)

    @pl.when(step == 1)
    def _():
        unpack_matrix(flat, 0, W_QKV, w_qkv)

    @pl.when(step == 2)
    def _():
        unpack_matrix(flat, 0, W_OUT, w_out)
        vec_ref[0:24, :] = flat[0:24, :]
        start = VECTORS["b_out"][0]
        vec_ref[24:30, :] = flat[start:start + 6, :]
        normal, _ = normalized(tokens_ref[...].astype(jnp.float32))
        h1 = (normal * as_row(flat, 0, 6) + as_row(flat, 6, 6)).astype(jnp.bfloat16)
        h2 = (normal * as_row(flat, 12, 6) + as_row(flat, 18, 6)).astype(jnp.bfloat16)
        h1t_ref[...] = h1.T
        h2_ref[...] = h2
        h2t_ref[...] = h2.T
        for n in range(9):
            start = VECTORS["b_qkv"][0] + 2 * n
            wide[:, 256 * n:256 * (n + 1)] = product(h1, w_qkv[:, 256 * n:256 * (n + 1)]) + as_row(flat, start, 2)
        low = lax.broadcasted_iota(jnp.int32, (128, 128), 1) < 64
        for m in range(6):
            q, k, v = (wide[:, 768 * p + 128 * m:768 * p + 128 * (m + 1)] for p in range(3))
            q = turn(q, tables_ref, 1.0)
            k = turn(k, tables_ref, 1.0)
            a = product(grad_ref[...], w_out[128 * m:128 * (m + 1), :], NT)
            swap = lambda t: pltpu.roll(t, 64, 1)
            blocks_ref[2 * m, 0] = jnp.where(low, q, swap(k)).astype(jnp.bfloat16)
            blocks_ref[2 * m + 1, 0] = jnp.where(low, swap(q), k).astype(jnp.bfloat16)
            blocks_ref[2 * m, 1] = jnp.where(low, v, swap(a)).astype(jnp.bfloat16)
            blocks_ref[2 * m + 1, 1] = jnp.where(low, swap(v), a).astype(jnp.bfloat16)


def const(*shape):
    return pl.BlockSpec(shape, lambda e: (0,) * len(shape))


def first_part(gathered, tokens, grad, tables):
    bf = lambda *s: jax.ShapeDtypeStruct(s, jnp.bfloat16)
    outs = [bf(768, 2304), bf(768, 768), bf(HEADS, 2, 128, 128), bf(768, 128), bf(128, 768), bf(768, 128),
            jax.ShapeDtypeStruct((32, 128), jnp.float32)]
    return pl.pallas_call(
        first_kernel,
        grid=(3,),
        out_shape=outs,
        in_specs=[pl.BlockSpec((16, 448, 128), lambda e: (e, 0, 0)), const(128, 768), const(128, 768), const(3, 128, 128)],
        out_specs=[const(*o.shape) for o in outs],
        scratch_shapes=[pltpu.VMEM((3 * EIGHTH + 16, 128), jnp.float32), pltpu.VMEM((128, 2304), jnp.float32)],
        compiler_params=pltpu.CompilerParams(vmem_limit_bytes=VMEM_LIMIT),
    )(gathered, tokens, grad, tables)


def gelu_pair(u):
    inside = 0.5 * (1.0 + lax.erf(u * 0.7071067811865476))
    return u * inside, inside + u * jnp.exp(-0.5 * u * u) * 0.3989422804014327


class Twin:
    def __init__(self, send, recv):
        self.send, self.recv, self.copies = send, recv, []
        self.pos, self.core = place()

    def push(self, src, dst):
        number = len(self.copies)
        copy = pltpu.make_async_remote_copy(src, dst, self.send.at[number], self.recv.at[number],
                                            device_id=device(self.pos, 1 - self.core), device_id_type=MESH)
        copy.start()
        self.copies.append(copy)
        return copy

    def wait_send(self):
        for copy in self.copies:
            copy.wait_send()


def middle_kernel(g_ref, h2_ref, grad_ref, h2t_ref, blocks_ref,
                  mlp_ref, dh2_ref, bias_ref, up_ref, halves_ref, back_ref,
                  gbuf, flat, w_up, w_down, act, slope, act_pair, h2_pair, g_pair, dup_pair, vec, vec2,
                  heads_in, heads_out, *rest):
    head_scratch, rest = rest[:6], rest[6:]
    there = Exchange(True, blocks_ref, heads_in, *rest[0:3])
    home = Exchange(False, heads_out, back_ref, *rest[3:6])
    twin = Twin(*rest[6:8])
    load, store = rest[8:10]
    core = lax.axis_index("dp_1")
    loads = [pltpu.make_async_copy(g_ref.at[pl.ds(32 + 16 * e, 16)], gbuf.at[pl.ds(16 * (e % 3), 16)], load.at[e]) for e in range(6)]
    for copy in loads[:3]:
        copy.start()
    there.greet()
    there.start()
    h2_pair[:, :128] = h2t_ref[...]
    g_pair[:128, :] = grad_ref[...]
    h2_copy = twin.push(h2_pair.at[:, pl.ds(0, 128)], h2_pair.at[:, pl.ds(128, 128)])
    g_copy = twin.push(g_pair.at[pl.ds(0, 128), :], g_pair.at[pl.ds(128, 128), :])

    def widen(eighth, at):
        @pl.loop(0, 16)
        def _(k):
            flat[pl.ds((at * 16 + k) * 433, 440), :] = gbuf[(eighth - 2) % 3 * 16 + k, 0:440, :].astype(jnp.float32)

    for e in range(4):
        loads[e].wait()
        widen(2 + e, e)
        if e < 3:
            loads[3 + e].start()
    unpack_matrix(flat, 2, W_UP, w_up)
    start = VECTORS["b_up"][0] - 2 * EIGHTH
    for n in range(12):
        at = slice(256 * n, 256 * (n + 1))
        up = product(h2_ref[...], w_up[:, at]) + as_row(flat, start + 2 * n, 2)
        value, slope[:, at] = gelu_pair(up)
        value = value.astype(jnp.bfloat16)
        act[:, at] = value
        act_pair[at, :128] = value.T
    act_copy = twin.push(act_pair.at[:, pl.ds(0, 128)], act_pair.at[:, pl.ds(128, 128)])
    for e in range(3):
        if e:
            loads[3 + e].wait()
        widen(5 + e, e)
    unpack_matrix(flat, 5, W_DOWN, w_down, 128)
    start = VECTORS["b_down"][0] - 5 * EIGHTH
    for n in range(12):
        at = slice(256 * n, 256 * (n + 1))
        dup = (product(grad_ref[...], w_down[at, :], NT) * slope[:, at]).astype(jnp.bfloat16)
        dup_pair[:128, at] = dup
        to_rows(vec, 48 + 2 * n, jnp.sum(dup.astype(jnp.float32), 0, keepdims=True))
    dup_copy = twin.push(dup_pair.at[pl.ds(0, 128), :], dup_pair.at[pl.ds(128, 128), :])
    bias_ref[...] = vec[48:72, :]
    shift = jnp.sum(grad_ref[...].astype(jnp.float32), 0, keepdims=True)
    to_rows(vec, 72, shift)
    vec[78:80, :] = jnp.zeros((2, 128), jnp.float32)
    vec_copy = twin.push(vec.at[pl.ds(48, 32), :], vec2)
    for n in range(3):
        at = slice(256 * n, 256 * (n + 1))
        mlp_ref[:, at] = product(act[...], w_down[:, at]) + as_row(flat, start + 2 * n, 2)
        dh2_ref[:, at] = product(dup_pair[:128, :], w_up[at, :], NT)
    there.wait()
    head_kernel(heads_in, heads_out, *head_scratch[:4], flat, *head_scratch[4:])
    home.start()
    for copy in (h2_copy, g_copy, act_copy, dup_copy, vec_copy):
        copy.wait_recv()
    vec_copy.wait_send()
    vec[48:80, :] = vec[48:80, :] + vec2[...]
    stores = []
    for t in (1, 2, 3):
        for c in range(2):
            if t > 1 or c == 1:
                pl.when(core == c)(
                    lambda number=2 * t + c: weight_eighth(number, ((W_UP, h2_pair, dup_pair), (W_DOWN, act_pair, g_pair)), vec, flat))

        @pl.loop(0, 16)
        def _(k):
            gbuf[16 * (t - 1) + k] = flat[pl.ds(MARGIN + 433 * k, 448), :].astype(jnp.bfloat16)

        copy = pltpu.make_async_copy(gbuf.at[pl.ds(16 * (t - 1), 16)], halves_ref.at[t - 1], store.at[t - 1])
        copy.start()
        stores.append(copy)

    @pl.when(core == 0)
    def _():
        @pl.loop(0, 12)
        def _(j):
            result = product(h2_pair[:96, :], dup_pair[:, pl.ds(pl.multiple_of(j * 256, 256), 256)])
            up_ref[pl.ds(2 * j, 96, stride=24), :] = result[:, :128]
            up_ref[pl.ds(2 * j + 1, 96, stride=24), :] = result[:, 128:]

    home.wait()
    there.wait_send()
    for copy in (h2_copy, g_copy, act_copy, dup_copy):
        copy.wait_send()
    for copy in stores:
        copy.wait()


def middle_part(gathered, h2, grad, h2t, blocks):
    f32 = lambda *s: jax.ShapeDtypeStruct(s, jnp.float32)
    bf = lambda *s: jax.ShapeDtypeStruct(s, jnp.bfloat16)
    vm = lambda *s: pltpu.VMEM(s, jnp.bfloat16)
    vf = lambda *s: pltpu.VMEM(s, jnp.float32)
    anywhere = pl.BlockSpec(memory_space=pl.ANY)
    outs = [f32(128, 768), f32(128, 768), f32(24, 128), f32(2304, 128)]
    dma = pltpu.SemaphoreType.DMA
    return pl.pallas_call(
        middle_kernel,
        grid=(1,),
        out_shape=outs + [bf(3, 16, 448, 128), bf(HEADS, 2, 128, 128)],
        in_specs=[anywhere, const(128, 768), const(128, 768), const(768, 128), anywhere],
        out_specs=[const(*o.shape) for o in outs] + [anywhere, anywhere],
        scratch_shapes=[vm(48, 448, 128), vf(4 * EIGHTH + 16, 128), vm(768, 3072), vm(3072, 768), vm(128, 3072),
                        vf(128, 3072), vm(3072, 256), vm(768, 256), vm(256, 768), vm(256, 3072), vf(80, 128), vf(32, 128),
                        vm(16, 2, 128, 128), vm(16, 2, 128, 128)]
        + HEAD_SCRATCH + Exchange.scratch + Exchange.scratch + [dma((5,)), dma((5,)), dma((6,)), dma((3,))],
        compiler_params=pltpu.CompilerParams(collective_id=2, has_side_effects=True, vmem_limit_bytes=VMEM_LIMIT),
    )(gathered, h2, grad, h2t, blocks)


def last_kernel(back_ref, tokens_ref, grad_ref, tables_ref, w_qkv, w_out, mlp_ref, dh2_ref, bias_ref, in_vec, h1t_ref,
                up_ref, halves_ref, layer_ref, input_ref, own_ref,
                sums, flat, h1_pair, att_pair, dqkv_pair, g_pair, vec, vec2, twin_send, twin_recv, load, *scratch):
    later = pltpu.make_async_copy(halves_ref, sums.at[pl.ds(1, 3)], load)
    later.start()
    scatter = Scatter(sums, own_ref, *scratch)
    greet(scatter.pos, scatter.core)
    twin = Twin(twin_send, twin_recv)
    h1_pair[:, :128] = h1t_ref[...]
    g_pair[:128, :] = grad_ref[...]
    lanes = lambda pair: twin.push(pair.at[:, pl.ds(0, 128)], pair.at[:, pl.ds(128, 128)])
    rows = lambda pair: twin.push(pair.at[pl.ds(0, 128), :], pair.at[pl.ds(128, 128), :])
    lanes(h1_pair)
    rows(g_pair)
    later.wait()
    scatter.before()
    low = lax.broadcasted_iota(jnp.int32, (128, 128), 1) < 64
    swap = lambda t: pltpu.roll(t, 64, 1)
    f32 = lambda t: t.astype(jnp.float32)
    attended = []
    for m in range(6):
        a, b = f32(back_ref[2 * m, 0]), f32(back_ref[2 * m + 1, 0])
        c, d = f32(back_ref[2 * m, 1]), f32(back_ref[2 * m + 1, 1])
        attended.append(jnp.where(low, a, swap(b)).astype(jnp.bfloat16))
        dq = turn(jnp.where(low, swap(a), b), tables_ref, -1.0)
        dk = turn(jnp.where(low, c, swap(d)), tables_ref, -1.0)
        dv = jnp.where(low, swap(c), d)
        for p, part in enumerate((dq, dk, dv)):
            dqkv_pair[:128, 768 * p + 128 * m:768 * p + 128 * (m + 1)] = part.astype(jnp.bfloat16)
    rows(dqkv_pair)
    attended = jnp.concatenate(attended, 1)
    att_pair[:, :128] = attended.T
    lanes(att_pair)
    tokens = f32(tokens_ref[...])
    grad = f32(grad_ref[...])
    normal, factor = normalized(tokens)
    total = grad
    row = 0
    for gain_at, dh in ((0, product(dqkv_pair[:128, :], w_qkv[...], NT)), (12, dh2_ref[...])):
        to_rows(vec, row, jnp.sum(dh * normal, 0, keepdims=True))
        to_rows(vec, row + 6, jnp.sum(dh, 0, keepdims=True))
        row += 12
        scaled = dh * as_row(in_vec, gain_at, 6)
        inner = scaled - jnp.mean(scaled, -1, keepdims=True) - normal * jnp.mean(scaled * normal, -1, keepdims=True)
        total = total + factor * inner
    input_ref[...] = total
    to_rows(vec, 24, jnp.sum(f32(dqkv_pair[:128, :]), 0, keepdims=True))
    shift = jnp.sum(grad, 0, keepdims=True)
    to_rows(vec, 42, shift)
    vec[48:72, :] = bias_ref[...]
    to_rows(vec, 72, shift)
    vec[78:80, :] = jnp.zeros((2, 128), jnp.float32)
    twin.push(vec, vec2)
    layer_ref[...] = (tokens + (product(attended, w_out[...]) + as_row(in_vec, 24, 6)) + mlp_ref[...]).astype(jnp.bfloat16)
    for copy in twin.copies:
        copy.wait_recv()
    twin.copies[-1].wait_send()
    vec[...] = vec[...] + vec2[...]
    pairs = ((W_QKV, h1_pair, dqkv_pair), (W_OUT, att_pair, g_pair))

    def keep(t):
        for z in range(4):
            @pl.loop(0, 4)
            def _(y):
                sums[t, z, y] = flat[pl.ds(MARGIN + 433 * (4 * z + y), 448), :].astype(jnp.bfloat16)

    for c in range(2):
        pl.when(scatter.core == c)(lambda c=c: weight_eighth(c, pairs, vec, flat))
    keep(0)

    @pl.when(scatter.core == 0)
    def _():
        weight_eighth(2, pairs, vec, flat)
        at = W_UP[0] - 2 * EIGHTH + MARGIN
        flat[at:at + 2304, :] = up_ref[...]
        keep(1)

    scatter.run()
    for copy in twin.copies[:-1]:
        copy.wait_send()


def last_part(*args):
    halves = args[-1].reshape(3, 4, 4, 448, 128)
    bf = lambda *s: jax.ShapeDtypeStruct(s, jnp.bfloat16)
    f32 = lambda *s: jax.ShapeDtypeStruct(s, jnp.float32)
    vm = lambda *s: pltpu.VMEM(s, jnp.bfloat16)
    vf = lambda *s: pltpu.VMEM(s, jnp.float32)
    dma = pltpu.SemaphoreType.DMA
    outs = [bf(128, 768), f32(128, 768), f32(448, 128)]
    return pl.pallas_call(
        last_kernel,
        grid=(1,),
        out_shape=outs,
        in_specs=[const(*a.shape) for a in args[:-1]] + [pl.BlockSpec(memory_space=pl.ANY)],
        out_specs=[const(*o.shape) for o in outs],
        scratch_shapes=[vm(4, 4, 4, 448, 128), vf(EIGHTH + 2 * MARGIN, 128), vm(768, 256), vm(768, 256), vm(256, 2304),
                        vm(256, 768), vf(80, 128), vf(80, 128), dma((5,)), dma((5,)), dma] + Scatter.scratch(),
        compiler_params=pltpu.CompilerParams(collective_id=1, has_side_effects=True, vmem_limit_bytes=VMEM_LIMIT),
    )(*args[:-1], halves)


def finish_kernel(layer_in, input_in, own_in, layer_ref, input_ref, own_ref):
    layer_ref[...] = layer_in[...]
    input_ref[...] = input_in[...]
    own_ref[...] = own_in[:433, :]


def finish(*args):
    shapes = [(128, 768), (128, 768), (433, 128)]
    return pl.pallas_call(
        finish_kernel,
        grid=(1,),
        out_shape=[jax.ShapeDtypeStruct(s, a.dtype) for s, a in zip(shapes, args)],
        in_specs=[const(*a.shape) for a in args],
        out_specs=[const(*s) for s in shapes],
    )(*args)


def rotary_tables(positions):
    lane = jnp.arange(128) % 64
    freq = jnp.tile(10000.0 ** (-jnp.arange(8).astype(jnp.float32) * 2.0 / 16), 16)
    angles = positions.astype(jnp.float32)[:, None] * freq[None, :]
    cosine, sine = jnp.cos(angles), jnp.sin(angles)
    return jnp.stack([jnp.where(lane < 16, cosine, 1.0), jnp.where(lane < 8, -sine, 0.0),
                      jnp.where((lane >= 8) & (lane < 16), sine, 0.0)])


def body(tokens, params, out_grad):
    piece = tokens.shape[1]
    x, grad = tokens[0], out_grad[0]
    gathered = gather(params.reshape(433, 128)).reshape(128, ROWS, 128)
    tables = rotary_tables(lax.axis_index(SEQ) * piece + jnp.arange(piece))
    w_qkv, w_out, blocks, h1t, h2, h2t, in_vec = first_part(gathered, x, grad, tables)
    mlp, dh2, bias, up_rows, halves_sum, back = middle_part(gathered, h2, grad, h2t, blocks)
    results = last_part(back, x, grad, tables, w_qkv, w_out, mlp, dh2, bias, in_vec, h1t, up_rows, halves_sum)
    layer_out, input_grad, own_sum = finish(*results)
    param_grad = own_sum.reshape(-1)
    return layer_out[None], input_grad[None], param_grad


def solution(mesh):
    finer = Mesh(mesh.devices.reshape(4, 2, 4, 4), DP_SEQ)
    in_specs = (P(DP, SEQ, None), P(DP_SEQ), P(DP, SEQ, None))
    out_specs = (P(DP, SEQ, None), P(DP, SEQ, None), P(DP_SEQ))
    return jax.shard_map(body, mesh=finer, in_specs=in_specs, out_specs=out_specs, check_vma=False)
```

```python
import functools

import jax
import jax.numpy as jnp
from jax import lax
from jax.experimental import pallas as pl
from jax.experimental.pallas import tpu as pltpu
from jax.sharding import Mesh
from jax.sharding import PartitionSpec as P

DP_SEQ = ("dp_0", "dp_1", "seq_0", "seq_1")
SEQ = ("seq_0", "seq_1")
DP = ("dp_0", "dp_1")
VMEM_LIMIT = 60 * 2**20
MESH = pl.DeviceIdType.MESH
ROWS = 448
PARTS = ((0, 144, (0, 2, 1)), (144, 144, (2, 1, 0)), (288, 160, (1, 0, 2)))


def place():
    return [lax.axis_index("dp_0"), lax.axis_index("seq_0"), lax.axis_index("seq_1")], lax.axis_index("dp_1")


def device(pos, core):
    return (pos[0], core, pos[1], pos[2])


def moved(pos, axis, by):
    out = list(pos)
    out[axis] = lax.rem(pos[axis] + by, 4)
    return out


def greet(pos, core, sibling=True):
    barrier = pltpu.get_barrier_semaphore()
    others = [device(moved(pos, a, by), core) for a in range(3) for by in (1, 2, 3)]
    if sibling:
        others.append(device(pos, 1 - core))
    for other in others:
        pl.semaphore_signal(barrier, inc=1, device_id=other, device_id_type=MESH)
    pl.semaphore_wait(barrier, len(others))


class Gather:
    scratch = [pltpu.SemaphoreType.DMA((3, 9, 4)), pltpu.SemaphoreType.DMA((3, 9, 4)),
               pltpu.SemaphoreType.DMA((3, 19)), pltpu.SemaphoreType.DMA((3, 19)), pltpu.SemaphoreType.DMA]
    rings = ("a", "b0", "b1", "b2", "b3", "c0", "c1", "c2", "c3")

    def __init__(self, own_ref, out_ref, send, recv, sib_send, sib_recv, local):
        self.own_ref, self.out_ref, self.local = own_ref, out_ref, local
        self.send_sem, self.recv_sem, self.sib_send, self.sib_recv = send, recv, sib_send, sib_recv
        self.pos, self.core = place()
        self.copies, self.sibs = {}, [[], [], []]

    def near(self, axis):
        q = self.pos[axis]
        return [q] + [lax.rem(q + k, 4) for k in (3, 1, 2)]

    def region(self, where, start, size):
        return self.out_ref.at[where[0], self.core, where[1], where[2], pl.ds(start, size), :]

    def base(self, part, ring):
        a, b, c = PARTS[part][2]
        where = list(self.pos)
        if ring == "a":
            return a, where
        number = int(ring[1])
        if ring[0] == "b":
            where[a] = self.near(a)[number]
            return b, where
        where[a] = slice(None)
        where[b] = self.near(b)[number]
        return c, where

    def at(self, part, ring, which):
        axis, where = self.base(part, ring)
        where[axis] = self.near(axis)[which]
        return where

    def push(self, part, ring, number, which, by, start, size, src=None):
        axis, _ = self.base(part, ring)
        n = self.rings.index(ring)
        ref = self.region(self.at(part, ring, which), start, size)
        copy = pltpu.make_async_remote_copy(
            ref if src is None else src, ref, self.send_sem.at[part, n, number], self.recv_sem.at[part, n, number],
            device_id=device(moved(self.pos, axis, by), self.core), device_id_type=MESH)
        copy.start()
        self.copies[part, ring, number] = copy

    def begin(self, part, ring):
        start, size, _ = PARTS[part]
        src = self.own_ref.at[pl.ds(start, size), :] if ring in ("a", "b0") else None
        self.push(part, ring, 0, 0, 1, start, size, src)
        self.push(part, ring, 1, 0, 3, start, size, src)
        if ring == "a":
            self.push(part, ring, 2, 0, 2, start, size, src)

    def onward(self, part, ring, left=None, right=None):
        start, size, _ = PARTS[part]
        half = size // 32 * 16
        self.copies[part, ring, 0].wait_recv()
        if ring != "a":
            self.push(part, ring, 2, 1, 1, start, half)
        if left:
            left()
        self.copies[part, ring, 1].wait_recv()
        if ring != "a":
            self.push(part, ring, 3, 2, 3, start + half, size - half)
        if right:
            right()

    def end(self, part, ring):
        self.copies[part, ring, 2].wait_recv()
        if ring != "a":
            self.copies[part, ring, 3].wait_recv()

    def sibling(self, part, where, src=None):
        start, size, _ = PARTS[part]
        number = len(self.sibs[part])
        ref = self.region(where, start, size)
        copy = pltpu.make_async_remote_copy(
            ref if src is None else src, ref, self.sib_send.at[part, number], self.sib_recv.at[part, number],
            device_id=device(self.pos, 1 - self.core), device_id_type=MESH)
        copy.start()
        self.sibs[part].append(copy)

    def share(self, part, ring, which):
        return lambda: self.sibling(part, self.at(part, ring, which))

    def row(self, part, number):
        a, b, _ = PARTS[part][2]
        where = list(self.pos)
        where[a] = slice(None)
        where[b] = self.near(b)[number]
        return where

    def run(self):
        parts = range(3)
        own = pltpu.make_async_copy(self.own_ref, self.out_ref.at[self.pos[0], self.core, self.pos[1], self.pos[2]], self.local)
        own.start()
        greet(self.pos, self.core)
        for p in parts:
            self.begin(p, "a")
        for p in parts:
            self.begin(p, "b0")
        for p in parts:
            start, size, _ = PARTS[p]
            self.sibling(p, self.pos, self.own_ref.at[pl.ds(start, size), :])
        own.wait()
        for p in parts:
            def arrived(which, p=p):
                self.begin(p, "b" + str(which))
                self.sibling(p, self.at(p, "a", which))
            self.onward(p, "a", lambda: arrived(1), lambda: arrived(2))
        for p in parts:
            self.onward(p, "b0")
        for p in parts:
            self.end(p, "a")
            self.begin(p, "b3")
            self.begin(p, "c0")
            self.sibling(p, self.at(p, "a", 3))
        for p in parts:
            self.onward(p, "b1")
            self.onward(p, "b2")
        for p in parts:
            self.end(p, "b0")
            self.onward(p, "b3")
            self.begin(p, "c1")
            self.begin(p, "c2")
            self.sibling(p, self.row(p, 1))
            self.sibling(p, self.row(p, 2))
        for p in parts:
            self.onward(p, "c0", self.share(p, "c0", 1), self.share(p, "c0", 2))
        for p in parts:
            for ring in ("b1", "b2", "b3"):
                self.end(p, ring)
            self.begin(p, "c3")
            self.sibling(p, self.row(p, 3))
        for ring in ("c1", "c2", "c3"):
            for p in parts:
                self.onward(p, ring, self.share(p, ring, 1), self.share(p, ring, 2))
            for p in parts:
                before = {"c1": "c0", "c2": "c1", "c3": "c2"}[ring]
                self.end(p, before)
                self.sibling(p, self.at(p, before, 3))
        for p in parts:
            self.end(p, "c3")
            self.sibling(p, self.at(p, "c3", 3))
        for copy in self.copies.values():
            copy.wait_send()
        for copies in self.sibs:
            for copy in copies:
                copy.wait_send()
                copy.wait_recv()


def gather_kernel(params_ref, out_ref, own_ref, *sems):
    own_ref[0:432, :] = params_ref[0:432, :]
    own_ref[432:448, :] = jnp.zeros((16, 128), jnp.bfloat16)
    own_ref[432:433, :] = params_ref[432:433, :]
    Gather(own_ref, out_ref, *sems).run()


def gather(params):
    return pl.pallas_call(
        gather_kernel,
        grid=(1,),
        out_shape=jax.ShapeDtypeStruct((4, 2, 4, 4, ROWS, 128), jnp.bfloat16),
        in_specs=[pl.BlockSpec((433, 128), lambda e: (0, 0))],
        out_specs=pl.BlockSpec(memory_space=pl.ANY),
        scratch_shapes=[pltpu.VMEM((ROWS, 128), jnp.bfloat16)] + Gather.scratch,
        compiler_params=pltpu.CompilerParams(collective_id=0, has_side_effects=True),
    )(params)


EIGHTH = 16 * 433
W_QKV = (24, 768, 18)
W_OUT = (13866, 768, 6)
W_UP = (18480, 768, 24)
W_DOWN = (36936, 3072, 6)
VECTORS = {"ln1_gain": (0, 6), "ln1_shift": (6, 6), "ln2_gain": (12, 6), "ln2_shift": (18, 6),
           "b_qkv": (13848, 18), "b_out": (18474, 6), "b_up": (36912, 24), "b_down": (55368, 6)}


HEADS = 12
TILE = 512
KEYS = 512


class Exchange:
    scratch = [pltpu.SemaphoreType.DMA((16,)), pltpu.SemaphoreType.DMA((16,)), pltpu.SemaphoreType.DMA]

    def __init__(self, to_heads, in_ref, out_ref, send, recv, local):
        self.to_heads, self.in_ref, self.out_ref = to_heads, in_ref, out_ref
        self.send, self.recv, self.local = send, recv, local
        self.x, self.core = lax.axis_index("dp_0"), lax.axis_index("dp_1")
        self.me = lax.axis_index("seq_0") * 4 + lax.axis_index("seq_1")
        self.others = [lax.rem(self.me + k, 16) for k in range(1, 16)]

    def where(self, t):
        return (self.x, self.core, lax.div(t, 4), lax.rem(t, 4))

    def copy(self, t):
        return pltpu.make_async_remote_copy(
            self.in_ref.at[t], self.out_ref.at[self.me], self.send.at[t], self.recv.at[self.me],
            device_id=self.where(t), device_id_type=MESH)

    def arrival(self, t):
        return pltpu.make_async_remote_copy(
            self.out_ref.at[t], self.out_ref.at[t], self.send.at[t], self.recv.at[t],
            device_id=self.where(t), device_id_type=MESH)

    def own(self):
        return pltpu.make_async_copy(self.in_ref.at[self.me], self.out_ref.at[self.me], self.local)

    def hello(self):
        barrier = pltpu.get_barrier_semaphore()
        for t in self.others:
            pl.semaphore_signal(barrier, inc=1, device_id=self.where(t), device_id_type=MESH)
        twin = (self.x, 1 - self.core, lax.div(self.me, 4), lax.rem(self.me, 4))
        pl.semaphore_signal(barrier, inc=1, device_id=twin, device_id_type=MESH)

    def meet(self):
        pl.semaphore_wait(pltpu.get_barrier_semaphore(), 16)

    def start(self):
        if self.to_heads:
            for t in self.others:
                pl.when(t < HEADS)(lambda t=t: self.copy(t).start())
            pl.when(self.me < HEADS)(lambda: self.own().start())
        else:
            @pl.when(self.me < HEADS)
            def _():
                for t in self.others:
                    self.copy(t).start()
                self.own().start()

    def wait(self):
        if self.to_heads:
            @pl.when(self.me < HEADS)
            def _():
                for t in self.others:
                    self.arrival(t).wait_recv()
                self.own().wait()
        else:
            for t in self.others:
                pl.when(t < HEADS)(lambda t=t: self.arrival(t).wait_recv())

            @pl.when(self.me < HEADS)
            def _():
                for t in self.others:
                    self.copy(t).wait_send()
                self.own().wait()

    def wait_send(self):
        for t in self.others:
            pl.when(t < HEADS)(lambda t=t: self.copy(t).wait_send())


NT = (((1,), (1,)), ((), ()))


def product(a, b, dims=(((1,), (0,)), ((), ()))):
    return lax.dot_general(a, b, dims, preferred_element_type=jnp.float32)


def unrolled(low, high, body, carry):
    for j in range(low, high):
        carry = body(j, carry)
    return carry


def head_kernel(in_ref, out_ref, k, v, kt, vt, scores, dk, dv):
    blocks = 2048 // TILE
    per = TILE // 128

    def rows(which, i):
        return jnp.concatenate([in_ref[i * per + p, which] for p in range(per)], 0)

    @pl.loop(0, blocks)
    def _(i):
        at = pl.ds(pl.multiple_of(i * TILE, TILE), TILE)
        key = rows(0, i)[:, 64:]
        value = rows(1, i)[:, :64]
        k[at, :] = key
        v[at, :] = value
        kt[:, at] = key.T
        vt[:, at] = value.T
        dk[at, :] = jnp.zeros((TILE, 64), jnp.float32)
        dv[at, :] = jnp.zeros((TILE, 64), jnp.float32)

    def block(i):
        query = rows(0, i)[:, :64] * jnp.bfloat16(0.125)
        grad = rows(1, i)[:, 64:]

        def tile(j):
            return pl.ds(j * KEYS, KEYS)

        def put(j, s):
            for n in range(TILE // 128):
                scores[pl.ds(j * KEYS + n * 2048, KEYS), :] = s[:, 128 * n:128 * (n + 1)]

        def get(j):
            return jnp.concatenate(
                [scores[pl.ds(j * KEYS + n * 2048, KEYS), :] for n in range(TILE // 128)], 1)

        last = i * TILE // KEYS

        def first(j, top):
            s = product(k[tile(j), :], query, NT)
            put(j, s)
            return jnp.maximum(top, jnp.max(s, 0, keepdims=True))

        top = unrolled(0, last, first, jnp.full((1, TILE), -1e30, jnp.float32))
        s = product(k[tile(last), :], query, NT)
        keep = lax.broadcasted_iota(jnp.int32, (KEYS, TILE), 0) - lax.broadcasted_iota(jnp.int32, (KEYS, TILE), 1) <= i * TILE - last * KEYS
        s = jnp.where(keep, s, -1e30)
        put(last, s)
        top = jnp.maximum(top, jnp.max(s, 0, keepdims=True))

        def second(j, carry):
            total, out = carry
            e = jnp.exp(get(j) - top)
            put(j, e)
            return total + jnp.sum(e, 0, keepdims=True), out + product(vt[:, tile(j)], e.astype(jnp.bfloat16))

        total, out = unrolled(0, last + 1, second, (jnp.zeros((1, TILE), jnp.float32), jnp.zeros((64, TILE), jnp.float32)))
        scale = 1.0 / total
        out = out * scale
        inner = jnp.sum(out * grad.astype(jnp.float32).T, 0, keepdims=True)

        def third(j, dq):
            p = get(j) * scale
            dp = product(v[tile(j), :], grad, NT)
            ds = (p * (dp - inner)).astype(jnp.bfloat16)
            dv[tile(j), :] += product(p.astype(jnp.bfloat16), grad)
            dk[tile(j), :] += product(ds, query)
            return dq + product(kt[:, tile(j)], ds)

        dq = unrolled(0, last + 1, third, jnp.zeros((64, TILE), jnp.float32)) * 0.125
        both = jnp.concatenate([out, dq], 0).T.astype(jnp.bfloat16)
        for p in range(per):
            out_ref[i * per + p, 0] = both[128 * p:128 * (p + 1)]

    for i in range(blocks):
        block(i)

    @pl.loop(0, blocks)
    def _(i):
        at = pl.ds(pl.multiple_of(i * TILE, TILE), TILE)
        both = jnp.concatenate([dk[at, :], dv[at, :]], 1).astype(jnp.bfloat16)
        for p in range(per):
            out_ref[i * per + p, 1] = both[128 * p:128 * (p + 1)]


HEAD_SCRATCH = [pltpu.VMEM((2048, 64), jnp.bfloat16), pltpu.VMEM((2048, 64), jnp.bfloat16),
                pltpu.VMEM((64, 2048), jnp.bfloat16), pltpu.VMEM((64, 2048), jnp.bfloat16),
                pltpu.VMEM((2048, 64), jnp.float32), pltpu.VMEM((2048, 64), jnp.float32)]


MARGIN = 384
CHUNK = 128


def weight_eighth(number, pairs, vec_ref, flat):
    low, high = number * EIGHTH, (number + 1) * EIGHTH
    at = MARGIN - low
    for (offset, rows, blocks), left, right in pairs:
        first = max(0, (low - offset) // blocks) // 16 * 16
        last = min(rows, -(-(high - offset) // blocks))
        last = -(-last // 16) * 16
        if last <= first:
            continue
        size = min(CHUNK, last - first)
        count = -(-(last - first) // size)
        base = offset + at

        @pl.loop(0, count)
        def _(i, first=first, last=last, size=size, blocks=blocks, base=base, left=left, right=right):
            row = pl.multiple_of(jnp.minimum(first + i * size, last - size), 16)
            lhs = left[pl.ds(row, size), :]

            @pl.loop(0, blocks // 2, unroll=3)
            def _(j):
                rhs = right[:, pl.ds(pl.multiple_of(j * 256, 256), 256)]
                result = product(lhs, rhs)
                start = base + row * blocks + 2 * j
                flat[pl.ds(start, size, stride=blocks), :] = result[:, :128]
                flat[pl.ds(start + 1, size, stride=blocks), :] = result[:, 128:]

    row = 0
    for name in ORDER:
        start, count = VECTORS[name]
        lo, hi = max(start, low), min(start + count, high)
        if lo < hi:
            flat[lo + at:hi + at, :] = vec_ref[row + lo - start:row + hi - start, :]
        row += count
    end = 55374
    if high > end:
        flat[end + at:high + at, :] = jnp.zeros((high - end, 128), jnp.float32)


def halves(size):
    half = size // 32 * 16
    return half, size - half


class Scatter:
    names = ("c0", "c1", "c2", "c3", "b", "a")
    @staticmethod
    def scratch():
        out = []
        for _, size, _ in PARTS:
            h0, h1 = halves(size)
            for name in Scatter.names:
                if name == "a":
                    out += [pltpu.VMEM((size, 128), jnp.bfloat16)] * 3
                else:
                    out += [pltpu.VMEM((4, n, 128), jnp.bfloat16) for n in (h0, h1, h1, h0, h0, h1, h0, h1)]
            out += [pltpu.VMEM((4, 4, size, 128), jnp.bfloat16), pltpu.VMEM((4, size, 128), jnp.bfloat16)]
        return out + [pltpu.SemaphoreType.DMA((3, 6, 10)), pltpu.SemaphoreType.DMA((3, 6, 10))]

    def __init__(self, in_ref, out_ref, *scratch):
        self.in_ref, self.out_ref = in_ref, out_ref
        self.send, self.recv = scratch[-2:]
        take = iter(scratch[:-2])
        self.buf, self.rows, self.line = {}, [], []
        for p in range(3):
            for name in self.names:
                self.buf[p, name] = [next(take) for _ in range(3 if name == "a" else 8)]
            self.rows.append(next(take))
            self.line.append(next(take))
        self.pos, self.core = place()
        self.copies = {}

    def near(self, axis):
        q = self.pos[axis]
        return [q] + [lax.rem(q + k, 4) for k in (3, 1, 2)]

    def axis(self, p, name):
        return PARTS[p][2]["abc".index(name[0])]

    def source(self, p, name, which, lo, n):
        a, b, c = PARTS[p][2]
        if name == "a":
            return self.line[p].at[self.near(a)[which], pl.ds(lo, n), :]
        if name == "b":
            return self.rows[p].at[which, :, pl.ds(lo, n), :]
        where = [slice(None)] * 3
        where[b] = self.near(b)[int(name[1])]
        where[c] = self.near(c)[which]
        return self.in_ref.at[where[0], where[1], where[2], pl.ds(PARTS[p][0] + lo, n), :]

    def push(self, p, name, number, src, by, when=None, dst=None, sem=None):
        n = self.names.index(name)
        sem = number if sem is None else sem
        copy = pltpu.make_async_remote_copy(
            src, self.buf[p, name][number] if dst is None else dst, self.send.at[p, n, sem], self.recv.at[p, n, sem],
            device_id=device(moved(self.pos, self.axis(p, name), by), self.core), device_id_type=MESH)
        if when is None:
            copy.start()
        else:
            pl.when(when)(copy.start)
        self.copies.setdefault((p, name, number), []).append(copy)

    def arrived(self, p, name, number):
        for copy in self.copies[p, name, number]:
            copy.wait_recv()

    def sends(self, p):
        h0, h1 = halves(PARTS[p][1])
        return ((0, 3, 0, h0, 1), (1, 3, h0, h1, 3), (2, 2, h0, h1, 1), (3, 1, 0, h0, 3))

    def begin(self, p, name, numbers=(0, 1, 2, 3)):
        for number, which, lo, n, by in self.sends(p):
            if number in numbers:
                self.push(p, name, number, self.source(p, name, which, lo, n), by)

    def ahead(self, name, later):
        for p in range(3):
            a, b, c = PARTS[p][2]
            for number, which, lo, n, by in self.sends(p):
                src = self.source(p, name, which, lo, n)
                if a == 0:
                    part = pl.ds(2 if later else 0, 2)
                    self.push(p, name, number, src.at[part], by, None, self.buf[p, name][number].at[part],
                              number if later else 6 + number)
                    continue
                x = self.near(0)[int(name[1])] if b == 0 else self.near(0)[which]
                if later:
                    self.push(p, name, number, src, by, x >= 2)
                else:
                    pl.when(x < 2)(self.copies[p, name, number][0].start)

    def direct(self, p):
        for number, (which, by) in enumerate(((1, 3), (2, 1), (3, 2))):
            self.push(p, "a", number, self.source(p, "a", which, 0, PARTS[p][1]), by)

    def total(self, p):
        start, size, _ = PARTS[p]
        for number in range(3):
            self.arrived(p, "a", number)
        value = self.source(p, "a", 0, 0, size)[...].astype(jnp.float32)
        for other in self.buf[p, "a"]:
            value = value + other[...].astype(jnp.float32)
        self.out_ref[start:start + size, :] = value

    def add(self, name, mine, others, put):
        def one(*at):
            total = mine[at + (slice(None), slice(None))].astype(jnp.float32)
            for other in others:
                total = total + other[at + (slice(None), slice(None))].astype(jnp.float32)
            put(at, total)

        pl.loop(0, 4)(lambda i: one(i))

    def onward(self, p, name):
        h0, h1 = halves(PARTS[p][1])
        b = self.buf[p, name]

        def to(ref):
            def put(at, total):
                ref[at + (slice(None), slice(None))] = total.astype(jnp.bfloat16)
            return put

        self.arrived(p, name, 0)
        self.add(name, self.source(p, name, 2, 0, h0), [b[0]], to(b[6]))
        self.push(p, name, 4, b[6], 1)
        self.arrived(p, name, 1)
        self.add(name, self.source(p, name, 1, h0, h1), [b[1]], to(b[7]))
        self.push(p, name, 5, b[7], 3)

    def end(self, p, name):
        h0, h1 = halves(PARTS[p][1])
        b = self.buf[p, name]
        for number in (3, 2, 4, 5):
            self.arrived(p, name, number)
        for lo, n, others in ((0, h0, [b[3], b[4]]), (h0, h1, [b[2], b[5]])):
            def put(at, total, lo=lo, n=n):
                if name == "b":
                    self.line[p][at + (pl.ds(lo, n), slice(None))] = total.astype(jnp.bfloat16)
                else:
                    self.rows[p][(int(name[1]),) + at + (pl.ds(lo, n), slice(None))] = total.astype(jnp.bfloat16)
            self.add(name, self.source(p, name, 0, lo, n), others, put)

    def before(self):
        for name in ("c3", "c1", "c2", "c0"):
            self.ahead(name, True)

    def run(self, meanwhile):
        parts = range(3)

        def each(step, name, *more):
            for p in parts:
                step(p, name, *more)

        self.ahead("c3", False)
        self.ahead("c1", False)
        meanwhile()
        each(self.onward, "c3")
        self.ahead("c2", False)
        each(self.onward, "c1")
        each(self.end, "c3")
        each(self.begin, "b", (0, 1))
        self.ahead("c0", False)
        each(self.onward, "c2")
        each(self.end, "c1")
        each(self.begin, "b", (3,))
        each(self.onward, "c0")
        each(self.end, "c2")
        each(self.begin, "b", (2,))
        each(self.onward, "b")
        for p in parts:
            self.end(p, "c0")
            self.end(p, "b")
            self.direct(p)
        for p in parts:
            self.total(p)
        for copies in self.copies.values():
            for copy in copies:
                copy.wait_send()


EPS = 1e-05
ORDER = ("ln1_gain", "ln1_shift", "ln2_gain", "ln2_shift", "b_qkv", "b_out", "b_up", "b_down")


def widen(g_ref, flat, step):
    @pl.loop(0, 16)
    def _(k):
        base = (step * 16 + k) * 433
        flat[pl.ds(base, 440), :] = g_ref[k, 0:440, :].astype(jnp.float32)


def unpack_matrix(flat, first, where, out, size=64):
    offset, rows, blocks = where
    start = offset - first * EIGHTH

    @pl.loop(0, rows // size)
    def _(i):
        for j in range(blocks):
            piece = flat[pl.ds(start + j + i * (size * blocks), size, stride=blocks), :]
            out[pl.ds(pl.multiple_of(i * size, size), size), 128 * j:128 * (j + 1)] = piece.astype(jnp.bfloat16)


def as_row(ref, start, count):
    return jnp.concatenate([ref[start + n:start + n + 1, :] for n in range(count)], 1)


def to_rows(ref, start, row):
    for n in range(row.shape[1] // 128):
        ref[start + n:start + n + 1, :] = row[:, 128 * n:128 * (n + 1)]


def normalized(values):
    center = jnp.mean(values, -1, keepdims=True)
    centered = values - center
    factor = lax.rsqrt(jnp.mean(centered * centered, -1, keepdims=True) + EPS)
    return centered * factor, factor


def turn(x, tables, sign):
    return x * tables[0] + (pltpu.roll(x, 120, 1) * tables[1] + pltpu.roll(x, 8, 1) * tables[2]) * sign


def const(*shape):
    return pl.BlockSpec(shape, lambda e: (0,) * len(shape))


def gelu_pair(u):
    inside = 0.5 * (1.0 + lax.erf(u * 0.7071067811865476))
    return u * inside, inside + u * jnp.exp(-0.5 * u * u) * 0.3989422804014327


class Twin:
    def __init__(self, send, recv):
        self.send, self.recv, self.copies = send, recv, []
        self.pos, self.core = place()

    def push(self, src, dst):
        number = len(self.copies)
        copy = pltpu.make_async_remote_copy(src, dst, self.send.at[number], self.recv.at[number],
                                            device_id=device(self.pos, 1 - self.core), device_id_type=MESH)
        copy.start()
        self.copies.append(copy)
        return copy

    def wait_send(self):
        for copy in self.copies:
            copy.wait_send()


def middle_kernel(g_ref, tokens_ref, grad_ref, tables_ref,
                  mlp_ref, dh2_ref, bias_ref, h1t_ref, vec_ref, up_ref, halves_ref, back_ref, w_qkv_ref, w_out_ref,
                  gbuf, flat, w_up, w_down, act, slope, act_pair, h2_pair, g_pair, dup_pair, vec, vec2,
                  heads_in, heads_out, w_qkv, w_out, wide, blocks, *rest):
    head_scratch, rest = rest[:6], rest[6:]
    there = Exchange(True, blocks, heads_in, *rest[0:3])
    home = Exchange(False, heads_out, back_ref, *rest[3:6])
    twin = Twin(*rest[6:8])
    load, store = rest[8:10]
    core = lax.axis_index("dp_1")
    there.hello()
    loads = [pltpu.make_async_copy(g_ref.at[pl.ds(16 * e, 16)], gbuf.at[pl.ds(e % 3 * 16, 16)], load.at[e]) for e in range(8)]
    for copy in loads[:3]:
        copy.start()
    stores = []

    def keep(src, dst):
        copy = pltpu.make_async_copy(src, dst, store.at[len(stores)])
        copy.start()
        stores.append(copy)

    def widen(eighth, at):
        @pl.loop(0, 16)
        def _(k):
            flat[pl.ds((at * 16 + k) * 433, 440), :] = gbuf[eighth % 3 * 16 + k, 0:440, :].astype(jnp.float32)

    for e in range(2):
        loads[e].wait()
        widen(e, e)
        loads[3 + e].start()
    unpack_matrix(flat, 0, W_QKV, w_qkv)
    keep(w_qkv, w_qkv_ref)
    loads[2].wait()
    widen(2, 2)
    unpack_matrix(flat, 0, W_OUT, w_out)
    keep(w_out, w_out_ref)
    vec_ref[0:24, :] = flat[0:24, :]
    start = VECTORS["b_out"][0]
    vec_ref[24:30, :] = flat[start:start + 6, :]
    normal, _ = normalized(tokens_ref[...].astype(jnp.float32))
    h1 = (normal * as_row(flat, 0, 6) + as_row(flat, 6, 6)).astype(jnp.bfloat16)
    h2 = (normal * as_row(flat, 12, 6) + as_row(flat, 18, 6)).astype(jnp.bfloat16)
    h1t_ref[...] = h1.T
    for n in range(9):
        start = VECTORS["b_qkv"][0] + 2 * n
        qkv = product(h1, w_qkv[:, 256 * n:256 * (n + 1)]) + as_row(flat, start, 2)
        wide[256 * n:256 * n + 128, :] = qkv[:, :128]
        wide[256 * n + 128:256 * (n + 1), :] = qkv[:, 128:]
    low = lax.broadcasted_iota(jnp.int32, (128, 128), 1) < 64
    swap = lambda t: pltpu.roll(t, 64, 1)
    for m in range(6):
        q, k, v = (wide[128 * (6 * p + m):128 * (6 * p + m + 1), :] for p in range(3))
        q = turn(q, tables_ref, 1.0)
        k = turn(k, tables_ref, 1.0)
        a = product(grad_ref[...], w_out[128 * m:128 * (m + 1), :], NT)
        blocks[2 * m, 0] = jnp.where(low, q, swap(k)).astype(jnp.bfloat16)
        blocks[2 * m + 1, 0] = jnp.where(low, swap(q), k).astype(jnp.bfloat16)
        blocks[2 * m, 1] = jnp.where(low, v, swap(a)).astype(jnp.bfloat16)
        blocks[2 * m + 1, 1] = jnp.where(low, swap(v), a).astype(jnp.bfloat16)
    there.meet()
    there.start()
    h2_pair[:, :128] = h2.T
    g_pair[:128, :] = grad_ref[...]
    h2_copy = twin.push(h2_pair.at[:, pl.ds(0, 128)], h2_pair.at[:, pl.ds(128, 128)])
    g_copy = twin.push(g_pair.at[pl.ds(0, 128), :], g_pair.at[pl.ds(128, 128), :])
    for e in range(2, 6):
        if e > 2:
            loads[e].wait()
        widen(e, e - 2)
        if e < 5:
            loads[3 + e].start()
    unpack_matrix(flat, 2, W_UP, w_up)
    start = VECTORS["b_up"][0] - 2 * EIGHTH
    for n in range(12):
        at = slice(256 * n, 256 * (n + 1))
        up = product(h2, w_up[:, at]) + as_row(flat, start + 2 * n, 2)
        value, slope[:, at] = gelu_pair(up)
        value = value.astype(jnp.bfloat16)
        act[:, at] = value
        act_pair[at, :128] = value.T
    act_copy = twin.push(act_pair.at[:, pl.ds(0, 128)], act_pair.at[:, pl.ds(128, 128)])
    for e in range(3):
        if e:
            loads[5 + e].wait()
        widen(5 + e, e)
    unpack_matrix(flat, 5, W_DOWN, w_down, 128)
    start = VECTORS["b_down"][0] - 5 * EIGHTH
    for n in range(12):
        at = slice(256 * n, 256 * (n + 1))
        dup = (product(grad_ref[...], w_down[at, :], NT) * slope[:, at]).astype(jnp.bfloat16)
        dup_pair[:128, at] = dup
        to_rows(vec, 48 + 2 * n, jnp.sum(dup.astype(jnp.float32), 0, keepdims=True))
    dup_copy = twin.push(dup_pair.at[pl.ds(0, 128), :], dup_pair.at[pl.ds(128, 128), :])
    bias_ref[...] = vec[48:72, :]
    shift = jnp.sum(grad_ref[...].astype(jnp.float32), 0, keepdims=True)
    to_rows(vec, 72, shift)
    vec[78:80, :] = jnp.zeros((2, 128), jnp.float32)
    vec_copy = twin.push(vec.at[pl.ds(48, 32), :], vec2)
    for n in range(3):
        at = slice(256 * n, 256 * (n + 1))
        mlp_ref[:, at] = product(act[...], w_down[:, at]) + as_row(flat, start + 2 * n, 2)
        dh2_ref[:, at] = product(dup_pair[:128, :], w_up[at, :], NT)
    there.wait()
    head_kernel(heads_in, heads_out, *head_scratch[:4], flat, *head_scratch[4:])
    home.start()
    for copy in (h2_copy, g_copy, act_copy, dup_copy, vec_copy):
        copy.wait_recv()
    vec_copy.wait_send()
    vec[48:80, :] = vec[48:80, :] + vec2[...]
    for t in (1, 2, 3):
        for c in range(2):
            if t > 1 or c == 1:
                pl.when(core == c)(
                    lambda number=2 * t + c: weight_eighth(number, ((W_UP, h2_pair, dup_pair), (W_DOWN, act_pair, g_pair)), vec, flat))

        @pl.loop(0, 16)
        def _(k):
            gbuf[16 * (t - 1) + k] = flat[pl.ds(MARGIN + 433 * k, 448), :].astype(jnp.bfloat16)

        keep(gbuf.at[pl.ds(16 * (t - 1), 16)], halves_ref.at[t - 1])

    @pl.when(core == 0)
    def _():
        @pl.loop(0, 12)
        def _(j):
            result = product(h2_pair[:96, :], dup_pair[:, pl.ds(pl.multiple_of(j * 256, 256), 256)])
            wide[pl.ds(2 * j, 96, stride=24), :] = result[:, :128]
            wide[pl.ds(2 * j + 1, 96, stride=24), :] = result[:, 128:]

    keep(wide, up_ref)

    home.wait()
    there.wait_send()
    for copy in (h2_copy, g_copy, act_copy, dup_copy):
        copy.wait_send()
    for copy in stores:
        copy.wait()


def middle_part(gathered, tokens, grad, tables):
    f32 = lambda *s: jax.ShapeDtypeStruct(s, jnp.float32)
    bf = lambda *s: jax.ShapeDtypeStruct(s, jnp.bfloat16)
    vm = lambda *s: pltpu.VMEM(s, jnp.bfloat16)
    vf = lambda *s: pltpu.VMEM(s, jnp.float32)
    anywhere = pl.BlockSpec(memory_space=pl.ANY)
    outs = [f32(128, 768), f32(128, 768), f32(24, 128), bf(768, 128), f32(32, 128)]
    far = [f32(2304, 128), bf(3, 16, 448, 128), bf(HEADS, 2, 128, 128), bf(768, 2304), bf(768, 768)]
    dma = pltpu.SemaphoreType.DMA
    return pl.pallas_call(
        middle_kernel,
        grid=(1,),
        out_shape=outs + far,
        in_specs=[anywhere, const(128, 768), const(128, 768), const(3, 128, 128)],
        out_specs=[const(*o.shape) for o in outs] + [anywhere] * len(far),
        scratch_shapes=[vm(48, 448, 128), vf(4 * EIGHTH + 16, 128), vm(768, 3072), vm(3072, 768), vm(128, 3072),
                        vf(128, 3072), vm(3072, 256), vm(768, 256), vm(256, 768), vm(256, 3072), vf(80, 128), vf(32, 128),
                        vm(16, 2, 128, 128), vm(16, 2, 128, 128), vm(768, 2304), vm(768, 768), vf(2304, 128),
                        vm(HEADS, 2, 128, 128)]
        + HEAD_SCRATCH + Exchange.scratch + Exchange.scratch + [dma((5,)), dma((5,)), dma((8,)), dma((6,))],
        compiler_params=pltpu.CompilerParams(collective_id=2, has_side_effects=True, vmem_limit_bytes=VMEM_LIMIT),
    )(gathered, tokens, grad, tables)


def last_kernel(back_ref, tokens_ref, grad_ref, tables_ref, mlp_ref, dh2_ref, bias_ref, in_vec, h1t_ref,
                w_qkv_ref, w_out_ref, up_in, halves_ref, layer_ref, input_ref, own_ref,
                sums, flat, h1_pair, att_pair, dqkv_pair, g_pair, vec, vec2, w_qkv, w_out, up_ref, twin_send, twin_recv, load, *scratch):
    pairs = ((halves_ref, sums.at[pl.ds(1, 3)]), (w_qkv_ref, w_qkv), (w_out_ref, w_out), (up_in, up_ref))
    later, qkv_load, out_load, up_load = (pltpu.make_async_copy(a, b, load.at[n]) for n, (a, b) in enumerate(pairs))
    for copy in (later, qkv_load, out_load, up_load):
        copy.start()
    scatter = Scatter(sums, own_ref, *scratch)
    greet(scatter.pos, scatter.core)
    twin = Twin(twin_send, twin_recv)
    h1_pair[:, :128] = h1t_ref[...]
    g_pair[:128, :] = grad_ref[...]
    lanes = lambda pair: twin.push(pair.at[:, pl.ds(0, 128)], pair.at[:, pl.ds(128, 128)])
    rows = lambda pair: twin.push(pair.at[pl.ds(0, 128), :], pair.at[pl.ds(128, 128), :])
    lanes(h1_pair)
    rows(g_pair)
    later.wait()
    scatter.before()
    low = lax.broadcasted_iota(jnp.int32, (128, 128), 1) < 64
    swap = lambda t: pltpu.roll(t, 64, 1)
    f32 = lambda t: t.astype(jnp.float32)
    attended = []
    for m in range(6):
        a, b = f32(back_ref[2 * m, 0]), f32(back_ref[2 * m + 1, 0])
        c, d = f32(back_ref[2 * m, 1]), f32(back_ref[2 * m + 1, 1])
        attended.append(jnp.where(low, a, swap(b)).astype(jnp.bfloat16))
        dq = turn(jnp.where(low, swap(a), b), tables_ref, -1.0)
        dk = turn(jnp.where(low, c, swap(d)), tables_ref, -1.0)
        dv = jnp.where(low, swap(c), d)
        for p, part in enumerate((dq, dk, dv)):
            dqkv_pair[:128, 768 * p + 128 * m:768 * p + 128 * (m + 1)] = part.astype(jnp.bfloat16)
    rows(dqkv_pair)
    attended = jnp.concatenate(attended, 1)
    att_pair[:, :128] = attended.T
    lanes(att_pair)
    tokens = f32(tokens_ref[...])
    grad = f32(grad_ref[...])
    normal, factor = normalized(tokens)
    qkv_load.wait()
    input_ref[...] = product(dqkv_pair[:128, :], w_qkv[...], NT)
    for row, dh in ((0, input_ref), (12, dh2_ref)):
        to_rows(vec, row, jnp.sum(dh[...] * normal, 0, keepdims=True))
        to_rows(vec, row + 6, jnp.sum(dh[...], 0, keepdims=True))
    to_rows(vec, 24, jnp.sum(f32(dqkv_pair[:128, :]), 0, keepdims=True))
    shift = jnp.sum(grad, 0, keepdims=True)
    to_rows(vec, 42, shift)
    vec[48:72, :] = bias_ref[...]
    to_rows(vec, 72, shift)
    vec[78:80, :] = jnp.zeros((2, 128), jnp.float32)
    twin.push(vec, vec2)
    out_load.wait()
    up_load.wait()

    def results():
        tokens = f32(tokens_ref[...])
        branch = lax.dot_general(att_pair[:, :128], w_out[...], (((0,), (0,)), ((), ())), preferred_element_type=jnp.float32)
        layer_ref[...] = (tokens + (branch + as_row(in_vec, 24, 6)) + mlp_ref[...]).astype(jnp.bfloat16)
        normal, factor = normalized(tokens)
        total = f32(grad_ref[...])
        for gain_at, dh in ((0, input_ref), (12, dh2_ref)):
            scaled = dh[...] * as_row(in_vec, gain_at, 6)
            inner = scaled - jnp.mean(scaled, -1, keepdims=True) - normal * jnp.mean(scaled * normal, -1, keepdims=True)
            total = total + factor * inner
        input_ref[...] = total

    for copy in twin.copies:
        copy.wait_recv()
    twin.copies[-1].wait_send()
    vec[...] = vec[...] + vec2[...]
    pairs = ((W_QKV, h1_pair, dqkv_pair), (W_OUT, att_pair, g_pair))

    def keep(t):
        for z in range(4):
            @pl.loop(0, 4)
            def _(y):
                sums[t, z, y] = flat[pl.ds(MARGIN + 433 * (4 * z + y), 448), :].astype(jnp.bfloat16)

    for c in range(2):
        pl.when(scatter.core == c)(lambda c=c: weight_eighth(c, pairs, vec, flat))
    keep(0)

    @pl.when(scatter.core == 0)
    def _():
        weight_eighth(2, pairs, vec, flat)
        at = W_UP[0] - 2 * EIGHTH + MARGIN
        flat[at:at + 2304, :] = up_ref[...]
        keep(1)

    scatter.run(results)
    for copy in twin.copies[:-1]:
        copy.wait_send()


def last_part(*args):
    halves = args[-1].reshape(3, 4, 4, 448, 128)
    bf = lambda *s: jax.ShapeDtypeStruct(s, jnp.bfloat16)
    f32 = lambda *s: jax.ShapeDtypeStruct(s, jnp.float32)
    vm = lambda *s: pltpu.VMEM(s, jnp.bfloat16)
    vf = lambda *s: pltpu.VMEM(s, jnp.float32)
    dma = pltpu.SemaphoreType.DMA
    outs = [bf(128, 768), f32(128, 768), f32(448, 128)]
    return pl.pallas_call(
        last_kernel,
        grid=(1,),
        out_shape=outs,
        in_specs=[const(*a.shape) for a in args[:-4]] + [pl.BlockSpec(memory_space=pl.ANY)] * 4,
        out_specs=[const(*o.shape) for o in outs],
        scratch_shapes=[vm(4, 4, 4, 448, 128), vf(EIGHTH + 2 * MARGIN, 128), vm(768, 256), vm(768, 256), vm(256, 2304),
                        vm(256, 768), vf(80, 128), vf(80, 128), vm(768, 2304), vm(768, 768), vf(2304, 128),
                        dma((5,)), dma((5,)), dma((4,))] + Scatter.scratch(),
        compiler_params=pltpu.CompilerParams(collective_id=1, has_side_effects=True, vmem_limit_bytes=VMEM_LIMIT),
    )(*args[:-1], halves)


def finish_kernel(layer_in, input_in, own_in, layer_ref, input_ref, own_ref):
    layer_ref[...] = layer_in[...]
    input_ref[...] = input_in[...]
    own_ref[...] = own_in[:433, :]


def finish(*args):
    shapes = [(128, 768), (128, 768), (433, 128)]
    return pl.pallas_call(
        finish_kernel,
        grid=(1,),
        out_shape=[jax.ShapeDtypeStruct(s, a.dtype) for s, a in zip(shapes, args)],
        in_specs=[const(*a.shape) for a in args],
        out_specs=[const(*s) for s in shapes],
    )(*args)


def rotary_tables(positions):
    lane = jnp.arange(128) % 64
    freq = jnp.tile(10000.0 ** (-jnp.arange(8).astype(jnp.float32) * 2.0 / 16), 16)
    angles = positions.astype(jnp.float32)[:, None] * freq[None, :]
    cosine, sine = jnp.cos(angles), jnp.sin(angles)
    return jnp.stack([jnp.where(lane < 16, cosine, 1.0), jnp.where(lane < 8, -sine, 0.0),
                      jnp.where((lane >= 8) & (lane < 16), sine, 0.0)])


def body(tokens, params, out_grad):
    piece = tokens.shape[1]
    x, grad = tokens[0], out_grad[0]
    gathered = gather(params.reshape(433, 128)).reshape(128, ROWS, 128)
    tables = rotary_tables(lax.axis_index(SEQ) * piece + jnp.arange(piece))
    mlp, dh2, bias, h1t, in_vec, up_rows, halves_sum, back, w_qkv, w_out = middle_part(gathered, x, grad, tables)
    results = last_part(back, x, grad, tables, mlp, dh2, bias, in_vec, h1t, w_qkv, w_out, up_rows, halves_sum)
    layer_out, input_grad, own_sum = finish(*results)
    param_grad = own_sum.reshape(-1)
    return layer_out[None], input_grad[None], param_grad


def solution(mesh):
    finer = Mesh(mesh.devices.reshape(4, 2, 4, 4), DP_SEQ)
    in_specs = (P(DP, SEQ, None), P(DP_SEQ), P(DP, SEQ, None))
    out_specs = (P(DP, SEQ, None), P(DP, SEQ, None), P(DP_SEQ))
    return jax.shard_map(body, mesh=finer, in_specs=in_specs, out_specs=out_specs, check_vma=False)
```

```python
import functools

import jax
import jax.numpy as jnp
from jax import lax
from jax.experimental import pallas as pl
from jax.experimental.pallas import tpu as pltpu
from jax.sharding import Mesh
from jax.sharding import PartitionSpec as P

DP_SEQ = ("dp_0", "dp_1", "seq_0", "seq_1")
SEQ = ("seq_0", "seq_1")
DP = ("dp_0", "dp_1")
VMEM_LIMIT = 60 * 2**20
MESH = pl.DeviceIdType.MESH
ROWS = 448
PARTS = ((0, 144, (0, 2, 1)), (144, 144, (2, 1, 0)), (288, 160, (1, 0, 2)))


def place():
    return [lax.axis_index("dp_0"), lax.axis_index("seq_0"), lax.axis_index("seq_1")], lax.axis_index("dp_1")


def device(pos, core):
    return (pos[0], core, pos[1], pos[2])


def moved(pos, axis, by):
    out = list(pos)
    out[axis] = lax.rem(pos[axis] + by, 4)
    return out


def hello(pos, core):
    barrier = pltpu.get_barrier_semaphore()
    others = [device(moved(pos, a, by), core) for a in range(3) for by in (1, 2, 3)] + [device(pos, 1 - core)]
    for other in others:
        pl.semaphore_signal(barrier, inc=1, device_id=other, device_id_type=MESH)
    return len(others)


def meet(count):
    pl.semaphore_wait(pltpu.get_barrier_semaphore(), count)


class Gather:
    scratch = [pltpu.SemaphoreType.DMA((3, 9, 4)), pltpu.SemaphoreType.DMA((3, 9, 4)),
               pltpu.SemaphoreType.DMA((3, 19)), pltpu.SemaphoreType.DMA((3, 19)), pltpu.SemaphoreType.DMA]
    rings = ("a", "b0", "b1", "b2", "b3", "c0", "c1", "c2", "c3")

    def __init__(self, own_ref, out_ref, send, recv, sib_send, sib_recv, local):
        self.own_ref, self.out_ref, self.local = own_ref, out_ref, local
        self.send_sem, self.recv_sem, self.sib_send, self.sib_recv = send, recv, sib_send, sib_recv
        self.pos, self.core = place()
        self.copies, self.sibs = {}, [[], [], []]

    def near(self, axis):
        q = self.pos[axis]
        return [q] + [lax.rem(q + k, 4) for k in (3, 1, 2)]

    def region(self, where, start, size):
        return self.out_ref.at[where[0], self.core, where[1], where[2], pl.ds(start, size), :]

    def base(self, part, ring):
        a, b, c = PARTS[part][2]
        where = list(self.pos)
        if ring == "a":
            return a, where
        number = int(ring[1])
        if ring[0] == "b":
            where[a] = self.near(a)[number]
            return b, where
        where[a] = slice(None)
        where[b] = self.near(b)[number]
        return c, where

    def at(self, part, ring, which):
        axis, where = self.base(part, ring)
        where[axis] = self.near(axis)[which]
        return where

    def push(self, part, ring, number, which, by, start, size, src=None):
        axis, _ = self.base(part, ring)
        n = self.rings.index(ring)
        ref = self.region(self.at(part, ring, which), start, size)
        copy = pltpu.make_async_remote_copy(
            ref if src is None else src, ref, self.send_sem.at[part, n, number], self.recv_sem.at[part, n, number],
            device_id=device(moved(self.pos, axis, by), self.core), device_id_type=MESH)
        copy.start()
        self.copies[part, ring, number] = copy

    def begin(self, part, ring):
        start, size, _ = PARTS[part]
        src = self.own_ref.at[pl.ds(start, size), :] if ring in ("a", "b0") else None
        self.push(part, ring, 0, 0, 1, start, size, src)
        self.push(part, ring, 1, 0, 3, start, size, src)
        if ring == "a":
            self.push(part, ring, 2, 0, 2, start, size, src)

    def onward(self, part, ring, left=None, right=None):
        start, size, _ = PARTS[part]
        half = size // 32 * 16
        self.copies[part, ring, 0].wait_recv()
        if ring != "a":
            self.push(part, ring, 2, 1, 1, start, half)
        if left:
            left()
        self.copies[part, ring, 1].wait_recv()
        if ring != "a":
            self.push(part, ring, 3, 2, 3, start + half, size - half)
        if right:
            right()

    def end(self, part, ring):
        self.copies[part, ring, 2].wait_recv()
        if ring != "a":
            self.copies[part, ring, 3].wait_recv()

    def sibling(self, part, where, src=None):
        start, size, _ = PARTS[part]
        number = len(self.sibs[part])
        ref = self.region(where, start, size)
        copy = pltpu.make_async_remote_copy(
            ref if src is None else src, ref, self.sib_send.at[part, number], self.sib_recv.at[part, number],
            device_id=device(self.pos, 1 - self.core), device_id_type=MESH)
        copy.start()
        self.sibs[part].append(copy)

    def share(self, part, ring, which):
        return lambda: self.sibling(part, self.at(part, ring, which))

    def row(self, part, number):
        a, b, _ = PARTS[part][2]
        where = list(self.pos)
        where[a] = slice(None)
        where[b] = self.near(b)[number]
        return where

    def run(self):
        parts = range(3)
        own = pltpu.make_async_copy(self.own_ref, self.out_ref.at[self.pos[0], self.core, self.pos[1], self.pos[2]], self.local)
        own.start()
        for p in parts:
            self.begin(p, "a")
        for p in parts:
            self.begin(p, "b0")
        for p in parts:
            start, size, _ = PARTS[p]
            self.sibling(p, self.pos, self.own_ref.at[pl.ds(start, size), :])
        own.wait()
        for p in parts:
            def arrived(which, p=p):
                self.begin(p, "b" + str(which))
                self.sibling(p, self.at(p, "a", which))
            self.onward(p, "a", lambda: arrived(1), lambda: arrived(2))
        for p in parts:
            self.onward(p, "b0")
        for p in parts:
            self.end(p, "a")
            self.begin(p, "b3")
            self.begin(p, "c0")
            self.sibling(p, self.at(p, "a", 3))
        for p in parts:
            self.onward(p, "b1")
            self.onward(p, "b2")
        for p in parts:
            self.end(p, "b0")
            self.onward(p, "b3")
            self.begin(p, "c1")
            self.begin(p, "c2")
            self.sibling(p, self.row(p, 1))
            self.sibling(p, self.row(p, 2))
        for p in parts:
            self.onward(p, "c0", self.share(p, "c0", 1), self.share(p, "c0", 2))
        for p in parts:
            for ring in ("b1", "b2", "b3"):
                self.end(p, ring)
            self.begin(p, "c3")
            self.sibling(p, self.row(p, 3))
        for ring in ("c1", "c2", "c3"):
            for p in parts:
                self.onward(p, ring, self.share(p, ring, 1), self.share(p, ring, 2))
            for p in parts:
                before = {"c1": "c0", "c2": "c1", "c3": "c2"}[ring]
                self.end(p, before)
                self.sibling(p, self.at(p, before, 3))
        for p in parts:
            self.end(p, "c3")
            self.sibling(p, self.at(p, "c3", 3))
        for copy in self.copies.values():
            copy.wait_send()
        for copies in self.sibs:
            for copy in copies:
                copy.wait_send()
                copy.wait_recv()


EIGHTH = 16 * 433
W_QKV = (24, 768, 18)
W_OUT = (13866, 768, 6)
W_UP = (18480, 768, 24)
W_DOWN = (36936, 3072, 6)
VECTORS = {"ln1_gain": (0, 6), "ln1_shift": (6, 6), "ln2_gain": (12, 6), "ln2_shift": (18, 6),
           "b_qkv": (13848, 18), "b_out": (18474, 6), "b_up": (36912, 24), "b_down": (55368, 6)}


HEADS = 12
TILE = 512
KEYS = 512


class Exchange:
    scratch = [pltpu.SemaphoreType.DMA((16,)), pltpu.SemaphoreType.DMA((16,)), pltpu.SemaphoreType.DMA]

    def __init__(self, in_ref, out_ref, send, recv, local):
        self.in_ref, self.out_ref = in_ref, out_ref
        self.send, self.recv, self.local = send, recv, local
        self.x, self.core = lax.axis_index("dp_0"), lax.axis_index("dp_1")
        self.me = lax.axis_index("seq_0") * 4 + lax.axis_index("seq_1")
        self.others = [lax.rem(self.me + k, 16) for k in range(1, 16)]

    def where(self, t):
        return (self.x, self.core, lax.div(t, 4), lax.rem(t, 4))

    def hello(self):
        barrier = pltpu.get_barrier_semaphore()
        for t in self.others:
            pl.semaphore_signal(barrier, inc=1, device_id=self.where(t), device_id_type=MESH)

    def copy(self, t):
        return pltpu.make_async_remote_copy(
            self.in_ref.at[t], self.out_ref.at[self.me], self.send.at[t], self.recv.at[self.me],
            device_id=self.where(t), device_id_type=MESH)

    def arrival(self, t):
        return pltpu.make_async_remote_copy(
            self.out_ref.at[t], self.out_ref.at[t], self.send.at[t], self.recv.at[t],
            device_id=self.where(t), device_id_type=MESH)

    def own(self):
        return pltpu.make_async_copy(self.in_ref.at[self.me], self.out_ref.at[self.me], self.local)


class ToHeads(Exchange):
    def start(self):
        for t in self.others:
            pl.when(t < HEADS)(lambda t=t: self.copy(t).start())
        pl.when(self.me < HEADS)(lambda: self.own().start())

    def wait(self):
        @pl.when(self.me < HEADS)
        def _():
            for t in self.others:
                self.arrival(t).wait_recv()
            self.own().wait()

    def wait_send(self):
        for t in self.others:
            pl.when(t < HEADS)(lambda t=t: self.copy(t).wait_send())


class FromHeads(Exchange):
    def start(self, first=0, last=16):
        for t in range(first, last):
            pl.when((self.me < HEADS) & (self.me != t))(lambda t=t: self.copy(jnp.int32(t)).start())
            pl.when((self.me < HEADS) & (self.me == t))(lambda: self.own().start())

    def wait(self):
        for t in self.others:
            pl.when(t < HEADS)(lambda t=t: self.arrival(t).wait_recv())

        @pl.when(self.me < HEADS)
        def _():
            for t in self.others:
                self.copy(t).wait_send()
            self.own().wait()


NT = (((1,), (1,)), ((), ()))


def product(a, b, dims=(((1,), (0,)), ((), ()))):
    return lax.dot_general(a, b, dims, preferred_element_type=jnp.float32)


def unrolled(low, high, body, carry):
    for j in range(low, high):
        carry = body(j, carry)
    return carry


def head_kernel(ready, in_ref, att_out, key_out, k, v, kt, vt, scores, dk, dv):
    blocks = 2048 // TILE
    per = TILE // 128

    def rows(which, i):
        return jnp.concatenate([in_ref[i * per + p, which] for p in range(per)], 0)

    @pl.loop(0, blocks)
    def _(i):
        at = pl.ds(pl.multiple_of(i * TILE, TILE), TILE)
        key = rows(0, i)[:, 64:]
        value = rows(1, i)[:, :64]
        k[at, :] = key
        v[at, :] = value
        kt[:, at] = key.T
        vt[:, at] = value.T
        dk[at, :] = jnp.zeros((TILE, 64), jnp.float32)
        dv[at, :] = jnp.zeros((TILE, 64), jnp.float32)

    def block(i):
        query = rows(0, i)[:, :64] * jnp.bfloat16(0.125)
        grad = rows(1, i)[:, 64:]

        def tile(j):
            return pl.ds(j * KEYS, KEYS)

        def put(j, s):
            for n in range(TILE // 128):
                scores[pl.ds(j * KEYS + n * 2048, KEYS), :] = s[:, 128 * n:128 * (n + 1)]

        def get(j):
            return jnp.concatenate(
                [scores[pl.ds(j * KEYS + n * 2048, KEYS), :] for n in range(TILE // 128)], 1)

        last = i * TILE // KEYS

        def first(j, top):
            s = product(k[tile(j), :], query, NT)
            put(j, s)
            return jnp.maximum(top, jnp.max(s, 0, keepdims=True))

        top = unrolled(0, last, first, jnp.full((1, TILE), -1e30, jnp.float32))
        s = product(k[tile(last), :], query, NT)
        keep = lax.broadcasted_iota(jnp.int32, (KEYS, TILE), 0) - lax.broadcasted_iota(jnp.int32, (KEYS, TILE), 1) <= i * TILE - last * KEYS
        s = jnp.where(keep, s, -1e30)
        put(last, s)
        top = jnp.maximum(top, jnp.max(s, 0, keepdims=True))

        def second(j, carry):
            total, out = carry
            e = jnp.exp(get(j) - top)
            put(j, e)
            return total + jnp.sum(e, 0, keepdims=True), out + product(vt[:, tile(j)], e.astype(jnp.bfloat16))

        total, out = unrolled(0, last + 1, second, (jnp.zeros((1, TILE), jnp.float32), jnp.zeros((64, TILE), jnp.float32)))
        scale = 1.0 / total
        out = out * scale
        inner = jnp.sum(out * grad.astype(jnp.float32).T, 0, keepdims=True)

        def third(j, dq):
            p = get(j) * scale
            dp = product(v[tile(j), :], grad, NT)
            ds = (p * (dp - inner)).astype(jnp.bfloat16)
            dv[tile(j), :] += product(p.astype(jnp.bfloat16), grad)
            dk[tile(j), :] += product(ds, query)
            return dq + product(kt[:, tile(j)], ds)

        dq = unrolled(0, last + 1, third, jnp.zeros((64, TILE), jnp.float32)) * 0.125
        both = jnp.concatenate([out, dq], 0).T.astype(jnp.bfloat16)
        for p in range(per):
            att_out[i * per + p] = both[128 * p:128 * (p + 1)]

    for i in range(blocks):
        block(i)
        ready(i * per, (i + 1) * per)

    @pl.loop(0, blocks)
    def _(i):
        at = pl.ds(pl.multiple_of(i * TILE, TILE), TILE)
        both = jnp.concatenate([dk[at, :], dv[at, :]], 1).astype(jnp.bfloat16)
        for p in range(per):
            key_out[i * per + p] = both[128 * p:128 * (p + 1)]


HEAD_SCRATCH = [pltpu.VMEM((2048, 64), jnp.bfloat16), pltpu.VMEM((2048, 64), jnp.bfloat16),
                pltpu.VMEM((64, 2048), jnp.bfloat16), pltpu.VMEM((64, 2048), jnp.bfloat16),
                pltpu.VMEM((2048, 64), jnp.float32), pltpu.VMEM((2048, 64), jnp.float32)]


MARGIN = 384
CHUNK = 128


def weight_eighth(number, pairs, vec_ref, flat):
    low, high = number * EIGHTH, (number + 1) * EIGHTH
    at = MARGIN - low
    for (offset, rows, blocks), left, right in pairs:
        first = max(0, (low - offset) // blocks) // 16 * 16
        last = min(rows, -(-(high - offset) // blocks))
        last = -(-last // 16) * 16
        if last <= first:
            continue
        size = min(CHUNK, last - first)
        count = -(-(last - first) // size)
        base = offset + at

        @pl.loop(0, count)
        def _(i, first=first, last=last, size=size, blocks=blocks, base=base, left=left, right=right):
            row = pl.multiple_of(jnp.minimum(first + i * size, last - size), 16)
            lhs = left[pl.ds(row, size), :]

            @pl.loop(0, blocks // 2, unroll=3)
            def _(j):
                rhs = right[:, pl.ds(pl.multiple_of(j * 256, 256), 256)]
                result = product(lhs, rhs)
                start = base + row * blocks + 2 * j
                flat[pl.ds(start, size, stride=blocks), :] = result[:, :128]
                flat[pl.ds(start + 1, size, stride=blocks), :] = result[:, 128:]

    row = 0
    for name in ORDER:
        start, count = VECTORS[name]
        lo, hi = max(start, low), min(start + count, high)
        if lo < hi:
            flat[lo + at:hi + at, :] = vec_ref[row + lo - start:row + hi - start, :]
        row += count
    end = 55374
    if high > end:
        flat[end + at:high + at, :] = jnp.zeros((high - end, 128), jnp.float32)


def halves(size):
    half = size // 32 * 16
    return half, size - half


class Scatter:
    names = ("c0", "c1", "c2", "c3", "b", "a")
    @staticmethod
    def scratch():
        out = []
        for _, size, _ in PARTS:
            h0, h1 = halves(size)
            for name in Scatter.names:
                if name == "a":
                    out += [pltpu.VMEM((size, 128), jnp.bfloat16)] * 3
                else:
                    out += [pltpu.VMEM((4, n, 128), jnp.bfloat16) for n in (h0, h1, h1, h0, h0, h1, h0, h1)]
            out += [pltpu.VMEM((4, 4, size, 128), jnp.bfloat16), pltpu.VMEM((4, size, 128), jnp.bfloat16)]
        return out + [pltpu.SemaphoreType.DMA((3, 6, 10)), pltpu.SemaphoreType.DMA((3, 6, 10))]

    def __init__(self, in_ref, out_ref, *scratch):
        self.in_ref, self.out_ref = in_ref, out_ref
        self.send, self.recv = scratch[-2:]
        take = iter(scratch[:-2])
        self.buf, self.rows, self.line = {}, [], []
        for p in range(3):
            for name in self.names:
                self.buf[p, name] = [next(take) for _ in range(3 if name == "a" else 8)]
            self.rows.append(next(take))
            self.line.append(next(take))
        self.pos, self.core = place()
        self.copies = {}

    def near(self, axis):
        q = self.pos[axis]
        return [q] + [lax.rem(q + k, 4) for k in (3, 1, 2)]

    def axis(self, p, name):
        return PARTS[p][2]["abc".index(name[0])]

    def source(self, p, name, which, lo, n):
        a, b, c = PARTS[p][2]
        if name == "a":
            return self.line[p].at[self.near(a)[which], pl.ds(lo, n), :]
        if name == "b":
            return self.rows[p].at[which, :, pl.ds(lo, n), :]
        where = [slice(None)] * 3
        where[b] = self.near(b)[int(name[1])]
        where[c] = self.near(c)[which]
        return self.in_ref.at[where[0], where[1], where[2], pl.ds(PARTS[p][0] + lo, n), :]

    def push(self, p, name, number, src, by, when=None, dst=None, sem=None):
        n = self.names.index(name)
        sem = number if sem is None else sem
        copy = pltpu.make_async_remote_copy(
            src, self.buf[p, name][number] if dst is None else dst, self.send.at[p, n, sem], self.recv.at[p, n, sem],
            device_id=device(moved(self.pos, self.axis(p, name), by), self.core), device_id_type=MESH)
        if when is None:
            copy.start()
        else:
            pl.when(when)(copy.start)
        self.copies.setdefault((p, name, number), []).append(copy)

    def arrived(self, p, name, number):
        for copy in self.copies[p, name, number]:
            copy.wait_recv()

    def sends(self, p):
        h0, h1 = halves(PARTS[p][1])
        return ((0, 3, 0, h0, 1), (1, 3, h0, h1, 3), (2, 2, h0, h1, 1), (3, 1, 0, h0, 3))

    def begin(self, p, name, numbers=(0, 1, 2, 3)):
        for number, which, lo, n, by in self.sends(p):
            if number in numbers:
                self.push(p, name, number, self.source(p, name, which, lo, n), by)

    def ahead(self, name, later, numbers):
        for p in range(3):
            a, b, c = PARTS[p][2]
            for number, which, lo, n, by in self.sends(p):
                if number not in numbers:
                    continue
                src = self.source(p, name, which, lo, n)
                if a == 0:
                    part = pl.ds(2 if later else 0, 2)
                    self.push(p, name, number, src.at[part], by, None, self.buf[p, name][number].at[part],
                              number if later else 6 + number)
                    continue
                x = self.near(0)[int(name[1])] if b == 0 else self.near(0)[which]
                if later:
                    self.push(p, name, number, src, by, x >= 2)
                else:
                    pl.when(x < 2)(self.copies[p, name, number][0].start)

    def direct(self, p):
        for number, (which, by) in enumerate(((1, 3), (2, 1), (3, 2))):
            self.push(p, "a", number, self.source(p, "a", which, 0, PARTS[p][1]), by)

    def total(self, p):
        start, size, _ = PARTS[p]
        for number in range(3):
            self.arrived(p, "a", number)
        value = self.source(p, "a", 0, 0, size)[...].astype(jnp.float32)
        for other in self.buf[p, "a"]:
            value = value + other[...].astype(jnp.float32)
        self.out_ref[start:start + size, :] = value

    def add(self, name, mine, others, put):
        def one(*at):
            total = mine[at + (slice(None), slice(None))].astype(jnp.float32)
            for other in others:
                total = total + other[at + (slice(None), slice(None))].astype(jnp.float32)
            put(at, total)

        pl.loop(0, 4)(lambda i: one(i))

    def onward(self, p, name):
        h0, h1 = halves(PARTS[p][1])
        b = self.buf[p, name]

        def to(ref):
            def put(at, total):
                ref[at + (slice(None), slice(None))] = total.astype(jnp.bfloat16)
            return put

        self.arrived(p, name, 0)
        self.add(name, self.source(p, name, 2, 0, h0), [b[0]], to(b[6]))
        self.push(p, name, 4, b[6], 1)
        self.arrived(p, name, 1)
        self.add(name, self.source(p, name, 1, h0, h1), [b[1]], to(b[7]))
        self.push(p, name, 5, b[7], 3)

    def end(self, p, name):
        h0, h1 = halves(PARTS[p][1])
        b = self.buf[p, name]
        for number in (3, 2, 4, 5):
            self.arrived(p, name, number)
        for lo, n, others in ((0, h0, [b[3], b[4]]), (h0, h1, [b[2], b[5]])):
            def put(at, total, lo=lo, n=n):
                if name == "b":
                    self.line[p][at + (pl.ds(lo, n), slice(None))] = total.astype(jnp.bfloat16)
                else:
                    self.rows[p][(int(name[1]),) + at + (pl.ds(lo, n), slice(None))] = total.astype(jnp.bfloat16)
            self.add(name, self.source(p, name, 0, lo, n), others, put)

    def before(self):
        for numbers in ((0, 1), (2, 3)):
            for name in ("c3", "c1", "c2", "c0"):
                self.ahead(name, True, numbers)

    def run(self, meanwhile):
        parts = range(3)

        def each(step, name, *more):
            for p in parts:
                step(p, name, *more)

        for name in ("c3", "c1", "c2", "c0"):
            self.ahead(name, False, (0, 1))
        self.ahead("c3", False, (2, 3))
        meanwhile()
        each(self.onward, "c3")
        self.ahead("c1", False, (2, 3))
        each(self.onward, "c1")
        each(self.end, "c3")
        each(self.begin, "b", (0, 1))
        self.ahead("c2", False, (2, 3))
        each(self.onward, "c2")
        each(self.end, "c1")
        each(self.begin, "b", (3,))
        self.ahead("c0", False, (2, 3))
        each(self.onward, "c0")
        each(self.end, "c2")
        each(self.begin, "b", (2,))
        each(self.onward, "b")
        for p in parts:
            self.end(p, "c0")
            self.end(p, "b")
            self.direct(p)
        for p in parts:
            self.total(p)
        for copies in self.copies.values():
            for copy in copies:
                copy.wait_send()


EPS = 1e-05
ORDER = ("ln1_gain", "ln1_shift", "ln2_gain", "ln2_shift", "b_qkv", "b_out", "b_up", "b_down")


def widen(g_ref, flat, step):
    @pl.loop(0, 16)
    def _(k):
        base = (step * 16 + k) * 433
        flat[pl.ds(base, 440), :] = g_ref[k, 0:440, :].astype(jnp.float32)


def unpack_matrix(flat, first, where, out, size=64):
    offset, rows, blocks = where
    start = offset - first * EIGHTH

    @pl.loop(0, rows // size)
    def _(i):
        for j in range(blocks):
            piece = flat[pl.ds(start + j + i * (size * blocks), size, stride=blocks), :]
            out[pl.ds(pl.multiple_of(i * size, size), size), 128 * j:128 * (j + 1)] = piece.astype(jnp.bfloat16)


def as_row(ref, start, count):
    return jnp.concatenate([ref[start + n:start + n + 1, :] for n in range(count)], 1)


def to_rows(ref, start, row):
    for n in range(row.shape[1] // 128):
        ref[start + n:start + n + 1, :] = row[:, 128 * n:128 * (n + 1)]


def normalized(values):
    center = jnp.mean(values, -1, keepdims=True)
    centered = values - center
    factor = lax.rsqrt(jnp.mean(centered * centered, -1, keepdims=True) + EPS)
    return centered * factor, factor


def turn(x, tables, sign):
    return x * tables[0] + (pltpu.roll(x, 120, 1) * tables[1] + pltpu.roll(x, 8, 1) * tables[2]) * sign


def const(*shape):
    return pl.BlockSpec(shape, lambda e: (0,) * len(shape))


def gelu_pair(u):
    inside = 0.5 * (1.0 + lax.erf(u * 0.7071067811865476))
    return u * inside, inside + u * jnp.exp(-0.5 * u * u) * 0.3989422804014327


class Twin:
    def __init__(self, send, recv):
        self.send, self.recv, self.copies = send, recv, []
        self.pos, self.core = place()

    def push(self, src, dst):
        number = len(self.copies)
        copy = pltpu.make_async_remote_copy(src, dst, self.send.at[number], self.recv.at[number],
                                            device_id=device(self.pos, 1 - self.core), device_id_type=MESH)
        copy.start()
        self.copies.append(copy)
        return copy

    def wait_send(self):
        for copy in self.copies:
            copy.wait_send()


def middle_kernel(params_ref, tokens_ref, grad_ref, tables_ref,
                  mlp_ref, dh2_ref, bias_ref, h1t_ref, vec_ref, up_ref, halves_ref, att_ref, key_ref, w_qkv_ref, w_out_ref, all_ref,
                  gbuf, flat, w_up, w_down, act, slope, act_pair, h2_pair, g_pair, dup_pair, vec, vec2,
                  heads_in, att_out, key_out, w_qkv, w_out, wide, blocks, own, *rest):
    head_scratch, rest = rest[:6], rest[6:]
    there = ToHeads(blocks, heads_in, *rest[0:3])
    home = FromHeads(att_out, att_ref, *rest[3:6])
    home_keys = FromHeads(key_out, key_ref, *rest[6:9])
    twin = Twin(*rest[9:11])
    load, store = rest[11:13]
    core = lax.axis_index("dp_1")
    gather = Gather(own, all_ref, *rest[13:])
    there.hello()
    count = hello(gather.pos, core)
    own[0:432, :] = params_ref[0:432, :]
    own[432:448, :] = jnp.zeros((16, 128), jnp.bfloat16)
    own[432:433, :] = params_ref[432:433, :]
    meet(count + 15)
    gather.run()
    loads = [pltpu.make_async_copy(all_ref.at[e // 2, e % 2], gbuf.at[e % 3], load.at[e]) for e in range(8)]
    for copy in loads[:3]:
        copy.start()
    stores = []

    def keep(src, dst):
        copy = pltpu.make_async_copy(src, dst, store.at[len(stores)])
        copy.start()
        stores.append(copy)

    def widen(eighth, at):
        @pl.loop(0, 16)
        def _(k):
            flat[pl.ds((at * 16 + k) * 433, 440), :] = gbuf[eighth % 3, lax.div(k, 4), lax.rem(k, 4), 0:440, :].astype(jnp.float32)

    for e in range(2):
        loads[e].wait()
        widen(e, e)
        loads[3 + e].start()
    unpack_matrix(flat, 0, W_QKV, w_qkv)
    keep(w_qkv, w_qkv_ref)
    loads[2].wait()
    widen(2, 2)
    unpack_matrix(flat, 0, W_OUT, w_out)
    keep(w_out, w_out_ref)
    vec_ref[0:24, :] = flat[0:24, :]
    start = VECTORS["b_out"][0]
    vec_ref[24:30, :] = flat[start:start + 6, :]
    normal, _ = normalized(tokens_ref[...].astype(jnp.float32))
    h1 = (normal * as_row(flat, 0, 6) + as_row(flat, 6, 6)).astype(jnp.bfloat16)
    h2 = (normal * as_row(flat, 12, 6) + as_row(flat, 18, 6)).astype(jnp.bfloat16)
    h1t_ref[...] = h1.T
    for n in range(9):
        start = VECTORS["b_qkv"][0] + 2 * n
        qkv = product(h1, w_qkv[:, 256 * n:256 * (n + 1)]) + as_row(flat, start, 2)
        wide[256 * n:256 * n + 128, :] = qkv[:, :128]
        wide[256 * n + 128:256 * (n + 1), :] = qkv[:, 128:]
    low = lax.broadcasted_iota(jnp.int32, (128, 128), 1) < 64
    swap = lambda t: pltpu.roll(t, 64, 1)
    for m in range(6):
        q, k, v = (wide[128 * (6 * p + m):128 * (6 * p + m + 1), :] for p in range(3))
        q = turn(q, tables_ref, 1.0)
        k = turn(k, tables_ref, 1.0)
        a = product(grad_ref[...], w_out[128 * m:128 * (m + 1), :], NT)
        blocks[2 * m, 0] = jnp.where(low, q, swap(k)).astype(jnp.bfloat16)
        blocks[2 * m + 1, 0] = jnp.where(low, swap(q), k).astype(jnp.bfloat16)
        blocks[2 * m, 1] = jnp.where(low, v, swap(a)).astype(jnp.bfloat16)
        blocks[2 * m + 1, 1] = jnp.where(low, swap(v), a).astype(jnp.bfloat16)
    there.start()
    h2_pair[:, :128] = h2.T
    g_pair[:128, :] = grad_ref[...]
    h2_copy = twin.push(h2_pair.at[:, pl.ds(0, 128)], h2_pair.at[:, pl.ds(128, 128)])
    g_copy = twin.push(g_pair.at[pl.ds(0, 128), :], g_pair.at[pl.ds(128, 128), :])
    for e in range(2, 6):
        if e > 2:
            loads[e].wait()
        widen(e, e - 2)
        if e < 5:
            loads[3 + e].start()
    unpack_matrix(flat, 2, W_UP, w_up)
    start = VECTORS["b_up"][0] - 2 * EIGHTH
    for n in range(12):
        at = slice(256 * n, 256 * (n + 1))
        up = product(h2, w_up[:, at]) + as_row(flat, start + 2 * n, 2)
        value, slope[:, at] = gelu_pair(up)
        value = value.astype(jnp.bfloat16)
        act[:, at] = value
        act_pair[at, :128] = value.T
    act_copy = twin.push(act_pair.at[:, pl.ds(0, 128)], act_pair.at[:, pl.ds(128, 128)])
    for e in range(3):
        if e:
            loads[5 + e].wait()
        widen(5 + e, e)
    unpack_matrix(flat, 5, W_DOWN, w_down, 128)
    start = VECTORS["b_down"][0] - 5 * EIGHTH
    for n in range(12):
        at = slice(256 * n, 256 * (n + 1))
        dup = (product(grad_ref[...], w_down[at, :], NT) * slope[:, at]).astype(jnp.bfloat16)
        dup_pair[:128, at] = dup
        to_rows(vec, 48 + 2 * n, jnp.sum(dup.astype(jnp.float32), 0, keepdims=True))
    dup_copy = twin.push(dup_pair.at[pl.ds(0, 128), :], dup_pair.at[pl.ds(128, 128), :])
    bias_ref[...] = vec[48:72, :]
    shift = jnp.sum(grad_ref[...].astype(jnp.float32), 0, keepdims=True)
    to_rows(vec, 72, shift)
    vec[78:80, :] = jnp.zeros((2, 128), jnp.float32)
    vec_copy = twin.push(vec.at[pl.ds(48, 32), :], vec2)
    for n in range(3):
        at = slice(256 * n, 256 * (n + 1))
        mlp_ref[:, at] = product(act[...], w_down[:, at]) + as_row(flat, start + 2 * n, 2)
        dh2_ref[:, at] = product(dup_pair[:128, :], w_up[at, :], NT)
    there.wait()
    head_kernel(home.start, heads_in, att_out, key_out, *head_scratch[:4], flat, *head_scratch[4:])
    home_keys.start()
    for copy in (h2_copy, g_copy, act_copy, dup_copy, vec_copy):
        copy.wait_recv()
    vec_copy.wait_send()
    vec[48:80, :] = vec[48:80, :] + vec2[...]
    for t in (1, 2, 3):
        for c in range(2):
            if t > 1 or c == 1:
                pl.when(core == c)(
                    lambda number=2 * t + c: weight_eighth(number, ((W_UP, h2_pair, dup_pair), (W_DOWN, act_pair, g_pair)), vec, flat))

        @pl.loop(0, 16)
        def _(k):
            gbuf[t - 1, lax.div(k, 4), lax.rem(k, 4)] = flat[pl.ds(MARGIN + 433 * k, 448), :].astype(jnp.bfloat16)

        keep(gbuf.at[t - 1], halves_ref.at[t - 1])

    @pl.when(core == 0)
    def _():
        @pl.loop(0, 12)
        def _(j):
            result = product(h2_pair[:96, :], dup_pair[:, pl.ds(pl.multiple_of(j * 256, 256), 256)])
            wide[pl.ds(2 * j, 96, stride=24), :] = result[:, :128]
            wide[pl.ds(2 * j + 1, 96, stride=24), :] = result[:, 128:]

    keep(wide, up_ref)

    home.wait()
    home_keys.wait()
    there.wait_send()
    for copy in (h2_copy, g_copy, act_copy, dup_copy):
        copy.wait_send()
    for copy in stores:
        copy.wait()


def middle_part(params, tokens, grad, tables):
    f32 = lambda *s: jax.ShapeDtypeStruct(s, jnp.float32)
    bf = lambda *s: jax.ShapeDtypeStruct(s, jnp.bfloat16)
    vm = lambda *s: pltpu.VMEM(s, jnp.bfloat16)
    vf = lambda *s: pltpu.VMEM(s, jnp.float32)
    anywhere = pl.BlockSpec(memory_space=pl.ANY)
    outs = [f32(128, 768), f32(128, 768), f32(24, 128), bf(768, 128), f32(32, 128)]
    far = [f32(2304, 128), bf(3, 4, 4, 448, 128), bf(HEADS, 128, 128), bf(HEADS, 128, 128),
           bf(768, 2304), bf(768, 768), bf(4, 2, 4, 4, 448, 128)]
    dma = pltpu.SemaphoreType.DMA
    return pl.pallas_call(
        middle_kernel,
        grid=(1,),
        out_shape=outs + far,
        in_specs=[const(433, 128), const(128, 768), const(128, 768), const(3, 128, 128)],
        out_specs=[const(*o.shape) for o in outs] + [anywhere] * len(far),
        scratch_shapes=[vm(3, 4, 4, 448, 128), vf(4 * EIGHTH + 16, 128), vm(768, 3072), vm(3072, 768), vm(128, 3072),
                        vf(128, 3072), vm(3072, 256), vm(768, 256), vm(256, 768), vm(256, 3072), vf(80, 128), vf(32, 128),
                        vm(16, 2, 128, 128), vm(16, 128, 128), vm(16, 128, 128), vm(768, 2304), vm(768, 768), vf(2304, 128),
                        vm(HEADS, 2, 128, 128), vm(448, 128)]
        + HEAD_SCRATCH + Exchange.scratch * 3 + [dma((5,)), dma((5,)), dma((8,)), dma((6,))] + Gather.scratch,
        compiler_params=pltpu.CompilerParams(collective_id=2, has_side_effects=True, vmem_limit_bytes=VMEM_LIMIT),
    )(params, tokens, grad, tables)


def last_kernel(att_ref, key_ref, tokens_ref, grad_ref, tables_ref, mlp_ref, dh2_ref, bias_ref, in_vec, h1t_ref,
                w_qkv_ref, w_out_ref, up_in, halves_ref, layer_ref, input_ref, own_ref,
                sums, flat, h1_pair, att_pair, dqkv_pair, g_pair, vec, vec2, w_qkv, w_out, up_ref, twin_send, twin_recv, load, *scratch):
    pairs = ((halves_ref, sums.at[pl.ds(1, 3)]), (w_qkv_ref, w_qkv), (w_out_ref, w_out), (up_in, up_ref))
    later, qkv_load, out_load, up_load = (pltpu.make_async_copy(a, b, load.at[n]) for n, (a, b) in enumerate(pairs))
    later.start()
    scatter = Scatter(sums, own_ref, *scratch)
    meet(hello(scatter.pos, scatter.core))
    twin = Twin(twin_send, twin_recv)
    h1_pair[:, :128] = h1t_ref[...]
    g_pair[:128, :] = grad_ref[...]
    lanes = lambda pair: twin.push(pair.at[:, pl.ds(0, 128)], pair.at[:, pl.ds(128, 128)])
    rows = lambda pair: twin.push(pair.at[pl.ds(0, 128), :], pair.at[pl.ds(128, 128), :])
    lanes(h1_pair)
    rows(g_pair)
    later.wait()
    for copy in (qkv_load, out_load, up_load):
        copy.start()
    scatter.before()
    low = lax.broadcasted_iota(jnp.int32, (128, 128), 1) < 64
    swap = lambda t: pltpu.roll(t, 64, 1)
    f32 = lambda t: t.astype(jnp.float32)
    attended = []
    for m in range(6):
        a, b = f32(att_ref[2 * m]), f32(att_ref[2 * m + 1])
        c, d = f32(key_ref[2 * m]), f32(key_ref[2 * m + 1])
        attended.append(jnp.where(low, a, swap(b)).astype(jnp.bfloat16))
        dq = turn(jnp.where(low, swap(a), b), tables_ref, -1.0)
        dk = turn(jnp.where(low, c, swap(d)), tables_ref, -1.0)
        dv = jnp.where(low, swap(c), d)
        for p, part in enumerate((dq, dk, dv)):
            dqkv_pair[:128, 768 * p + 128 * m:768 * p + 128 * (m + 1)] = part.astype(jnp.bfloat16)
    rows(dqkv_pair)
    attended = jnp.concatenate(attended, 1)
    att_pair[:, :128] = attended.T
    lanes(att_pair)
    tokens = f32(tokens_ref[...])
    grad = f32(grad_ref[...])
    normal, factor = normalized(tokens)
    qkv_load.wait()
    input_ref[...] = product(dqkv_pair[:128, :], w_qkv[...], NT)
    for row, dh in ((0, input_ref), (12, dh2_ref)):
        to_rows(vec, row, jnp.sum(dh[...] * normal, 0, keepdims=True))
        to_rows(vec, row + 6, jnp.sum(dh[...], 0, keepdims=True))
    to_rows(vec, 24, jnp.sum(f32(dqkv_pair[:128, :]), 0, keepdims=True))
    shift = jnp.sum(grad, 0, keepdims=True)
    to_rows(vec, 42, shift)
    vec[48:72, :] = bias_ref[...]
    to_rows(vec, 72, shift)
    vec[78:80, :] = jnp.zeros((2, 128), jnp.float32)
    twin.push(vec, vec2)
    out_load.wait()
    up_load.wait()

    def results():
        tokens = f32(tokens_ref[...])
        branch = lax.dot_general(att_pair[:, :128], w_out[...], (((0,), (0,)), ((), ())), preferred_element_type=jnp.float32)
        layer_ref[...] = (tokens + (branch + as_row(in_vec, 24, 6)) + mlp_ref[...]).astype(jnp.bfloat16)
        normal, factor = normalized(tokens)
        total = f32(grad_ref[...])
        for gain_at, dh in ((0, input_ref), (12, dh2_ref)):
            scaled = dh[...] * as_row(in_vec, gain_at, 6)
            inner = scaled - jnp.mean(scaled, -1, keepdims=True) - normal * jnp.mean(scaled * normal, -1, keepdims=True)
            total = total + factor * inner
        input_ref[...] = total

    for copy in twin.copies:
        copy.wait_recv()
    twin.copies[-1].wait_send()
    vec[...] = vec[...] + vec2[...]
    pairs = ((W_QKV, h1_pair, dqkv_pair), (W_OUT, att_pair, g_pair))

    def keep(t):
        for z in range(4):
            @pl.loop(0, 4)
            def _(y):
                sums[t, z, y] = flat[pl.ds(MARGIN + 433 * (4 * z + y), 448), :].astype(jnp.bfloat16)

    for c in range(2):
        pl.when(scatter.core == c)(lambda c=c: weight_eighth(c, pairs, vec, flat))
    keep(0)

    @pl.when(scatter.core == 0)
    def _():
        weight_eighth(2, pairs, vec, flat)
        at = W_UP[0] - 2 * EIGHTH + MARGIN
        flat[at:at + 2304, :] = up_ref[...]
        keep(1)

    scatter.run(results)
    for copy in twin.copies[:-1]:
        copy.wait_send()


def last_part(*args):
    bf = lambda *s: jax.ShapeDtypeStruct(s, jnp.bfloat16)
    f32 = lambda *s: jax.ShapeDtypeStruct(s, jnp.float32)
    vm = lambda *s: pltpu.VMEM(s, jnp.bfloat16)
    vf = lambda *s: pltpu.VMEM(s, jnp.float32)
    dma = pltpu.SemaphoreType.DMA
    outs = [bf(128, 768), f32(128, 768), f32(448, 128)]
    return pl.pallas_call(
        last_kernel,
        grid=(1,),
        out_shape=outs,
        in_specs=[const(*a.shape) for a in args[:-4]] + [pl.BlockSpec(memory_space=pl.ANY)] * 4,
        out_specs=[const(*o.shape) for o in outs],
        scratch_shapes=[vm(4, 4, 4, 448, 128), vf(EIGHTH + 2 * MARGIN, 128), vm(768, 256), vm(768, 256), vm(256, 2304),
                        vm(256, 768), vf(80, 128), vf(80, 128), vm(768, 2304), vm(768, 768), vf(2304, 128),
                        dma((5,)), dma((5,)), dma((4,))] + Scatter.scratch(),
        compiler_params=pltpu.CompilerParams(collective_id=1, has_side_effects=True, vmem_limit_bytes=VMEM_LIMIT),
    )(*args)


def finish_kernel(layer_in, input_in, own_in, layer_ref, input_ref, own_ref):
    layer_ref[...] = layer_in[...]
    input_ref[...] = input_in[...]
    own_ref[...] = own_in[:433, :]


def finish(*args):
    shapes = [(128, 768), (128, 768), (433, 128)]
    return pl.pallas_call(
        finish_kernel,
        grid=(1,),
        out_shape=[jax.ShapeDtypeStruct(s, a.dtype) for s, a in zip(shapes, args)],
        in_specs=[const(*a.shape) for a in args],
        out_specs=[const(*s) for s in shapes],
    )(*args)


def rotary_tables(positions):
    lane = jnp.arange(128) % 64
    freq = jnp.tile(10000.0 ** (-jnp.arange(8).astype(jnp.float32) * 2.0 / 16), 16)
    angles = positions.astype(jnp.float32)[:, None] * freq[None, :]
    cosine, sine = jnp.cos(angles), jnp.sin(angles)
    return jnp.stack([jnp.where(lane < 16, cosine, 1.0), jnp.where(lane < 8, -sine, 0.0),
                      jnp.where((lane >= 8) & (lane < 16), sine, 0.0)])


def body(tokens, params, out_grad):
    piece = tokens.shape[1]
    x, grad = tokens[0], out_grad[0]
    tables = rotary_tables(lax.axis_index(SEQ) * piece + jnp.arange(piece))
    mlp, dh2, bias, h1t, in_vec, up_rows, later, att, keys, w_qkv, w_out, _ = middle_part(
        params.reshape(433, 128), x, grad, tables
    )
    results = last_part(att, keys, x, grad, tables, mlp, dh2, bias, in_vec, h1t, w_qkv, w_out, up_rows, later)
    layer_out, input_grad, own_sum = finish(*results)
    param_grad = own_sum.reshape(-1)
    return layer_out[None], input_grad[None], param_grad


def solution(mesh):
    finer = Mesh(mesh.devices.reshape(4, 2, 4, 4), DP_SEQ)
    in_specs = (P(DP, SEQ, None), P(DP_SEQ), P(DP, SEQ, None))
    out_specs = (P(DP, SEQ, None), P(DP, SEQ, None), P(DP_SEQ))
    return jax.shard_map(body, mesh=finer, in_specs=in_specs, out_specs=out_specs, check_vma=False)
```

```python
import functools

import jax
import jax.numpy as jnp
from jax import lax
from jax.experimental import pallas as pl
from jax.experimental.pallas import tpu as pltpu
from jax.sharding import Mesh
from jax.sharding import PartitionSpec as P

DP_SEQ = ("dp_0", "dp_1", "seq_0", "seq_1")
SEQ = ("seq_0", "seq_1")
DP = ("dp_0", "dp_1")
VMEM_LIMIT = 60 * 2**20
MESH = pl.DeviceIdType.MESH
ROWS = 448
PARTS = ((0, 144, (0, 2, 1)), (144, 144, (2, 1, 0)), (288, 160, (1, 0, 2)))


def place():
    return [lax.axis_index("dp_0"), lax.axis_index("seq_0"), lax.axis_index("seq_1")], lax.axis_index("dp_1")


def device(pos, core):
    return (pos[0], core, pos[1], pos[2])


def moved(pos, axis, by):
    out = list(pos)
    out[axis] = lax.rem(pos[axis] + by, 4)
    return out


def hello(pos, core):
    barrier = pltpu.get_barrier_semaphore()
    others = [device(moved(pos, a, by), core) for a in range(3) for by in (1, 2, 3)] + [device(pos, 1 - core)]
    for other in others:
        pl.semaphore_signal(barrier, inc=1, device_id=other, device_id_type=MESH)
    return len(others)


def meet(count):
    pl.semaphore_wait(pltpu.get_barrier_semaphore(), count)


class Gather:
    scratch = [pltpu.SemaphoreType.DMA((3, 9, 4)), pltpu.SemaphoreType.DMA((3, 9, 4)),
               pltpu.SemaphoreType.DMA((3, 19)), pltpu.SemaphoreType.DMA((3, 19)), pltpu.SemaphoreType.DMA]
    rings = ("a", "b0", "b1", "b2", "b3", "c0", "c1", "c2", "c3")

    def __init__(self, own_ref, out_ref, send, recv, sib_send, sib_recv, local):
        self.own_ref, self.out_ref, self.local = own_ref, out_ref, local
        self.send_sem, self.recv_sem, self.sib_send, self.sib_recv = send, recv, sib_send, sib_recv
        self.pos, self.core = place()
        self.copies, self.sibs = {}, [[], [], []]

    def near(self, axis):
        q = self.pos[axis]
        return [q] + [lax.rem(q + k, 4) for k in (3, 1, 2)]

    def region(self, where, start, size):
        return self.out_ref.at[where[0], self.core, where[1], where[2], pl.ds(start, size), :]

    def base(self, part, ring):
        a, b, c = PARTS[part][2]
        where = list(self.pos)
        if ring == "a":
            return a, where
        number = int(ring[1])
        if ring[0] == "b":
            where[a] = self.near(a)[number]
            return b, where
        where[a] = slice(None)
        where[b] = self.near(b)[number]
        return c, where

    def at(self, part, ring, which):
        axis, where = self.base(part, ring)
        where[axis] = self.near(axis)[which]
        return where

    def push(self, part, ring, number, which, by, start, size, src=None):
        axis, _ = self.base(part, ring)
        n = self.rings.index(ring)
        ref = self.region(self.at(part, ring, which), start, size)
        copy = pltpu.make_async_remote_copy(
            ref if src is None else src, ref, self.send_sem.at[part, n, number], self.recv_sem.at[part, n, number],
            device_id=device(moved(self.pos, axis, by), self.core), device_id_type=MESH)
        copy.start()
        self.copies[part, ring, number] = copy

    def begin(self, part, ring):
        start, size, _ = PARTS[part]
        src = self.own_ref.at[pl.ds(start, size), :] if ring in ("a", "b0") else None
        self.push(part, ring, 0, 0, 1, start, size, src)
        self.push(part, ring, 1, 0, 3, start, size, src)
        if ring == "a":
            self.push(part, ring, 2, 0, 2, start, size, src)

    def onward(self, part, ring, left=None, right=None):
        start, size, _ = PARTS[part]
        half = size // 32 * 16
        self.copies[part, ring, 0].wait_recv()
        if ring != "a":
            self.push(part, ring, 2, 1, 1, start, half)
        if left:
            left()
        self.copies[part, ring, 1].wait_recv()
        if ring != "a":
            self.push(part, ring, 3, 2, 3, start + half, size - half)
        if right:
            right()

    def end(self, part, ring):
        self.copies[part, ring, 2].wait_recv()
        if ring != "a":
            self.copies[part, ring, 3].wait_recv()

    def sibling(self, part, where, src=None):
        start, size, _ = PARTS[part]
        number = len(self.sibs[part])
        ref = self.region(where, start, size)
        copy = pltpu.make_async_remote_copy(
            ref if src is None else src, ref, self.sib_send.at[part, number], self.sib_recv.at[part, number],
            device_id=device(self.pos, 1 - self.core), device_id_type=MESH)
        copy.start()
        self.sibs[part].append(copy)

    def share(self, part, ring, which):
        return lambda: self.sibling(part, self.at(part, ring, which))

    def row(self, part, number):
        a, b, _ = PARTS[part][2]
        where = list(self.pos)
        where[a] = slice(None)
        where[b] = self.near(b)[number]
        return where

    def run(self):
        parts = range(3)
        own = pltpu.make_async_copy(self.own_ref, self.out_ref.at[self.pos[0], self.core, self.pos[1], self.pos[2]], self.local)
        own.start()
        for p in parts:
            self.begin(p, "a")
        for p in parts:
            self.begin(p, "b0")
        for p in parts:
            start, size, _ = PARTS[p]
            self.sibling(p, self.pos, self.own_ref.at[pl.ds(start, size), :])
        own.wait()
        for p in parts:
            def arrived(which, p=p):
                self.begin(p, "b" + str(which))
                self.sibling(p, self.at(p, "a", which))
            self.onward(p, "a", lambda: arrived(1), lambda: arrived(2))
        for p in parts:
            self.onward(p, "b0")
        for p in parts:
            self.end(p, "a")
            self.begin(p, "b3")
            self.begin(p, "c0")
            self.sibling(p, self.at(p, "a", 3))
        for p in parts:
            self.onward(p, "b1")
            self.onward(p, "b2")
        for p in parts:
            self.end(p, "b0")
            self.onward(p, "b3")
            self.begin(p, "c1")
            self.begin(p, "c2")
            self.sibling(p, self.row(p, 1))
            self.sibling(p, self.row(p, 2))
        for p in parts:
            self.onward(p, "c0", self.share(p, "c0", 1), self.share(p, "c0", 2))
        for p in parts:
            for ring in ("b1", "b2", "b3"):
                self.end(p, ring)
            self.begin(p, "c3")
            self.sibling(p, self.row(p, 3))
        for ring in ("c1", "c2", "c3"):
            for p in parts:
                self.onward(p, ring, self.share(p, ring, 1), self.share(p, ring, 2))
            for p in parts:
                before = {"c1": "c0", "c2": "c1", "c3": "c2"}[ring]
                self.end(p, before)
                self.sibling(p, self.at(p, before, 3))
        for p in parts:
            self.end(p, "c3")
            self.sibling(p, self.at(p, "c3", 3))
        for copies in self.sibs:
            for copy in copies:
                copy.wait_recv()

    def wait_send(self):
        for copy in self.copies.values():
            copy.wait_send()
        for copies in self.sibs:
            for copy in copies:
                copy.wait_send()


EIGHTH = 16 * 433
W_QKV = (24, 768, 18)
W_OUT = (13866, 768, 6)
W_UP = (18480, 768, 24)
W_DOWN = (36936, 3072, 6)
VECTORS = {"ln1_gain": (0, 6), "ln1_shift": (6, 6), "ln2_gain": (12, 6), "ln2_shift": (18, 6),
           "b_qkv": (13848, 18), "b_out": (18474, 6), "b_up": (36912, 24), "b_down": (55368, 6)}


HEADS = 12
TILE = 512
KEYS = 512


class Exchange:
    scratch = [pltpu.SemaphoreType.DMA((16,)), pltpu.SemaphoreType.DMA((16,)), pltpu.SemaphoreType.DMA]

    def __init__(self, in_ref, out_ref, send, recv, local):
        self.in_ref, self.out_ref = in_ref, out_ref
        self.send, self.recv, self.local = send, recv, local
        self.x, self.core = lax.axis_index("dp_0"), lax.axis_index("dp_1")
        self.me = lax.axis_index("seq_0") * 4 + lax.axis_index("seq_1")
        self.others = [lax.rem(self.me + k, 16) for k in range(1, 16)]

    def where(self, t):
        return (self.x, self.core, lax.div(t, 4), lax.rem(t, 4))

    def hello(self):
        barrier = pltpu.get_barrier_semaphore()
        for t in self.others:
            pl.semaphore_signal(barrier, inc=1, device_id=self.where(t), device_id_type=MESH)

    def copy(self, t):
        return pltpu.make_async_remote_copy(
            self.in_ref.at[t], self.out_ref.at[self.me], self.send.at[t], self.recv.at[self.me],
            device_id=self.where(t), device_id_type=MESH)

    def arrival(self, t):
        return pltpu.make_async_remote_copy(
            self.out_ref.at[t], self.out_ref.at[t], self.send.at[t], self.recv.at[t],
            device_id=self.where(t), device_id_type=MESH)

    def own(self):
        return pltpu.make_async_copy(self.in_ref.at[self.me], self.out_ref.at[self.me], self.local)


class ToHeads(Exchange):
    def start(self):
        for t in self.others:
            pl.when(t < HEADS)(lambda t=t: self.copy(t).start())
        pl.when(self.me < HEADS)(lambda: self.own().start())

    def wait(self):
        @pl.when(self.me < HEADS)
        def _():
            for t in self.others:
                self.arrival(t).wait_recv()
            self.own().wait()

    def wait_send(self):
        for t in self.others:
            pl.when(t < HEADS)(lambda t=t: self.copy(t).wait_send())


class FromHeads(Exchange):
    def start(self, first=0, last=16):
        for t in range(first, last):
            pl.when((self.me < HEADS) & (self.me != t))(lambda t=t: self.copy(jnp.int32(t)).start())
            pl.when((self.me < HEADS) & (self.me == t))(lambda: self.own().start())

    def wait(self):
        for t in self.others:
            pl.when(t < HEADS)(lambda t=t: self.arrival(t).wait_recv())

        @pl.when(self.me < HEADS)
        def _():
            for t in self.others:
                self.copy(t).wait_send()
            self.own().wait()


NT = (((1,), (1,)), ((), ()))


def product(a, b, dims=(((1,), (0,)), ((), ()))):
    return lax.dot_general(a, b, dims, preferred_element_type=jnp.float32)


def unrolled(low, high, body, carry):
    for j in range(low, high):
        carry = body(j, carry)
    return carry


def head_kernel(ready, in_ref, att_out, key_out, k, v, kt, vt, scores, dk, dv):
    blocks = 2048 // TILE
    per = TILE // 128

    def rows(which, i):
        return jnp.concatenate([in_ref[i * per + p, which] for p in range(per)], 0)

    @pl.loop(0, blocks)
    def _(i):
        at = pl.ds(pl.multiple_of(i * TILE, TILE), TILE)
        key = rows(0, i)[:, 64:]
        value = rows(1, i)[:, :64]
        k[at, :] = key
        v[at, :] = value
        kt[:, at] = key.T
        vt[:, at] = value.T
        dk[at, :] = jnp.zeros((TILE, 64), jnp.float32)
        dv[at, :] = jnp.zeros((TILE, 64), jnp.float32)

    def block(i):
        query = rows(0, i)[:, :64] * jnp.bfloat16(0.125)
        grad = rows(1, i)[:, 64:]

        def tile(j):
            return pl.ds(j * KEYS, KEYS)

        def put(j, s):
            for n in range(TILE // 128):
                scores[pl.ds(j * KEYS + n * 2048, KEYS), :] = s[:, 128 * n:128 * (n + 1)]

        def get(j):
            return jnp.concatenate(
                [scores[pl.ds(j * KEYS + n * 2048, KEYS), :] for n in range(TILE // 128)], 1)

        last = i * TILE // KEYS

        def first(j, top):
            s = product(k[tile(j), :], query, NT)
            put(j, s)
            return jnp.maximum(top, jnp.max(s, 0, keepdims=True))

        top = unrolled(0, last, first, jnp.full((1, TILE), -1e30, jnp.float32))
        s = product(k[tile(last), :], query, NT)
        keep = lax.broadcasted_iota(jnp.int32, (KEYS, TILE), 0) - lax.broadcasted_iota(jnp.int32, (KEYS, TILE), 1) <= i * TILE - last * KEYS
        s = jnp.where(keep, s, -1e30)
        put(last, s)
        top = jnp.maximum(top, jnp.max(s, 0, keepdims=True))

        def second(j, carry):
            total, out = carry
            e = jnp.exp(get(j) - top)
            put(j, e)
            return total + jnp.sum(e, 0, keepdims=True), out + product(vt[:, tile(j)], e.astype(jnp.bfloat16))

        total, out = unrolled(0, last + 1, second, (jnp.zeros((1, TILE), jnp.float32), jnp.zeros((64, TILE), jnp.float32)))
        scale = 1.0 / total
        out = out * scale
        inner = jnp.sum(out * grad.astype(jnp.float32).T, 0, keepdims=True)

        def third(j, dq):
            p = get(j) * scale
            dp = product(v[tile(j), :], grad, NT)
            ds = (p * (dp - inner)).astype(jnp.bfloat16)
            dv[tile(j), :] += product(p.astype(jnp.bfloat16), grad)
            dk[tile(j), :] += product(ds, query)
            return dq + product(kt[:, tile(j)], ds)

        dq = unrolled(0, last + 1, third, jnp.zeros((64, TILE), jnp.float32)) * 0.125
        both = jnp.concatenate([out, dq], 0).T.astype(jnp.bfloat16)
        for p in range(per):
            att_out[i * per + p] = both[128 * p:128 * (p + 1)]

    for i in range(blocks):
        block(i)
        ready(i * per, (i + 1) * per)

    @pl.loop(0, blocks)
    def _(i):
        at = pl.ds(pl.multiple_of(i * TILE, TILE), TILE)
        both = jnp.concatenate([dk[at, :], dv[at, :]], 1).astype(jnp.bfloat16)
        for p in range(per):
            key_out[i * per + p] = both[128 * p:128 * (p + 1)]


HEAD_SCRATCH = [pltpu.VMEM((2048, 64), jnp.bfloat16), pltpu.VMEM((2048, 64), jnp.bfloat16),
                pltpu.VMEM((64, 2048), jnp.bfloat16), pltpu.VMEM((64, 2048), jnp.bfloat16),
                pltpu.VMEM((2048, 64), jnp.float32), pltpu.VMEM((2048, 64), jnp.float32)]


MARGIN = 384
CHUNK = 128


def weight_eighth(number, pairs, vec_ref, flat):
    low, high = number * EIGHTH, (number + 1) * EIGHTH
    at = MARGIN - low
    for (offset, rows, blocks), left, right in pairs:
        first = max(0, (low - offset) // blocks) // 16 * 16
        last = min(rows, -(-(high - offset) // blocks))
        last = -(-last // 16) * 16
        if last <= first:
            continue
        size = min(CHUNK, last - first)
        count = -(-(last - first) // size)
        base = offset + at

        @pl.loop(0, count)
        def _(i, first=first, last=last, size=size, blocks=blocks, base=base, left=left, right=right):
            row = pl.multiple_of(jnp.minimum(first + i * size, last - size), 16)
            lhs = left[pl.ds(row, size), :]

            @pl.loop(0, blocks // 2, unroll=3)
            def _(j):
                rhs = right[:, pl.ds(pl.multiple_of(j * 256, 256), 256)]
                result = product(lhs, rhs)
                start = base + row * blocks + 2 * j
                flat[pl.ds(start, size, stride=blocks), :] = result[:, :128]
                flat[pl.ds(start + 1, size, stride=blocks), :] = result[:, 128:]

    row = 0
    for name in ORDER:
        start, count = VECTORS[name]
        lo, hi = max(start, low), min(start + count, high)
        if lo < hi:
            flat[lo + at:hi + at, :] = vec_ref[row + lo - start:row + hi - start, :]
        row += count
    end = 55374
    if high > end:
        flat[end + at:high + at, :] = jnp.zeros((high - end, 128), jnp.float32)


def halves(size):
    half = size // 32 * 16
    return half, size - half


class Scatter:
    names = ("c0", "c1", "c2", "c3", "b", "a")
    @staticmethod
    def scratch():
        out = []
        for _, size, _ in PARTS:
            h0, h1 = halves(size)
            for name in Scatter.names:
                if name == "a":
                    out += [pltpu.VMEM((size, 128), jnp.bfloat16)] * 3
                else:
                    out += [pltpu.VMEM((4, n, 128), jnp.bfloat16) for n in (h0, h1, h1, h0, h0, h1, h0, h1)]
            out += [pltpu.VMEM((4, 4, size, 128), jnp.bfloat16), pltpu.VMEM((4, size, 128), jnp.bfloat16)]
        return out + [pltpu.SemaphoreType.DMA((3, 6, 10)), pltpu.SemaphoreType.DMA((3, 6, 10))]

    def __init__(self, in_ref, out_ref, *scratch):
        self.in_ref, self.out_ref = in_ref, out_ref
        self.send, self.recv = scratch[-2:]
        take = iter(scratch[:-2])
        self.buf, self.rows, self.line = {}, [], []
        for p in range(3):
            for name in self.names:
                self.buf[p, name] = [next(take) for _ in range(3 if name == "a" else 8)]
            self.rows.append(next(take))
            self.line.append(next(take))
        self.pos, self.core = place()
        self.copies = {}

    def near(self, axis):
        q = self.pos[axis]
        return [q] + [lax.rem(q + k, 4) for k in (3, 1, 2)]

    def axis(self, p, name):
        return PARTS[p][2]["abc".index(name[0])]

    def source(self, p, name, which, lo, n):
        a, b, c = PARTS[p][2]
        if name == "a":
            return self.line[p].at[self.near(a)[which], pl.ds(lo, n), :]
        if name == "b":
            return self.rows[p].at[which, :, pl.ds(lo, n), :]
        where = [slice(None)] * 3
        where[b] = self.near(b)[int(name[1])]
        where[c] = self.near(c)[which]
        return self.in_ref.at[where[0], where[1], where[2], pl.ds(PARTS[p][0] + lo, n), :]

    def push(self, p, name, number, src, by, when=None, dst=None, sem=None):
        n = self.names.index(name)
        sem = number if sem is None else sem
        copy = pltpu.make_async_remote_copy(
            src, self.buf[p, name][number] if dst is None else dst, self.send.at[p, n, sem], self.recv.at[p, n, sem],
            device_id=device(moved(self.pos, self.axis(p, name), by), self.core), device_id_type=MESH)
        if when is None:
            copy.start()
        else:
            pl.when(when)(copy.start)
        self.copies.setdefault((p, name, number), []).append(copy)

    def arrived(self, p, name, number):
        for copy in self.copies[p, name, number]:
            copy.wait_recv()

    def sends(self, p):
        h0, h1 = halves(PARTS[p][1])
        return ((0, 3, 0, h0, 1), (1, 3, h0, h1, 3), (2, 2, h0, h1, 1), (3, 1, 0, h0, 3))

    def begin(self, p, name, numbers=(0, 1, 2, 3)):
        for number, which, lo, n, by in self.sends(p):
            if number in numbers:
                self.push(p, name, number, self.source(p, name, which, lo, n), by)

    def ahead(self, name, later, numbers):
        for p in range(3):
            a, b, c = PARTS[p][2]
            for number, which, lo, n, by in self.sends(p):
                if number not in numbers:
                    continue
                src = self.source(p, name, which, lo, n)
                if a == 0:
                    part = pl.ds(2 if later else 0, 2)
                    self.push(p, name, number, src.at[part], by, None, self.buf[p, name][number].at[part],
                              number if later else 6 + number)
                    continue
                x = self.near(0)[int(name[1])] if b == 0 else self.near(0)[which]
                if later:
                    self.push(p, name, number, src, by, x >= 2)
                else:
                    pl.when(x < 2)(self.copies[p, name, number][0].start)

    def direct(self, p):
        for number, (which, by) in enumerate(((1, 3), (2, 1), (3, 2))):
            self.push(p, "a", number, self.source(p, "a", which, 0, PARTS[p][1]), by)

    def total(self, p):
        start, size, _ = PARTS[p]
        for number in range(3):
            self.arrived(p, "a", number)
        value = self.source(p, "a", 0, 0, size)[...].astype(jnp.float32)
        for other in self.buf[p, "a"]:
            value = value + other[...].astype(jnp.float32)
        self.out_ref[start:start + size, :] = value

    def add(self, name, mine, others, put):
        def one(*at):
            total = mine[at + (slice(None), slice(None))].astype(jnp.float32)
            for other in others:
                total = total + other[at + (slice(None), slice(None))].astype(jnp.float32)
            put(at, total)

        pl.loop(0, 4)(lambda i: one(i))

    def onward(self, p, name):
        h0, h1 = halves(PARTS[p][1])
        b = self.buf[p, name]

        def to(ref):
            def put(at, total):
                ref[at + (slice(None), slice(None))] = total.astype(jnp.bfloat16)
            return put

        self.arrived(p, name, 0)
        self.add(name, self.source(p, name, 2, 0, h0), [b[0]], to(b[6]))
        self.push(p, name, 4, b[6], 1)
        self.arrived(p, name, 1)
        self.add(name, self.source(p, name, 1, h0, h1), [b[1]], to(b[7]))
        self.push(p, name, 5, b[7], 3)

    def end(self, p, name):
        h0, h1 = halves(PARTS[p][1])
        b = self.buf[p, name]
        for number in (3, 2, 4, 5):
            self.arrived(p, name, number)
        for lo, n, others in ((0, h0, [b[3], b[4]]), (h0, h1, [b[2], b[5]])):
            def put(at, total, lo=lo, n=n):
                if name == "b":
                    self.line[p][at + (pl.ds(lo, n), slice(None))] = total.astype(jnp.bfloat16)
                else:
                    self.rows[p][(int(name[1]),) + at + (pl.ds(lo, n), slice(None))] = total.astype(jnp.bfloat16)
            self.add(name, self.source(p, name, 0, lo, n), others, put)

    def before(self):
        for numbers in ((0, 1), (2, 3)):
            for name in ("c3", "c1", "c2", "c0"):
                self.ahead(name, True, numbers)

    def run(self, meanwhile):
        parts = range(3)

        def each(step, name, *more):
            for p in parts:
                step(p, name, *more)

        for name in ("c3", "c1", "c2", "c0"):
            self.ahead(name, False, (0, 1))
        self.ahead("c3", False, (2, 3))
        meanwhile()
        each(self.onward, "c3")
        self.ahead("c1", False, (2, 3))
        each(self.onward, "c1")
        each(self.end, "c3")
        each(self.begin, "b", (0, 1))
        self.ahead("c2", False, (2, 3))
        each(self.onward, "c2")
        each(self.end, "c1")
        each(self.begin, "b", (3,))
        self.ahead("c0", False, (2, 3))
        each(self.onward, "c0")
        each(self.end, "c2")
        each(self.begin, "b", (2,))
        each(self.onward, "b")
        for p in parts:
            self.end(p, "c0")
            self.end(p, "b")
            self.direct(p)
        for p in parts:
            self.total(p)
        for copies in self.copies.values():
            for copy in copies:
                copy.wait_send()


EPS = 1e-05
ORDER = ("ln1_gain", "ln1_shift", "ln2_gain", "ln2_shift", "b_qkv", "b_out", "b_up", "b_down")


def widen(g_ref, flat, step):
    @pl.loop(0, 16)
    def _(k):
        base = (step * 16 + k) * 433
        flat[pl.ds(base, 440), :] = g_ref[k, 0:440, :].astype(jnp.float32)


def unpack_matrix(flat, first, where, out, size=64):
    offset, rows, blocks = where
    start = offset - first * EIGHTH

    @pl.loop(0, rows // size)
    def _(i):
        for j in range(blocks):
            piece = flat[pl.ds(start + j + i * (size * blocks), size, stride=blocks), :]
            out[pl.ds(pl.multiple_of(i * size, size), size), 128 * j:128 * (j + 1)] = piece.astype(jnp.bfloat16)


def as_row(ref, start, count):
    return jnp.concatenate([ref[start + n:start + n + 1, :] for n in range(count)], 1)


def to_rows(ref, start, row):
    for n in range(row.shape[1] // 128):
        ref[start + n:start + n + 1, :] = row[:, 128 * n:128 * (n + 1)]


def normalized(values):
    center = jnp.mean(values, -1, keepdims=True)
    centered = values - center
    factor = lax.rsqrt(jnp.mean(centered * centered, -1, keepdims=True) + EPS)
    return centered * factor, factor


def turn(x, tables, sign):
    return x * tables[0] + (pltpu.roll(x, 120, 1) * tables[1] + pltpu.roll(x, 8, 1) * tables[2]) * sign


def const(*shape):
    return pl.BlockSpec(shape, lambda e: (0,) * len(shape))


def gelu_pair(u):
    inside = 0.5 * (1.0 + lax.erf(u * 0.7071067811865476))
    return u * inside, inside + u * jnp.exp(-0.5 * u * u) * 0.3989422804014327


class Twin:
    def __init__(self, send, recv):
        self.send, self.recv, self.copies = send, recv, []
        self.pos, self.core = place()

    def push(self, src, dst):
        number = len(self.copies)
        copy = pltpu.make_async_remote_copy(src, dst, self.send.at[number], self.recv.at[number],
                                            device_id=device(self.pos, 1 - self.core), device_id_type=MESH)
        copy.start()
        self.copies.append(copy)
        return copy

    def wait_send(self):
        for copy in self.copies:
            copy.wait_send()


def middle_kernel(params_ref, tokens_ref, grad_ref, tables_ref,
                  mlp_ref, dh2_ref, bias_ref, h1t_ref, vec_ref, up_ref, halves_ref, att_ref, key_ref, w_qkv_ref, w_out_ref, all_ref,
                  gbuf, flat, w_up, w_down, act, slope, act_pair, h2_pair, g_pair, dup_pair, vec, vec2,
                  heads_in, att_out, key_out, w_qkv, w_out, wide, blocks, own, *rest):
    head_scratch, rest = rest[:6], rest[6:]
    there = ToHeads(blocks, heads_in, *rest[0:3])
    home = FromHeads(att_out, att_ref, *rest[3:6])
    home_keys = FromHeads(key_out, key_ref, *rest[6:9])
    twin = Twin(*rest[9:11])
    load, store = rest[11:13]
    core = lax.axis_index("dp_1")
    gather = Gather(own, all_ref, *rest[13:])
    there.hello()
    count = hello(gather.pos, core)
    own[0:432, :] = params_ref[0:432, :]
    own[432:448, :] = jnp.zeros((16, 128), jnp.bfloat16)
    own[432:433, :] = params_ref[432:433, :]
    meet(count + 15)
    gather.run()
    loads = [pltpu.make_async_copy(all_ref.at[e // 2, e % 2], gbuf.at[e % 3], load.at[e]) for e in range(8)]
    for copy in loads[:3]:
        copy.start()
    stores = []

    def keep(src, dst):
        copy = pltpu.make_async_copy(src, dst, store.at[len(stores)])
        copy.start()
        stores.append(copy)

    def widen(eighth, at):
        @pl.loop(0, 16)
        def _(k):
            flat[pl.ds((at * 16 + k) * 433, 440), :] = gbuf[eighth % 3, lax.div(k, 4), lax.rem(k, 4), 0:440, :].astype(jnp.float32)

    for e in range(2):
        loads[e].wait()
        widen(e, e)
        loads[3 + e].start()
    unpack_matrix(flat, 0, W_QKV, w_qkv)
    keep(w_qkv, w_qkv_ref)
    loads[2].wait()
    widen(2, 2)
    unpack_matrix(flat, 0, W_OUT, w_out)
    keep(w_out, w_out_ref)
    vec_ref[0:24, :] = flat[0:24, :]
    start = VECTORS["b_out"][0]
    vec_ref[24:30, :] = flat[start:start + 6, :]
    normal, _ = normalized(tokens_ref[...].astype(jnp.float32))
    h1 = (normal * as_row(flat, 0, 6) + as_row(flat, 6, 6)).astype(jnp.bfloat16)
    h2 = (normal * as_row(flat, 12, 6) + as_row(flat, 18, 6)).astype(jnp.bfloat16)
    h1t_ref[...] = h1.T
    for n in range(9):
        start = VECTORS["b_qkv"][0] + 2 * n
        qkv = product(h1, w_qkv[:, 256 * n:256 * (n + 1)]) + as_row(flat, start, 2)
        wide[256 * n:256 * n + 128, :] = qkv[:, :128]
        wide[256 * n + 128:256 * (n + 1), :] = qkv[:, 128:]
    low = lax.broadcasted_iota(jnp.int32, (128, 128), 1) < 64
    swap = lambda t: pltpu.roll(t, 64, 1)
    for m in range(6):
        q, k, v = (wide[128 * (6 * p + m):128 * (6 * p + m + 1), :] for p in range(3))
        q = turn(q, tables_ref, 1.0)
        k = turn(k, tables_ref, 1.0)
        a = product(grad_ref[...], w_out[128 * m:128 * (m + 1), :], NT)
        blocks[2 * m, 0] = jnp.where(low, q, swap(k)).astype(jnp.bfloat16)
        blocks[2 * m + 1, 0] = jnp.where(low, swap(q), k).astype(jnp.bfloat16)
        blocks[2 * m, 1] = jnp.where(low, v, swap(a)).astype(jnp.bfloat16)
        blocks[2 * m + 1, 1] = jnp.where(low, swap(v), a).astype(jnp.bfloat16)
    there.start()
    h2_pair[:, :128] = h2.T
    g_pair[:128, :] = grad_ref[...]
    h2_copy = twin.push(h2_pair.at[:, pl.ds(0, 128)], h2_pair.at[:, pl.ds(128, 128)])
    g_copy = twin.push(g_pair.at[pl.ds(0, 128), :], g_pair.at[pl.ds(128, 128), :])
    for e in range(2, 6):
        if e > 2:
            loads[e].wait()
        widen(e, e - 2)
        if e < 5:
            loads[3 + e].start()
    unpack_matrix(flat, 2, W_UP, w_up)
    start = VECTORS["b_up"][0] - 2 * EIGHTH
    for n in range(12):
        at = slice(256 * n, 256 * (n + 1))
        up = product(h2, w_up[:, at]) + as_row(flat, start + 2 * n, 2)
        value, slope[:, at] = gelu_pair(up)
        value = value.astype(jnp.bfloat16)
        act[:, at] = value
        act_pair[at, :128] = value.T
    act_copy = twin.push(act_pair.at[:, pl.ds(0, 128)], act_pair.at[:, pl.ds(128, 128)])
    for e in range(3):
        if e:
            loads[5 + e].wait()
        widen(5 + e, e)
    unpack_matrix(flat, 5, W_DOWN, w_down, 128)
    start = VECTORS["b_down"][0] - 5 * EIGHTH
    for n in range(12):
        at = slice(256 * n, 256 * (n + 1))
        dup = (product(grad_ref[...], w_down[at, :], NT) * slope[:, at]).astype(jnp.bfloat16)
        dup_pair[:128, at] = dup
        to_rows(vec, 48 + 2 * n, jnp.sum(dup.astype(jnp.float32), 0, keepdims=True))
    dup_copy = twin.push(dup_pair.at[pl.ds(0, 128), :], dup_pair.at[pl.ds(128, 128), :])
    bias_ref[...] = vec[48:72, :]
    shift = jnp.sum(grad_ref[...].astype(jnp.float32), 0, keepdims=True)
    to_rows(vec, 72, shift)
    vec[78:80, :] = jnp.zeros((2, 128), jnp.float32)
    vec_copy = twin.push(vec.at[pl.ds(48, 32), :], vec2)
    for n in range(3):
        at = slice(256 * n, 256 * (n + 1))
        mlp_ref[:, at] = product(act[...], w_down[:, at]) + as_row(flat, start + 2 * n, 2)
        dh2_ref[:, at] = product(dup_pair[:128, :], w_up[at, :], NT)
    there.wait()
    head_kernel(home.start, heads_in, att_out, key_out, *head_scratch[:4], flat, *head_scratch[4:])
    home_keys.start()
    for copy in (h2_copy, g_copy, act_copy, dup_copy, vec_copy):
        copy.wait_recv()
    vec_copy.wait_send()
    vec[48:80, :] = vec[48:80, :] + vec2[...]
    for t in (1, 2, 3):
        for c in range(2):
            if t > 1 or c == 1:
                pl.when(core == c)(
                    lambda number=2 * t + c: weight_eighth(number, ((W_UP, h2_pair, dup_pair), (W_DOWN, act_pair, g_pair)), vec, flat))

        @pl.loop(0, 16)
        def _(k):
            gbuf[t - 1, lax.div(k, 4), lax.rem(k, 4)] = flat[pl.ds(MARGIN + 433 * k, 448), :].astype(jnp.bfloat16)

        keep(gbuf.at[t - 1], halves_ref.at[t - 1])

    @pl.when(core == 0)
    def _():
        @pl.loop(0, 12)
        def _(j):
            result = product(h2_pair[:96, :], dup_pair[:, pl.ds(pl.multiple_of(j * 256, 256), 256)])
            wide[pl.ds(2 * j, 96, stride=24), :] = result[:, :128]
            wide[pl.ds(2 * j + 1, 96, stride=24), :] = result[:, 128:]

    keep(wide.at[pl.ds(0, 2304)], up_ref)

    home.wait()
    home_keys.wait()
    there.wait_send()
    gather.wait_send()
    for copy in (h2_copy, g_copy, act_copy, dup_copy):
        copy.wait_send()
    for copy in stores:
        copy.wait()


def middle_part(params, tokens, grad, tables):
    f32 = lambda *s: jax.ShapeDtypeStruct(s, jnp.float32)
    bf = lambda *s: jax.ShapeDtypeStruct(s, jnp.bfloat16)
    vm = lambda *s: pltpu.VMEM(s, jnp.bfloat16)
    vf = lambda *s: pltpu.VMEM(s, jnp.float32)
    anywhere = pl.BlockSpec(memory_space=pl.ANY)
    outs = [f32(128, 768), f32(128, 768), f32(24, 128), bf(768, 128), f32(32, 128)]
    far = [f32(2304, 128), bf(3, 4, 4, 448, 128), bf(HEADS, 128, 128), bf(HEADS, 128, 128),
           bf(768, 2304), bf(768, 768), bf(4, 2, 4, 4, 448, 128)]
    dma = pltpu.SemaphoreType.DMA
    return pl.pallas_call(
        middle_kernel,
        grid=(1,),
        out_shape=outs + far,
        in_specs=[const(433, 128), const(128, 768), const(128, 768), const(3, 128, 128)],
        out_specs=[const(*o.shape) for o in outs] + [anywhere] * len(far),
        scratch_shapes=[vm(3, 4, 4, 448, 128), vf(4 * EIGHTH + 16, 128), vm(768, 3072), vm(3072, 768), vm(128, 3072),
                        vf(128, 3072), vm(3072, 256), vm(768, 256), vm(256, 768), vm(256, 3072), vf(80, 128), vf(32, 128),
                        vm(16, 2, 128, 128), vm(16, 128, 128), vm(16, 128, 128), vm(768, 2304), vm(768, 768), vf(2336, 128),
                        vm(HEADS, 2, 128, 128), vm(448, 128)]
        + HEAD_SCRATCH + Exchange.scratch * 3 + [dma((5,)), dma((5,)), dma((8,)), dma((6,))] + Gather.scratch,
        compiler_params=pltpu.CompilerParams(collective_id=2, has_side_effects=True, vmem_limit_bytes=VMEM_LIMIT),
    )(params, tokens, grad, tables)


def last_kernel(att_ref, key_ref, tokens_ref, grad_ref, tables_ref, mlp_ref, dh2_ref, bias_ref, in_vec, h1t_ref,
                w_qkv_ref, w_out_ref, up_in, halves_ref, layer_ref, input_ref, own_ref,
                sums, flat, h1_pair, att_pair, dqkv_pair, g_pair, vec, vec2, w_qkv, w_out, up_ref, twin_send, twin_recv, load, *scratch):
    pairs = ((halves_ref, sums.at[pl.ds(1, 3)]), (w_qkv_ref, w_qkv), (w_out_ref, w_out), (up_in, up_ref))
    later, qkv_load, out_load, up_load = (pltpu.make_async_copy(a, b, load.at[n]) for n, (a, b) in enumerate(pairs))
    later.start()
    scatter = Scatter(sums, own_ref, *scratch)
    meet(hello(scatter.pos, scatter.core))
    twin = Twin(twin_send, twin_recv)
    h1_pair[:, :128] = h1t_ref[...]
    g_pair[:128, :] = grad_ref[...]
    lanes = lambda pair: twin.push(pair.at[:, pl.ds(0, 128)], pair.at[:, pl.ds(128, 128)])
    rows = lambda pair: twin.push(pair.at[pl.ds(0, 128), :], pair.at[pl.ds(128, 128), :])
    lanes(h1_pair)
    rows(g_pair)
    later.wait()
    for copy in (qkv_load, out_load, up_load):
        copy.start()
    scatter.before()
    low = lax.broadcasted_iota(jnp.int32, (128, 128), 1) < 64
    swap = lambda t: pltpu.roll(t, 64, 1)
    f32 = lambda t: t.astype(jnp.float32)
    attended = []
    for m in range(6):
        a, b = f32(att_ref[2 * m]), f32(att_ref[2 * m + 1])
        c, d = f32(key_ref[2 * m]), f32(key_ref[2 * m + 1])
        attended.append(jnp.where(low, a, swap(b)).astype(jnp.bfloat16))
        dq = turn(jnp.where(low, swap(a), b), tables_ref, -1.0)
        dk = turn(jnp.where(low, c, swap(d)), tables_ref, -1.0)
        dv = jnp.where(low, swap(c), d)
        for p, part in enumerate((dq, dk, dv)):
            dqkv_pair[:128, 768 * p + 128 * m:768 * p + 128 * (m + 1)] = part.astype(jnp.bfloat16)
    rows(dqkv_pair)
    attended = jnp.concatenate(attended, 1)
    att_pair[:, :128] = attended.T
    lanes(att_pair)
    tokens = f32(tokens_ref[...])
    grad = f32(grad_ref[...])
    normal, factor = normalized(tokens)
    qkv_load.wait()
    input_ref[...] = product(dqkv_pair[:128, :], w_qkv[...], NT)
    for row, dh in ((0, input_ref), (12, dh2_ref)):
        to_rows(vec, row, jnp.sum(dh[...] * normal, 0, keepdims=True))
        to_rows(vec, row + 6, jnp.sum(dh[...], 0, keepdims=True))
    to_rows(vec, 24, jnp.sum(f32(dqkv_pair[:128, :]), 0, keepdims=True))
    shift = jnp.sum(grad, 0, keepdims=True)
    to_rows(vec, 42, shift)
    vec[48:72, :] = bias_ref[...]
    to_rows(vec, 72, shift)
    vec[78:80, :] = jnp.zeros((2, 128), jnp.float32)
    twin.push(vec, vec2)
    out_load.wait()
    up_load.wait()

    def results():
        tokens = f32(tokens_ref[...])
        branch = lax.dot_general(att_pair[:, :128], w_out[...], (((0,), (0,)), ((), ())), preferred_element_type=jnp.float32)
        layer_ref[...] = (tokens + (branch + as_row(in_vec, 24, 6)) + mlp_ref[...]).astype(jnp.bfloat16)
        normal, factor = normalized(tokens)
        total = f32(grad_ref[...])
        for gain_at, dh in ((0, input_ref), (12, dh2_ref)):
            scaled = dh[...] * as_row(in_vec, gain_at, 6)
            inner = scaled - jnp.mean(scaled, -1, keepdims=True) - normal * jnp.mean(scaled * normal, -1, keepdims=True)
            total = total + factor * inner
        input_ref[...] = total

    for copy in twin.copies:
        copy.wait_recv()
    twin.copies[-1].wait_send()
    vec[...] = vec[...] + vec2[...]
    pairs = ((W_QKV, h1_pair, dqkv_pair), (W_OUT, att_pair, g_pair))

    def keep(t):
        for z in range(4):
            @pl.loop(0, 4)
            def _(y):
                sums[t, z, y] = flat[pl.ds(MARGIN + 433 * (4 * z + y), 448), :].astype(jnp.bfloat16)

    for c in range(2):
        pl.when(scatter.core == c)(lambda c=c: weight_eighth(c, pairs, vec, flat))
    keep(0)

    @pl.when(scatter.core == 0)
    def _():
        weight_eighth(2, pairs, vec, flat)
        at = W_UP[0] - 2 * EIGHTH + MARGIN
        flat[at:at + 2304, :] = up_ref[...]
        keep(1)

    scatter.run(results)
    for copy in twin.copies[:-1]:
        copy.wait_send()


def last_part(*args):
    bf = lambda *s: jax.ShapeDtypeStruct(s, jnp.bfloat16)
    f32 = lambda *s: jax.ShapeDtypeStruct(s, jnp.float32)
    vm = lambda *s: pltpu.VMEM(s, jnp.bfloat16)
    vf = lambda *s: pltpu.VMEM(s, jnp.float32)
    dma = pltpu.SemaphoreType.DMA
    outs = [bf(128, 768), f32(128, 768), f32(448, 128)]
    return pl.pallas_call(
        last_kernel,
        grid=(1,),
        out_shape=outs,
        in_specs=[const(*a.shape) for a in args[:-4]] + [pl.BlockSpec(memory_space=pl.ANY)] * 4,
        out_specs=[const(*o.shape) for o in outs],
        scratch_shapes=[vm(4, 4, 4, 448, 128), vf(EIGHTH + 2 * MARGIN, 128), vm(768, 256), vm(768, 256), vm(256, 2304),
                        vm(256, 768), vf(80, 128), vf(80, 128), vm(768, 2304), vm(768, 768), vf(2304, 128),
                        dma((5,)), dma((5,)), dma((4,))] + Scatter.scratch(),
        compiler_params=pltpu.CompilerParams(collective_id=1, has_side_effects=True, vmem_limit_bytes=VMEM_LIMIT),
    )(*args)


def finish_kernel(layer_in, input_in, own_in, layer_ref, input_ref, own_ref):
    layer_ref[...] = layer_in[...]
    input_ref[...] = input_in[...]
    own_ref[...] = own_in[:433, :]


def finish(*args):
    shapes = [(128, 768), (128, 768), (433, 128)]
    return pl.pallas_call(
        finish_kernel,
        grid=(1,),
        out_shape=[jax.ShapeDtypeStruct(s, a.dtype) for s, a in zip(shapes, args)],
        in_specs=[const(*a.shape) for a in args],
        out_specs=[const(*s) for s in shapes],
    )(*args)


def rotary_tables(positions):
    lane = jnp.arange(128) % 64
    freq = jnp.tile(10000.0 ** (-jnp.arange(8).astype(jnp.float32) * 2.0 / 16), 16)
    angles = positions.astype(jnp.float32)[:, None] * freq[None, :]
    cosine, sine = jnp.cos(angles), jnp.sin(angles)
    return jnp.stack([jnp.where(lane < 16, cosine, 1.0), jnp.where(lane < 8, -sine, 0.0),
                      jnp.where((lane >= 8) & (lane < 16), sine, 0.0)])


def body(tokens, params, out_grad):
    piece = tokens.shape[1]
    x, grad = tokens[0], out_grad[0]
    tables = rotary_tables(lax.axis_index(SEQ) * piece + jnp.arange(piece))
    mlp, dh2, bias, h1t, in_vec, up_rows, later, att, keys, w_qkv, w_out, _ = middle_part(
        params.reshape(433, 128), x, grad, tables
    )
    results = last_part(att, keys, x, grad, tables, mlp, dh2, bias, in_vec, h1t, w_qkv, w_out, up_rows, later)
    layer_out, input_grad, own_sum = finish(*results)
    param_grad = own_sum.reshape(-1)
    return layer_out[None], input_grad[None], param_grad


def solution(mesh):
    finer = Mesh(mesh.devices.reshape(4, 2, 4, 4), DP_SEQ)
    in_specs = (P(DP, SEQ, None), P(DP_SEQ), P(DP, SEQ, None))
    out_specs = (P(DP, SEQ, None), P(DP, SEQ, None), P(DP_SEQ))
    return jax.shard_map(body, mesh=finer, in_specs=in_specs, out_specs=out_specs, check_vma=False)
```
